128 devices in a mesh: group: 8 (over z, x_hi), head: 16 (over x_lo, y, core).
Axes of the slice: x: 4 (x_hi: 2, x_lo: 2; x = x_hi * 2 + x_lo), y: 4, z: 4, core: 2. Of those that a mesh axis runs over, the one named last changes fastest.
Arguments:
- states: float32 [256, 32, 128, 128], P('group', 'head'), may hold values from -6 to 6
- placement: int32 [256, 1], replicated, may hold values from 0 to 31; in each aligned block of 32 rows (0 to 31, 32 to 63, ...) at most 2 rows name the same one
- queries: bfloat16 [8, 16, 8, 2, 8, 512], P('group', 'head'), may hold values from -6 to 6
- key_vectors: bfloat16 [8, 16, 8, 2, 8, 512], P('group', 'head'), may hold values from -6 to 6
- value_vectors: bfloat16 [8, 16, 8, 2, 8, 1024], P('group', 'head'), may hold values from -6 to 6
- gate_inputs: bfloat16 [8, 16, 8, 2, 8, 1024], P('group', 'head'), may hold values from -6 to 6
- write_strength: float32 [8, 16, 8, 2, 8, 8], P('group', 'head'), may hold values from 0.05 to 1
- decay_rate: float32 [8, 16, 8, 2, 8, 8], P('group', 'head'), may hold values from 0.02 to 1
- norm_gain: float32 [128], replicated, may hold values from 0.25 to 1.75
Outputs:
- decoded: bfloat16 [8, 16, 8, 2, 8, 1024], P('group', 'head')
- final_states: float32 [8, 16, 8, 2, 8, 128, 128], P('group', 'head')
The draws below stay inside these ranges and needn't reach their ends.
Inputs may be any that keep to these rules, and one draw needn't show every extreme that they name: `placement`: among the requests of one prefill group no decode group is named more than 2 times, and some decode group exactly 2 times.
All inputs are finite; a program needn't handle non-finite values.
Results may differ from the reference program's by a relative error of at most 0.001.
Values sent between devices are 32-bit elements; how exact they have to be, the bound alone decides.
No kernel may reach another device: no remote copies, remote signals or barrier semaphores. Data moves between devices by JAX's collectives and lax.ppermute only.
A program may use at most 128 MiB of HBM per device.

```python
import math
import jax
import jax.numpy as jnp
import numpy as np
from jax import lax

VALUE_HEADS = 32
KEY_DIM = 128
VALUE_DIM = 128
DECODE_STEPS = 8
SUBGROUPS = 4
SLOT_CAP = 2
GROUP_REQS = 32
REQUESTS = 256
DEC_SLOTS = 16
BLOCK_HEADS = 8
BLOCK_KEYS = 4
N_GROUP = 8
N_HEAD = 16


def draw_decay_rate(key, part):
    key = jax.random.fold_in(key, 17)
    seed_frequency, seed_processor, seed_surge, seed_layering = jax.random.split(key, 4)
    lead_shape = (N_GROUP, N_HEAD, N_GROUP, SLOT_CAP, 1, BLOCK_HEADS)
    entire_dimensions = (N_GROUP, N_HEAD, N_GROUP, SLOT_CAP, DECODE_STEPS, BLOCK_HEADS)
    high_rate = 1.5
    incoming_frequency = jnp.exp(jax.random.uniform(seed_frequency, lead_shape, jnp.float32, math.log(0.002), math.log(high_rate)))
    processor_multiplier = jnp.exp(jax.random.uniform(seed_processor, (N_GROUP, N_HEAD, 1, 1, 1, 1), jnp.float32, math.log(0.5), math.log(2.0)))
    surge_extent = jax.random.bernoulli(seed_surge, 0.1, entire_dimensions)
    layer_total = jax.random.uniform(seed_layering, entire_dimensions, jnp.float32, 0.5, 0.8)
    return (jnp.exp(-incoming_frequency * processor_multiplier) * jnp.where(surge_extent, layer_total, 1.0)).astype(jnp.float32)


def levels(key, dims, shards, smallest, largest):
    factor_of, own = 1.0, jax.random.fold_in(key, 6)
    for position, blocks in shards:
        draws = jnp.exp(jax.random.uniform(jax.random.fold_in(own, position), (blocks,), jnp.float32, smallest / len(shards), largest / len(shards)))
        factor_of = factor_of * jnp.repeat(draws, dims[position] // blocks).reshape([-1 if axis == position else 1 for axis in range(len(dims))])
    return factor_of


def deal_out(own_key, own, number, rows, count, top, reach, skew):
    order = jax.random.permutation(own_key, count)
    packed, ordinary = load_shares(count, rows * top, reach, skew, True), load_shares(count, rows * top, reach, skew, False)
    places = jnp.arange(count)

    def named(sizes, turn):
        used = int((sizes > 0).sum())
        fixed = max(1, used // 4)
        passed = fixed + (places - fixed + turn * (used - fixed)) % max(1, count - fixed)
        return jnp.zeros((count,), jnp.int32).at[order[jnp.where(places < fixed, places, passed)]].set(jnp.asarray(sizes, jnp.int32))

    sizes = jnp.where(number % 4 == 0, named(packed, number // 4), named(ordinary, number - number // 4 - 1))
    mixed = jax.random.permutation(jax.random.fold_in(own, 3), count)
    source_of, sink = mixed[0:count // 2 * 2:2], mixed[1:count // 2 * 2:2]
    room = jnp.minimum(sizes[source_of] - 1, reach - sizes[sink]) // 2
    room = jnp.where((source_of == order[0]) | (sink == order[0]) | (sizes[sink] == 0), 0, jnp.maximum(room, 0))
    passed = jax.random.randint(jax.random.fold_in(own, 4), (count // 2,), 0, 1 << 20) % (room + 1)
    sizes = sizes.at[source_of].add(-passed).at[sink].add(passed)
    members = jnp.searchsorted(jnp.cumsum(sizes), jnp.arange(rows * top), side="right").astype(jnp.int32)
    listing = members.reshape(top, rows).T
    listing = listing[jax.random.permutation(jax.random.fold_in(own, 1), rows)]
    turn = jax.random.randint(jax.random.fold_in(own, 2), (rows, 1), 0, top)
    return jnp.take_along_axis(listing, (jnp.arange(top)[None, :] + turn) % top, axis=1)


def load_shares(amount, total, reach, slope, full):
    loads = [(1 << 20) // math.isqrt(rank ** slope) + 1 for rank in range(1, amount + 1)]
    largest = reach if full else min(reach, max(-(-total // amount), total * loads[0] // sum(loads)))
    least = 1 if total - largest >= amount - 1 else 0
    counts, spare = [largest] + [least] * (amount - 1), total - largest - least * (amount - 1)
    while spare > 0:
        movable = [i for i in range(1, amount) if counts[i] < largest] or [i for i in range(1, amount) if counts[i] < reach]
        pool, remaining = sum([loads[i] for i in movable]), spare
        for i in movable:
            extra = min(reach - counts[i], max(1, remaining * loads[i] // pool), spare)
            counts[i] = counts[i] + extra
            spare = spare - extra
    return np.array(counts)


def centred(own_key, extent, width, bound, shards=(), kind=jnp.bfloat16):
    entries = width * jax.random.normal(own_key, extent, jnp.float32)
    if shards:
        entries = entries * levels(own_key, extent, shards, -0.22, 0.18)
    return jnp.clip(entries, -bound, bound).astype(kind)


def setup_inputs(seed: int = 0) -> dict:
    arg_keys = jax.random.split(jax.random.key(seed), 10)
    states = centred(arg_keys[0], (REQUESTS, VALUE_HEADS, KEY_DIM, VALUE_DIM), 1.0, 6.0, ((0, 8), (1, 16)), jnp.float32)
    placement_keys = jax.random.split(jax.random.fold_in(arg_keys[1], 1), REQUESTS // GROUP_REQS)
    placement_turns = jax.random.permutation(jax.random.fold_in(arg_keys[1], 3), REQUESTS // GROUP_REQS)
    placement = jax.vmap(lambda own, number: deal_out(jax.random.fold_in(arg_keys[1], 2), own, number, GROUP_REQS, N_GROUP * SUBGROUPS, 1, SLOT_CAP, 2))(placement_keys, placement_turns).reshape((REQUESTS, 1))
    queries = centred(arg_keys[2], (N_GROUP, N_HEAD, N_GROUP, SLOT_CAP, DECODE_STEPS, BLOCK_KEYS * KEY_DIM), 1.0, 6.0, ((0, 8), (1, 16)))
    key_vectors = centred(arg_keys[3], (N_GROUP, N_HEAD, N_GROUP, SLOT_CAP, DECODE_STEPS, BLOCK_KEYS * KEY_DIM), 1.0, 6.0, ((0, 8), (1, 16)))
    value_vectors = centred(arg_keys[4], (N_GROUP, N_HEAD, N_GROUP, SLOT_CAP, DECODE_STEPS, BLOCK_HEADS * VALUE_DIM), 1.0, 6.0, ((0, 8), (1, 16)))
    gate_inputs = centred(arg_keys[5], (N_GROUP, N_HEAD, N_GROUP, SLOT_CAP, DECODE_STEPS, BLOCK_HEADS * VALUE_DIM), 1.0, 6.0, ((0, 8), (1, 16)))
    write_strength = jnp.clip(0.05 + 0.95 * jax.random.uniform(arg_keys[6], (N_GROUP, N_HEAD, N_GROUP, SLOT_CAP, DECODE_STEPS, BLOCK_HEADS), jnp.float32) ** levels(arg_keys[6], (N_GROUP, N_HEAD, N_GROUP, SLOT_CAP, DECODE_STEPS, BLOCK_HEADS), ((0, 8), (1, 16)), -0.2, 0.2), 0.05, 1.0)
    decay_rate = draw_decay_rate(jax.random.fold_in(arg_keys[9], 71), 0)
    norm_gain = jnp.clip(1.0 + 0.15 * jax.random.normal(arg_keys[8], (VALUE_DIM,), jnp.float32), 0.25, 1.75)
    return dict(states=states, placement=placement, queries=queries, key_vectors=key_vectors, value_vectors=value_vectors, gate_inputs=gate_inputs, write_strength=write_strength, decay_rate=decay_rate, norm_gain=norm_gain)


def slot_table(placement):
    placed_all = placement[:, 0].reshape(N_GROUP, GROUP_REQS)
    dec_groups = N_GROUP * SUBGROUPS
    one_hot = (placed_all[:, :, None] == jnp.arange(dec_groups, dtype=jnp.int32)[None, None, :]).astype(jnp.int32)
    ranking = (jnp.cumsum(one_hot, axis=1) - 1).astype(jnp.int32)
    matched = one_hot[..., None] * (ranking[..., None] == jnp.arange(SLOT_CAP, dtype=jnp.int32)).astype(jnp.int32)
    global_rows = jnp.arange(GROUP_REQS, dtype=jnp.int32)[None, :, None, None] + GROUP_REQS * jnp.arange(N_GROUP, dtype=jnp.int32)[:, None, None, None]
    source_rows = lax.optimization_barrier(jnp.sum(matched * global_rows, axis=1)).astype(jnp.int32)
    live_slots = lax.optimization_barrier(jnp.sum(matched, axis=1)).astype(jnp.int32)
    return (source_rows, live_slots)

def decode(initial, live_mask, queries, key_vectors, value_vectors, gate_inputs, write_strength, decay_rate, norm_gain):
    slot_count, heads, key_size, value_size = initial.shape
    step_count = queries.shape[1]
    query_f = queries.astype(jnp.float32).reshape(slot_count, step_count, heads // 2, key_size)
    query_unit = query_f * lax.rsqrt(lax.optimization_barrier(jnp.sum(query_f * query_f, axis=-1, keepdims=True)) + 1e-06) / math.sqrt(key_size)
    query_unit = jnp.repeat(query_unit, 2, axis=2)
    key_f = key_vectors.astype(jnp.float32).reshape(slot_count, step_count, heads // 2, key_size)
    key_unit = key_f * lax.rsqrt(lax.optimization_barrier(jnp.sum(key_f * key_f, axis=-1, keepdims=True)) + 1e-06)
    key_unit = jnp.repeat(key_unit, 2, axis=2)
    value_f = value_vectors.astype(jnp.float32).reshape(slot_count, step_count, heads, value_size)
    gate_f = gate_inputs.astype(jnp.float32).reshape(slot_count, step_count, heads, value_size)
    state = initial
    produced = []
    for step_index in range(step_count):
        state = decay_rate[:, step_index, :, None, None] * state
        predicted = jnp.einsum('shi,shij->shj', key_unit[:, step_index], state, precision=lax.Precision.HIGHEST)
        residual = value_f[:, step_index] - predicted
        state = state + write_strength[:, step_index, :, None, None] * key_unit[:, step_index, :, :, None] * residual[:, :, None, :]
        readout = jnp.einsum('shi,shij->shj', query_unit[:, step_index], state, precision=lax.Precision.HIGHEST)
        normed = readout * lax.rsqrt(lax.optimization_barrier(jnp.mean(readout * readout, axis=-1, keepdims=True)) + 1e-06)
        normed = normed * norm_gain * jax.nn.silu(gate_f[:, step_index])
        produced.append(normed.reshape(slot_count, heads * value_size))
    tokens = jnp.stack(produced, axis=1)
    tokens = jnp.where(live_mask[:, None, None], tokens, 0.0).astype(jnp.bfloat16)
    state = jnp.where(live_mask[:, None, None, None], state, 0.0)
    return (tokens, state)

def reference(states, placement, queries, key_vectors, value_vectors, gate_inputs, write_strength, decay_rate, norm_gain):
    source_rows, live_slots = slot_table(placement)
    device_count = N_GROUP * N_HEAD
    devices = jnp.arange(device_count, dtype=jnp.int32)
    dec_group = devices // N_HEAD * SUBGROUPS + devices % N_HEAD % SUBGROUPS
    head_block = devices % N_HEAD // SUBGROUPS

    def per_device(items):
        group_id, block_id, query_d, key_d, value_d, gate_d, write_d, decay_d = items
        chosen = source_rows[:, group_id, :].reshape(DEC_SLOTS)
        live_mask = live_slots[:, group_id, :].reshape(DEC_SLOTS) > 0
        picked = jnp.take(states, chosen, axis=0)
        initial = lax.dynamic_slice_in_dim(picked, (block_id * BLOCK_HEADS).astype(jnp.int32), BLOCK_HEADS, axis=1)
        initial = jnp.where(live_mask[:, None, None, None], initial, 0.0)
        return decode(initial, live_mask, query_d, key_d, value_d, gate_d, write_d, decay_d, norm_gain)
    items = (dec_group, head_block, queries.reshape(device_count, DEC_SLOTS, DECODE_STEPS, BLOCK_KEYS * KEY_DIM), key_vectors.reshape(device_count, DEC_SLOTS, DECODE_STEPS, BLOCK_KEYS * KEY_DIM), value_vectors.reshape(device_count, DEC_SLOTS, DECODE_STEPS, BLOCK_HEADS * VALUE_DIM), gate_inputs.reshape(device_count, DEC_SLOTS, DECODE_STEPS, BLOCK_HEADS * VALUE_DIM), write_strength.reshape(device_count, DEC_SLOTS, DECODE_STEPS, BLOCK_HEADS), decay_rate.reshape(device_count, DEC_SLOTS, DECODE_STEPS, BLOCK_HEADS))
    tokens, finals = lax.map(per_device, items)
    decoded = tokens.reshape(N_GROUP, N_HEAD, N_GROUP, SLOT_CAP, DECODE_STEPS, BLOCK_HEADS * VALUE_DIM)
    final_states = finals.reshape(N_GROUP, N_HEAD, N_GROUP, SLOT_CAP, BLOCK_HEADS, KEY_DIM, VALUE_DIM)
    return (decoded, final_states)
```

```python
import math

import jax
import jax.numpy as jnp
from jax import lax
from jax.experimental import pallas as pl
from jax.experimental.pallas import tpu as pltpu
from jax.sharding import Mesh
from jax.sharding import PartitionSpec as P

SUBGROUPS = 4
SLOT_CAP = 2
EPS = 1e-06


def pack_kernel(n_group, reqs, placed, states, cells, live, count, sems):
    group = lax.axis_index("group")
    mine = group * SUBGROUPS + lax.axis_index("sub")
    dec_groups = n_group * SUBGROUPS

    def clear(d, carry):
        count[d] = 0
        return carry

    lax.fori_loop(0, dec_groups, clear, 0)

    def copy(r):
        d = placed[group * reqs + r]
        rank = count[d]
        count[d] = rank + 1
        return pltpu.make_async_copy(states.at[r], cells.at[d, rank], sems.at[r])

    def send(r, carry):
        copy(r).start()
        return carry

    lax.fori_loop(0, reqs, send, 0)

    for s in range(n_group):

        def tally(r, total, s=s):
            return total + jnp.where(placed[s * reqs + r] == mine, 1, 0)

        live[s] = lax.fori_loop(0, reqs, tally, 0, unroll=8)

    def drain(r, carry):
        pltpu.make_async_copy(states.at[r], cells.at[0, 0], sems.at[r]).wait()
        return carry

    lax.fori_loop(0, reqs, drain, 0)


def pack(placed, states, n_group):
    reqs, heads, key_size, value_size = states.shape
    cells = (n_group * SUBGROUPS, SLOT_CAP, heads, key_size, value_size)
    return pl.pallas_call(
        lambda *refs: pack_kernel(n_group, reqs, *refs),
        out_shape=(
            jax.ShapeDtypeStruct(cells, states.dtype),
            jax.ShapeDtypeStruct((n_group,), jnp.int32),
        ),
        in_specs=[
            pl.BlockSpec(memory_space=pltpu.SMEM),
            pl.BlockSpec(memory_space=pl.ANY),
        ],
        out_specs=(
            pl.BlockSpec(memory_space=pl.ANY),
            pl.BlockSpec(memory_space=pltpu.SMEM),
        ),
        scratch_shapes=[
            pltpu.SMEM((n_group * SUBGROUPS,), jnp.int32),
            pltpu.SemaphoreType.DMA((reqs,)),
        ],
    )(placed, states)


def split(x):
    high = x.astype(jnp.bfloat16)
    return high, (x - high.astype(jnp.float32)).astype(jnp.bfloat16)


def pair(left, right, shape):
    return jnp.concatenate(
        [jnp.broadcast_to(left, shape), jnp.broadcast_to(right, shape)], axis=1
    )


def key_head(first, second, query, key, value, gate, strength, decay, gain):
    steps, size = key.shape
    half = (steps, first.shape[1])
    state = jnp.concatenate([first, second], axis=1)
    both = jnp.concatenate([key, query], axis=0)
    key_f, query_f = key.astype(jnp.float32), query.astype(jnp.float32)
    key_norm = lax.rsqrt(jnp.sum(key_f * key_f, axis=1, keepdims=True) + EPS)
    query_norm = lax.rsqrt(jnp.sum(query_f * query_f, axis=1, keepdims=True) + EPS) / math.sqrt(size)
    high, low = split(state)
    product = jnp.dot(
        jnp.concatenate([both, both], axis=1),
        jnp.concatenate([high, low], axis=0),
        preferred_element_type=jnp.float32,
    )
    gram = lax.dot_general(
        both, key, (((1,), (1,)), ((), ())), preferred_element_type=jnp.float32
    )
    decay_w = pair(decay[:, 0:1], decay[:, 1:2], half)
    norm_w = jnp.broadcast_to(key_norm, (steps, 2 * half[1]))
    write_w = pair(strength[:, 0:1], strength[:, 1:2], half) * norm_w
    row = lax.broadcasted_iota(jnp.int32, (steps, 2 * half[1]), 0)
    writes = jnp.zeros((steps, 2 * half[1]), jnp.float32)
    readout = writes
    kept = jnp.ones((1, 2 * half[1]), jnp.float32)
    for t in range(steps):
        fade = decay_w[t : t + 1]
        product = product * fade
        residual = value[t : t + 1] - norm_w[t : t + 1] * product[t : t + 1]
        write = write_w[t : t + 1] * residual
        product = product + gram[:, t : t + 1] * write
        readout = jnp.where(row == t, product[steps:], readout)
        writes = jnp.where(row == t, write, writes * fade)
        kept = kept * fade
    high, low = split(writes)
    update = lax.dot_general(
        jnp.concatenate([key, key], axis=0),
        jnp.concatenate([high, low], axis=0),
        (((0,), (0,)), ((), ())),
        preferred_element_type=jnp.float32,
    )
    state = kept * state + update
    readout = readout * query_norm
    halves = [readout[:, : half[1]], readout[:, half[1] :]]
    halves = [
        x * lax.rsqrt(jnp.mean(x * x, axis=1, keepdims=True) + EPS) * gain for x in halves
    ]
    token = jnp.concatenate(halves, axis=1) * (gate * jax.nn.sigmoid(gate))
    return token, state


def decode_kernel(live, cells, query, key, value, gate, strength, decay, gain, tokens, finals):
    s = pl.program_id(0)
    sources, heads = cells.shape[1], cells.shape[3]
    size, width = cells.shape[4], cells.shape[5]
    for k in range(SLOT_CAP):
        at = (0, 0, 0, k)

        @pl.when(live[s] > k)
        def _(k=k, at=at):
            for i in range(sources):
                keys = slice(i * size, (i + 1) * size)
                values = slice(i * heads * width, (i + 1) * heads * width)
                token, state = key_head(
                    cells[0, i, k, 0],
                    cells[0, i, k, 1],
                    query[at][:, keys],
                    key[at][:, keys],
                    value[at][:, values].astype(jnp.float32),
                    gate[at][:, values].astype(jnp.float32),
                    strength[at][:, heads * i : heads * (i + 1)],
                    decay[at][:, heads * i : heads * (i + 1)],
                    gain[...],
                )
                tokens[0, 0, 0, k, :, values] = token.astype(tokens.dtype)
                for a in range(heads):
                    finals[0, 0, 0, k, heads * i + a] = state[:, a * width : (a + 1) * width]

        @pl.when(live[s] <= k)
        def _(k=k):
            tokens[0, 0, 0, k] = jnp.zeros(tokens.shape[4:], tokens.dtype)
            finals[0, 0, 0, k] = jnp.zeros(finals.shape[4:], finals.dtype)


def decode(live, arrived, queries, key_vectors, value_vectors, gate_inputs, strength, decay, gain):
    n_group = queries.shape[2]
    _, cap, heads, key_size, value_size = arrived.shape
    cells = arrived.reshape(n_group, SUBGROUPS, cap, heads, key_size, value_size)
    block_heads = SUBGROUPS * heads
    out_shape = (
        jax.ShapeDtypeStruct(value_vectors.shape, jnp.bfloat16),
        jax.ShapeDtypeStruct(
            (1, 1, n_group, cap, block_heads, key_size, value_size), jnp.float32
        ),
    )

    def per_source(shape):
        block = (1, 1, 1) + shape[3:]
        return pl.BlockSpec(block, lambda s: (0, 0, s) + (0,) * (len(shape) - 3))

    return pl.pallas_call(
        decode_kernel,
        grid=(n_group,),
        out_shape=out_shape,
        in_specs=[
            pl.BlockSpec(memory_space=pltpu.SMEM),
            pl.BlockSpec((1,) + cells.shape[1:], lambda s: (s, 0, 0, 0, 0, 0)),
            per_source(queries.shape),
            per_source(key_vectors.shape),
            per_source(value_vectors.shape),
            per_source(gate_inputs.shape),
            per_source(strength.shape),
            per_source(decay.shape),
            pl.BlockSpec((1, value_size), lambda s: (0, 0)),
        ],
        out_specs=tuple(per_source(o.shape) for o in out_shape),
        compiler_params=pltpu.CompilerParams(vmem_limit_bytes=32 * 1024 * 1024),
    )(live, cells, queries, key_vectors, value_vectors, gate_inputs, strength, decay, gain)


def local(states, placement, queries, key_vectors, value_vectors, gate_inputs, strength, decay, gain):
    n_group = lax.axis_size("group")
    placed = placement.reshape(placement.shape[0])
    cells, live = pack(placed, states, n_group)
    arrived = lax.all_to_all(cells, ("group", "sub"), split_axis=0, concat_axis=0, tiled=True)
    return decode(
        live,
        arrived,
        queries,
        key_vectors,
        value_vectors,
        gate_inputs,
        strength,
        decay,
        gain.reshape(1, gain.shape[0]),
    )


def solution(mesh):
    n_group, n_head = mesh.devices.shape
    quads = Mesh(
        mesh.devices.reshape(n_group, n_head // SUBGROUPS, SUBGROUPS), ("group", "block", "sub")
    )
    spread = P("group", ("block", "sub"))
    return jax.shard_map(
        local,
        mesh=quads,
        in_specs=(spread, P(), spread, spread, spread, spread, spread, spread, P()),
        out_specs=(spread, spread),
        check_vma=False,
    )
```

```python
import math

import jax
import jax.numpy as jnp
from jax import lax
from jax.experimental import pallas as pl
from jax.experimental.pallas import tpu as pltpu
from jax.sharding import Mesh
from jax.sharding import PartitionSpec as P

SUBGROUPS = 4
SLOT_CAP = 2
EPS = 1e-06


def pack_kernel(n_group, reqs, placed, states, cells, live, count, held, arrive, leave):
    group = lax.axis_index("group")
    mine = group * SUBGROUPS + lax.axis_index("sub")
    dec_groups = n_group * SUBGROUPS

    def clear(d, carry):
        count[d] = 0
        return carry

    lax.fori_loop(0, dec_groups, clear, 0)

    def fetch(r, carry):
        pltpu.make_async_copy(states.at[r], held.at[r], arrive.at[r]).start()
        return carry

    lax.fori_loop(0, reqs, fetch, 0, unroll=4)

    def send(r, carry):
        d = placed[group * reqs + r]
        rank = count[d]
        count[d] = rank + 1
        pltpu.make_async_copy(states.at[r], held.at[r], arrive.at[r]).wait()
        pltpu.make_async_copy(held.at[r], cells.at[d, rank], leave.at[r]).start()
        return carry

    lax.fori_loop(0, reqs, send, 0)

    for s in range(n_group):

        def tally(r, total, s=s):
            return total + jnp.where(placed[s * reqs + r] == mine, 1, 0)

        live[s] = lax.fori_loop(0, reqs, tally, 0, unroll=8)

    def drain(r, carry):
        pltpu.make_async_copy(held.at[r], cells.at[0, 0], leave.at[r]).wait()
        return carry

    lax.fori_loop(0, reqs, drain, 0, unroll=4)


def pack(placed, states, n_group):
    reqs, heads, key_size, value_size = states.shape
    cells = (n_group * SUBGROUPS, SLOT_CAP, heads, key_size, value_size)
    return pl.pallas_call(
        lambda *refs: pack_kernel(n_group, reqs, *refs),
        out_shape=(
            jax.ShapeDtypeStruct(cells, states.dtype),
            jax.ShapeDtypeStruct((n_group,), jnp.int32),
        ),
        in_specs=[
            pl.BlockSpec(memory_space=pltpu.SMEM),
            pl.BlockSpec(memory_space=pl.ANY),
        ],
        out_specs=(
            pl.BlockSpec(memory_space=pl.ANY),
            pl.BlockSpec(memory_space=pltpu.SMEM),
        ),
        scratch_shapes=[
            pltpu.SMEM((n_group * SUBGROUPS,), jnp.int32),
            pltpu.VMEM(states.shape, states.dtype),
            pltpu.SemaphoreType.DMA((reqs,)),
            pltpu.SemaphoreType.DMA((reqs,)),
        ],
        compiler_params=pltpu.CompilerParams(vmem_limit_bytes=16 * 1024 * 1024),
    )(placed, states)


def split(x):
    high = x.astype(jnp.bfloat16)
    return high, (x - high.astype(jnp.float32)).astype(jnp.bfloat16)


def pair(left, right, shape):
    return jnp.concatenate(
        [jnp.broadcast_to(left, shape), jnp.broadcast_to(right, shape)], axis=1
    )


def key_head(first, second, query, key, value, gate, strength, decay, gain):
    steps, size = key.shape
    half = (steps, first.shape[1])
    state = jnp.concatenate([first, second], axis=1)
    both = jnp.concatenate([key, query], axis=0)
    key_f, query_f = key.astype(jnp.float32), query.astype(jnp.float32)
    key_norm = lax.rsqrt(jnp.sum(key_f * key_f, axis=1, keepdims=True) + EPS)
    query_norm = lax.rsqrt(jnp.sum(query_f * query_f, axis=1, keepdims=True) + EPS) / math.sqrt(size)
    high, low = split(state)
    product = jnp.dot(
        jnp.concatenate([both, both], axis=1),
        jnp.concatenate([high, low], axis=0),
        preferred_element_type=jnp.float32,
    )
    gram = lax.dot_general(
        both, key, (((1,), (1,)), ((), ())), preferred_element_type=jnp.float32
    )
    decay_w = pair(decay[:, 0:1], decay[:, 1:2], half)
    norm_w = jnp.broadcast_to(key_norm, (steps, 2 * half[1]))
    write_w = pair(strength[:, 0:1], strength[:, 1:2], half) * norm_w
    row = lax.broadcasted_iota(jnp.int32, (steps, 2 * half[1]), 0)
    writes = jnp.zeros((steps, 2 * half[1]), jnp.float32)
    readout = writes
    kept = jnp.ones((1, 2 * half[1]), jnp.float32)
    for t in range(steps):
        fade = decay_w[t : t + 1]
        product = product * fade
        residual = value[t : t + 1] - norm_w[t : t + 1] * product[t : t + 1]
        write = write_w[t : t + 1] * residual
        product = product + gram[:, t : t + 1] * write
        readout = jnp.where(row == t, product[steps:], readout)
        writes = jnp.where(row == t, write, writes * fade)
        kept = kept * fade
    high, low = split(writes)
    update = lax.dot_general(
        jnp.concatenate([key, key], axis=0),
        jnp.concatenate([high, low], axis=0),
        (((0,), (0,)), ((), ())),
        preferred_element_type=jnp.float32,
    )
    state = kept * state + update
    readout = readout * query_norm
    halves = [readout[:, : half[1]], readout[:, half[1] :]]
    halves = [
        x * lax.rsqrt(jnp.mean(x * x, axis=1, keepdims=True) + EPS) * gain for x in halves
    ]
    token = jnp.concatenate(halves, axis=1) * (gate * jax.nn.sigmoid(gate))
    return token, state


def decode_kernel(live, cells, query, key, value, gate, strength, decay, gain, tokens, finals):
    s = pl.program_id(0)
    sources, heads = cells.shape[1], cells.shape[3]
    size, width = cells.shape[4], cells.shape[5]
    for k in range(SLOT_CAP):
        at = (0, 0, 0, k)

        @pl.when(live[s] > k)
        def _(k=k, at=at):
            for i in range(sources):
                keys = slice(i * size, (i + 1) * size)
                values = slice(i * heads * width, (i + 1) * heads * width)
                token, state = key_head(
                    cells[0, i, k, 0],
                    cells[0, i, k, 1],
                    query[at][:, keys],
                    key[at][:, keys],
                    value[at][:, values].astype(jnp.float32),
                    gate[at][:, values].astype(jnp.float32),
                    strength[at][:, heads * i : heads * (i + 1)],
                    decay[at][:, heads * i : heads * (i + 1)],
                    gain[...],
                )
                tokens[0, 0, 0, k, :, values] = token.astype(tokens.dtype)
                for a in range(heads):
                    finals[0, 0, 0, k, heads * i + a] = state[:, a * width : (a + 1) * width]

        @pl.when(live[s] <= k)
        def _(k=k):
            tokens[0, 0, 0, k] = jnp.zeros(tokens.shape[4:], tokens.dtype)
            finals[0, 0, 0, k] = jnp.zeros(finals.shape[4:], finals.dtype)


def decode(live, arrived, queries, key_vectors, value_vectors, gate_inputs, strength, decay, gain):
    n_group = queries.shape[2]
    _, cap, heads, key_size, value_size = arrived.shape
    cells = arrived.reshape(n_group, SUBGROUPS, cap, heads, key_size, value_size)
    block_heads = SUBGROUPS * heads
    out_shape = (
        jax.ShapeDtypeStruct(value_vectors.shape, jnp.bfloat16),
        jax.ShapeDtypeStruct(
            (1, 1, n_group, cap, block_heads, key_size, value_size), jnp.float32
        ),
    )

    def per_source(shape):
        block = (1, 1, 1) + shape[3:]
        return pl.BlockSpec(block, lambda s: (0, 0, s) + (0,) * (len(shape) - 3))

    return pl.pallas_call(
        decode_kernel,
        grid=(n_group,),
        out_shape=out_shape,
        in_specs=[
            pl.BlockSpec(memory_space=pltpu.SMEM),
            pl.BlockSpec((1,) + cells.shape[1:], lambda s: (s, 0, 0, 0, 0, 0)),
            per_source(queries.shape),
            per_source(key_vectors.shape),
            per_source(value_vectors.shape),
            per_source(gate_inputs.shape),
            per_source(strength.shape),
            per_source(decay.shape),
            pl.BlockSpec((1, value_size), lambda s: (0, 0)),
        ],
        out_specs=tuple(per_source(o.shape) for o in out_shape),
        compiler_params=pltpu.CompilerParams(vmem_limit_bytes=32 * 1024 * 1024),
    )(live, cells, queries, key_vectors, value_vectors, gate_inputs, strength, decay, gain)


def local(states, placement, queries, key_vectors, value_vectors, gate_inputs, strength, decay, gain):
    n_group = lax.axis_size("group")
    placed = placement.reshape(placement.shape[0])
    cells, live = pack(placed, states, n_group)
    arrived = lax.all_to_all(cells, ("group", "sub"), split_axis=0, concat_axis=0, tiled=True)
    return decode(
        live,
        arrived,
        queries,
        key_vectors,
        value_vectors,
        gate_inputs,
        strength,
        decay,
        gain.reshape(1, gain.shape[0]),
    )


def solution(mesh):
    n_group, n_head = mesh.devices.shape
    quads = Mesh(
        mesh.devices.reshape(n_group, n_head // SUBGROUPS, SUBGROUPS), ("group", "block", "sub")
    )
    spread = P("group", ("block", "sub"))
    return jax.shard_map(
        local,
        mesh=quads,
        in_specs=(spread, P(), spread, spread, spread, spread, spread, spread, P()),
        out_specs=(spread, spread),
        check_vma=False,
    )
```

```python
import math

import jax
import jax.numpy as jnp
from jax import lax
from jax.experimental import pallas as pl
from jax.experimental.pallas import tpu as pltpu
from jax.sharding import Mesh
from jax.sharding import PartitionSpec as P

SUBGROUPS = 4
SLOT_CAP = 2
EPS = 1e-06


def pack_kernel(n_group, reqs, placed, states, cells, live, count, sems):
    group = lax.axis_index("group")
    mine = group * SUBGROUPS + lax.axis_index("sub")

    def clear(d, carry):
        count[d] = 0
        return carry

    lax.fori_loop(0, n_group * SUBGROUPS, clear, 0, unroll=8)

    def send(r, carry):
        d = placed[group * reqs + r]
        rank = count[d]
        count[d] = rank + 1
        pltpu.make_async_copy(states.at[r], cells.at[d, rank], sems.at[r]).start()
        return carry

    lax.fori_loop(0, reqs, send, 0, unroll=4)

    for s in range(n_group):

        def tally(r, total, s=s):
            return total + jnp.where(placed[s * reqs + r] == mine, 1, 0)

        live[s] = lax.fori_loop(0, reqs, tally, 0, unroll=8)

    def drain(r, carry):
        pltpu.make_async_copy(states.at[r], cells.at[0, 0], sems.at[r]).wait()
        return carry

    lax.fori_loop(0, reqs, drain, 0, unroll=4)


def pack(placed, states, n_group):
    reqs, heads, key_size, value_size = states.shape
    cells = (n_group * SUBGROUPS, SLOT_CAP, heads, key_size, value_size)
    return pl.pallas_call(
        lambda *refs: pack_kernel(n_group, reqs, *refs),
        out_shape=(
            pltpu.VMEM(cells, states.dtype),
            jax.ShapeDtypeStruct((n_group,), jnp.int32),
        ),
        in_specs=[
            pl.BlockSpec(memory_space=pltpu.SMEM),
            pl.BlockSpec(memory_space=pltpu.HBM),
        ],
        out_specs=(
            pl.BlockSpec(memory_space=pltpu.VMEM),
            pl.BlockSpec(memory_space=pltpu.SMEM),
        ),
        scratch_shapes=[
            pltpu.SMEM((n_group * SUBGROUPS,), jnp.int32),
            pltpu.SemaphoreType.DMA((reqs,)),
        ],
        compiler_params=pltpu.CompilerParams(vmem_limit_bytes=32 * 1024 * 1024),
    )(placed, pltpu.with_memory_space_constraint(states, pltpu.HBM))


def split(x):
    high = x.astype(jnp.bfloat16)
    return high, (x - high.astype(jnp.float32)).astype(jnp.bfloat16)


def wide(columns, width):
    return jnp.concatenate(
        [jnp.broadcast_to(c, (c.shape[0], width)) for c in columns], axis=1
    )


def decode_kernel(
    live, cells, query, key, value, gate, strength, decay, gain, tokens, finals,
    by_key, by_query, gram_key, gram_query, values, fades, writes, key_norms, kept,
):
    s = pl.program_id(0)
    sources, heads, size, width = cells.shape[1], cells.shape[3], cells.shape[4], cells.shape[5]
    steps = key.shape[4]
    units = [(k, i) for k in range(SLOT_CAP) for i in range(sources)]
    count = len(units)

    def keys(i):
        return slice(i * size, (i + 1) * size)

    def lanes(i):
        return slice(i * heads * width, (i + 1) * heads * width)

    def state_of(k, i):
        return jnp.concatenate([cells[0, i, k, a] for a in range(heads)], axis=1)

    def spread(ref, u, x):
        for a in range(heads):
            ref[a, pl.ds(u, steps, stride=count), :] = x[:, a * width : (a + 1) * width]

    def gather(ref, u):
        return jnp.concatenate(
            [ref[a, pl.ds(u, steps, stride=count), :] for a in range(heads)], axis=1
        )

    for u, (k, i) in enumerate(units):
        key_f = key[0, 0, 0, k, :, keys(i)].astype(jnp.float32)
        query_f = query[0, 0, 0, k, :, keys(i)].astype(jnp.float32)
        both = jnp.concatenate([key_f, query_f], axis=0).astype(jnp.bfloat16)
        high, low = split(state_of(k, i))
        product = jnp.dot(
            jnp.concatenate([both, both], axis=1),
            jnp.concatenate([high, low], axis=0),
            preferred_element_type=jnp.float32,
        )
        gram = lax.dot_general(
            both,
            key_f.astype(jnp.bfloat16),
            (((1,), (1,)), ((), ())),
            preferred_element_type=jnp.float32,
        )
        norm = lax.rsqrt(jnp.sum(key_f * key_f, axis=1, keepdims=True) + EPS)
        both_heads = [heads * i + a for a in range(heads)]
        spread(by_key, u, product[:steps])
        spread(by_query, u, product[steps:])
        gram_key[pl.ds(u, steps, stride=count), :] = gram[:steps]
        gram_query[pl.ds(u, steps, stride=count), :] = gram[steps:]
        spread(values, u, value[0, 0, 0, k, :, lanes(i)].astype(jnp.float32))
        spread(fades, u, wide([decay[0, 0, 0, k, :, h : h + 1] for h in both_heads], width))
        spread(
            writes, u, wide([strength[0, 0, 0, k, :, h : h + 1] * norm for h in both_heads], width)
        )
        key_norms[pl.ds(u, steps, stride=count), :] = wide([norm], width)

    def rows(t):
        return slice(t * count, (t + 1) * count)

    on_key = [[by_key[a, rows(t)] for a in range(heads)] for t in range(steps)]
    on_query = [[by_query[a, rows(t)] for a in range(heads)] for t in range(steps)]
    written, total = [], None
    for t in range(steps):
        fade = [fades[a, rows(t)] for a in range(heads)]
        total = fade if total is None else [x * f for x, f in zip(total, fade)]
        norm = key_norms[rows(t)]
        write = []
        for a in range(heads):
            residual = values[a, rows(t)] - norm * (on_key[t][a] * fade[a])
            write.append(writes[a, rows(t)] * residual)
        written = [[w * f for w, f in zip(old, fade)] for old in written] + [write]
        for later in range(t, steps):
            for on, grams in ((on_key, gram_key), (on_query, gram_query)):
                if on is on_query or later > t:
                    dot = jnp.broadcast_to(grams[rows(later)][:, t : t + 1], norm.shape)
                    on[later] = [x * f + dot * w for x, f, w in zip(on[later], fade, write)]
    kept[...] = jnp.concatenate(total, axis=1)
    for t in range(steps):
        for a in range(heads):
            by_key[a, rows(t)] = written[t][a]
            by_query[a, rows(t)] = on_query[t][a]

    for u, (k, i) in enumerate(units):
        key_f = key[0, 0, 0, k, :, keys(i)].astype(jnp.float32)
        query_f = query[0, 0, 0, k, :, keys(i)].astype(jnp.float32)
        high, low = split(gather(by_key, u))
        update = lax.dot_general(
            jnp.concatenate([key_f, key_f], axis=0).astype(jnp.bfloat16),
            jnp.concatenate([high.astype(jnp.float32), low.astype(jnp.float32)], axis=0).astype(
                jnp.bfloat16
            ),
            (((0,), (0,)), ((), ())),
            preferred_element_type=jnp.float32,
        )
        state = kept[u : u + 1, :] * state_of(k, i) + update
        for a in range(heads):
            finals[0, 0, 0, k, heads * i + a] = state[:, a * width : (a + 1) * width]
        norm = lax.rsqrt(jnp.sum(query_f * query_f, axis=1, keepdims=True) + EPS) / math.sqrt(size)
        readout = gather(by_query, u) * norm
        normed = []
        for a in range(heads):
            x = readout[:, a * width : (a + 1) * width]
            normed.append(x * lax.rsqrt(jnp.mean(x * x, axis=1, keepdims=True) + EPS) * gain[...])
        opened = gate[0, 0, 0, k, :, lanes(i)].astype(jnp.float32)
        token = jnp.concatenate(normed, axis=1) * (opened * jax.nn.sigmoid(opened))
        tokens[0, 0, 0, k, :, lanes(i)] = token.astype(tokens.dtype)

    for k in range(SLOT_CAP):

        @pl.when(live[s] <= k)
        def _(k=k):
            tokens[0, 0, 0, k] = jnp.zeros(tokens.shape[4:], tokens.dtype)
            finals[0, 0, 0, k] = jnp.zeros(finals.shape[4:], finals.dtype)


def decode(
    live, arrived, queries, key_vectors, value_vectors, gate_inputs, strength, decay, gain, space=None
):
    n_group = queries.shape[2]
    _, cap, heads, key_size, value_size = arrived.shape
    cells = arrived.reshape(n_group, SUBGROUPS, cap, heads, key_size, value_size)
    if space is not None:
        cells = pltpu.with_memory_space_constraint(cells, space)
    block_heads = SUBGROUPS * heads
    out_shape = (
        jax.ShapeDtypeStruct(value_vectors.shape, jnp.bfloat16),
        jax.ShapeDtypeStruct(
            (1, 1, n_group, cap, block_heads, key_size, value_size), jnp.float32
        ),
    )

    steps, units = queries.shape[4], cap * SUBGROUPS
    rows = steps * units
    by_step = (heads, rows, value_size)
    scratch = [by_step, by_step, (rows, steps), (rows, steps), by_step, by_step, by_step]
    scratch += [(rows, value_size), (units, heads * value_size)]

    def per_source(shape):
        block = (1, 1, 1) + shape[3:]
        return pl.BlockSpec(block, lambda s: (0, 0, s) + (0,) * (len(shape) - 3))

    return pl.pallas_call(
        decode_kernel,
        grid=(n_group,),
        out_shape=out_shape,
        in_specs=[
            pl.BlockSpec(memory_space=pltpu.SMEM),
            pl.BlockSpec((1,) + cells.shape[1:], lambda s: (s, 0, 0, 0, 0, 0)),
            per_source(queries.shape),
            per_source(key_vectors.shape),
            per_source(value_vectors.shape),
            per_source(gate_inputs.shape),
            per_source(strength.shape),
            per_source(decay.shape),
            pl.BlockSpec((1, value_size), lambda s: (0, 0)),
        ],
        out_specs=tuple(per_source(o.shape) for o in out_shape),
        scratch_shapes=[pltpu.VMEM(shape, jnp.float32) for shape in scratch],
        compiler_params=pltpu.CompilerParams(vmem_limit_bytes=32 * 1024 * 1024),
    )(live, cells, queries, key_vectors, value_vectors, gate_inputs, strength, decay, gain)


def local(states, placement, queries, key_vectors, value_vectors, gate_inputs, strength, decay, gain):
    n_group = lax.axis_size("group")
    placed = placement.reshape(placement.shape[0])
    cells, live = pack(placed, states, n_group)
    arrived = lax.all_to_all(cells, ("group", "sub"), split_axis=0, concat_axis=0, tiled=True)
    return decode(
        live,
        arrived,
        queries,
        key_vectors,
        value_vectors,
        gate_inputs,
        strength,
        decay,
        gain.reshape(1, gain.shape[0]),
    )


def solution(mesh):
    n_group, n_head = mesh.devices.shape
    quads = Mesh(
        mesh.devices.reshape(n_group, n_head // SUBGROUPS, SUBGROUPS), ("group", "block", "sub")
    )
    spread = P("group", ("block", "sub"))
    return jax.shard_map(
        local,
        mesh=quads,
        in_specs=(spread, P(), spread, spread, spread, spread, spread, spread, P()),
        out_specs=(spread, spread),
        check_vma=False,
    )
```

```python
import math

import jax
import jax.numpy as jnp
from jax import lax
from jax.experimental import pallas as pl
from jax.experimental.pallas import tpu as pltpu
from jax.sharding import Mesh
from jax.sharding import PartitionSpec as P

SUBGROUPS = 4
SLOT_CAP = 2
CORES = 2
SOURCES = 2
EPS = 1e-06


def pack_kernel(n_group, reqs, spare, placed, states, cells, live, count, sems):
    group = lax.axis_index("group")
    mine = group * SUBGROUPS + lax.axis_index("sub")
    heads = states.shape[1]

    def clear(d, carry):
        count[d] = 0
        return carry

    lax.fori_loop(0, n_group * SUBGROUPS, clear, 0, unroll=8)

    def send(r, carry):
        d = placed[group * reqs + r]
        rank = count[d]
        count[d] = rank + 1
        if spare:

            @pl.when(rank == 0)
            def _():
                pltpu.make_async_copy(
                    states.at[r], cells.at[d, pl.ds(0, heads)], sems.at[r]
                ).start()

            @pl.when(rank > 0)
            def _():
                for a in range(heads):
                    pltpu.make_async_copy(
                        states.at[r, a], cells.at[d // CORES * CORES + a, heads], sems.at[r]
                    ).start()

        else:
            pltpu.make_async_copy(states.at[r], cells.at[d, rank], sems.at[r]).start()
        return carry

    lax.fori_loop(0, reqs, send, 0, unroll=4)

    for s in range(n_group):

        def tally(r, total, s=s):
            return total + jnp.where(placed[s * reqs + r] == mine, 1, 0)

        live[s] = lax.fori_loop(0, reqs, tally, 0, unroll=8)

    def drain(r, carry):
        landed = cells.at[0, pl.ds(0, heads)] if spare else cells.at[0, 0]
        pltpu.make_async_copy(states.at[r], landed, sems.at[r]).wait()
        return carry

    lax.fori_loop(0, reqs, drain, 0, unroll=4)


def pack(placed, states, n_group, spare):
    reqs, heads, key_size, value_size = states.shape
    cell = (heads + 1,) if spare else (SLOT_CAP, heads)
    cells = (n_group * SUBGROUPS,) + cell + (key_size, value_size)
    return pl.pallas_call(
        lambda *refs: pack_kernel(n_group, reqs, spare, *refs),
        out_shape=(
            pltpu.VMEM(cells, states.dtype),
            jax.ShapeDtypeStruct((n_group,), jnp.int32),
        ),
        in_specs=[
            pl.BlockSpec(memory_space=pltpu.SMEM),
            pl.BlockSpec(memory_space=pltpu.HBM),
        ],
        out_specs=(
            pl.BlockSpec(memory_space=pltpu.VMEM),
            pl.BlockSpec(memory_space=pltpu.SMEM),
        ),
        scratch_shapes=[
            pltpu.SMEM((n_group * SUBGROUPS,), jnp.int32),
            pltpu.SemaphoreType.DMA((reqs,)),
        ],
        compiler_params=pltpu.CompilerParams(vmem_limit_bytes=32 * 1024 * 1024),
    )(placed, pltpu.with_memory_space_constraint(states, pltpu.HBM))


def split(x):
    high = x.astype(jnp.bfloat16)
    return high, (x - high.astype(jnp.float32)).astype(jnp.bfloat16)


def wide(columns, width):
    return jnp.concatenate(
        [jnp.broadcast_to(c, (c.shape[0], width)) for c in columns], axis=1
    )


def decode_kernel(
    load, slot, first, live, query, key, value, gate, strength, decay, gain, tokens, finals,
    by_key, by_query, gram_key, gram_query, values, fades, writes, key_norms, kept,
):
    size, width = finals.shape[5], finals.shape[6]
    heads = finals.shape[4] // SUBGROUPS
    steps = key.shape[4]
    units = [(n, i) for n in range(SOURCES) for i in range(SUBGROUPS)]
    count = len(units)

    def keys(i):
        return slice(i * size, (i + 1) * size)

    def lanes(i):
        return slice(i * heads * width, (i + 1) * heads * width)

    def state_of(n, i):
        return jnp.concatenate(load(n, i), axis=1)

    def spread(ref, u, x):
        for a in range(heads):
            ref[a, pl.ds(u, steps, stride=count), :] = x[:, a * width : (a + 1) * width]

    def gather(ref, u):
        return jnp.concatenate(
            [ref[a, pl.ds(u, steps, stride=count), :] for a in range(heads)], axis=1
        )

    for u, (n, i) in enumerate(units):
        key_f = key[0, 0, n, 0, :, keys(i)].astype(jnp.float32)
        query_f = query[0, 0, n, 0, :, keys(i)].astype(jnp.float32)
        both = jnp.concatenate([key_f, query_f], axis=0).astype(jnp.bfloat16)
        high, low = split(state_of(n, i))
        product = jnp.dot(
            jnp.concatenate([both, both], axis=1),
            jnp.concatenate([high, low], axis=0),
            preferred_element_type=jnp.float32,
        )
        gram = lax.dot_general(
            both,
            key_f.astype(jnp.bfloat16),
            (((1,), (1,)), ((), ())),
            preferred_element_type=jnp.float32,
        )
        norm = lax.rsqrt(jnp.sum(key_f * key_f, axis=1, keepdims=True) + EPS)
        both_heads = [heads * i + a for a in range(heads)]
        spread(by_key, u, product[:steps])
        spread(by_query, u, product[steps:])
        gram_key[pl.ds(u, steps, stride=count), :] = gram[:steps]
        gram_query[pl.ds(u, steps, stride=count), :] = gram[steps:]
        spread(values, u, value[0, 0, n, 0, :, lanes(i)].astype(jnp.float32))
        spread(fades, u, wide([decay[0, 0, n, 0, :, h : h + 1] for h in both_heads], width))
        spread(
            writes, u, wide([strength[0, 0, n, 0, :, h : h + 1] * norm for h in both_heads], width)
        )
        key_norms[pl.ds(u, steps, stride=count), :] = wide([norm], width)

    def rows(t):
        return slice(t * count, (t + 1) * count)

    on_key = [[by_key[a, rows(t)] for a in range(heads)] for t in range(steps)]
    on_query = [[by_query[a, rows(t)] for a in range(heads)] for t in range(steps)]
    written, total = [], None
    for t in range(steps):
        fade = [fades[a, rows(t)] for a in range(heads)]
        total = fade if total is None else [x * f for x, f in zip(total, fade)]
        norm = key_norms[rows(t)]
        write = []
        for a in range(heads):
            residual = values[a, rows(t)] - norm * (on_key[t][a] * fade[a])
            write.append(writes[a, rows(t)] * residual)
        written = [[w * f for w, f in zip(old, fade)] for old in written] + [write]
        for later in range(t, steps):
            for on, grams in ((on_key, gram_key), (on_query, gram_query)):
                if on is on_query or later > t:
                    dot = jnp.broadcast_to(grams[rows(later)][:, t : t + 1], norm.shape)
                    on[later] = [x * f + dot * w for x, f, w in zip(on[later], fade, write)]
    kept[...] = jnp.concatenate(total, axis=1)
    for t in range(steps):
        for a in range(heads):
            by_key[a, rows(t)] = written[t][a]
            by_query[a, rows(t)] = on_query[t][a]

    for u, (n, i) in enumerate(units):
        key_f = key[0, 0, n, 0, :, keys(i)].astype(jnp.float32)
        query_f = query[0, 0, n, 0, :, keys(i)].astype(jnp.float32)
        high, low = split(gather(by_key, u))
        update = lax.dot_general(
            jnp.concatenate([key_f, key_f], axis=0).astype(jnp.bfloat16),
            jnp.concatenate([high.astype(jnp.float32), low.astype(jnp.float32)], axis=0).astype(
                jnp.bfloat16
            ),
            (((0,), (0,)), ((), ())),
            preferred_element_type=jnp.float32,
        )
        state = kept[u : u + 1, :] * state_of(n, i) + update
        for a in range(heads):
            finals[0, 0, n, 0, heads * i + a] = state[:, a * width : (a + 1) * width]
        norm = lax.rsqrt(jnp.sum(query_f * query_f, axis=1, keepdims=True) + EPS) / math.sqrt(size)
        readout = gather(by_query, u) * norm
        normed = []
        for a in range(heads):
            x = readout[:, a * width : (a + 1) * width]
            normed.append(x * lax.rsqrt(jnp.mean(x * x, axis=1, keepdims=True) + EPS) * gain[...])
        opened = gate[0, 0, n, 0, :, lanes(i)].astype(jnp.float32)
        token = jnp.concatenate(normed, axis=1) * (opened * jax.nn.sigmoid(opened))
        tokens[0, 0, n, 0, :, lanes(i)] = token.astype(tokens.dtype)

    for n in range(SOURCES):

        @pl.when(live[first + n] <= slot)
        def _(n=n):
            tokens[0, 0, n, 0] = jnp.zeros(tokens.shape[4:], tokens.dtype)
            finals[0, 0, n, 0] = jnp.zeros(finals.shape[4:], finals.dtype)


def decode(live, sources, load, slot, small, gain, earlier=None):
    queries, values = small[0], small[2]
    n_group, cap, steps = queries.shape[2:5]
    key_size, value_size = queries.shape[5] // SUBGROUPS, gain.shape[1]
    heads = values.shape[5] // (SUBGROUPS * value_size)
    out_shape = (
        jax.ShapeDtypeStruct(values.shape, jnp.bfloat16),
        jax.ShapeDtypeStruct(
            (1, 1, n_group, cap, SUBGROUPS * heads, key_size, value_size), jnp.float32
        ),
    )
    units = SOURCES * SUBGROUPS
    rows = steps * units
    by_step = (heads, rows, value_size)
    scratch = [by_step, by_step, (rows, steps), (rows, steps), by_step, by_step, by_step]
    scratch += [(rows, value_size), (units, heads * value_size)]
    groups = n_group // SOURCES

    def slot_of(j):
        return j // groups if slot is None else slot

    def per_slot(shape):
        block = (1, 1, SOURCES, 1) + shape[4:]
        return pl.BlockSpec(
            block, lambda j: (0, 0, j % groups, slot_of(j)) + (0,) * (len(shape) - 4)
        )

    def source_spec(block, index):
        return pl.BlockSpec(block, lambda j: index(j % groups, slot_of(j)))

    kept = () if earlier is None else earlier

    def kernel(live, *refs):
        blocks, refs = refs[: len(sources)], refs[len(sources) :]
        ins, refs = refs[: len(small) + 1], refs[len(small) + 1 + len(kept) :]
        j = pl.program_id(0)
        decode_kernel(
            lambda n, i: load(n, i, *blocks), slot_of(j), (j % groups) * SOURCES, live, *ins, *refs
        )

    first_kept = 1 + len(sources) + len(small) + 1
    return pl.pallas_call(
        kernel,
        grid=(groups * (cap if slot is None else 1),),
        out_shape=out_shape,
        in_specs=[pl.BlockSpec(memory_space=pltpu.SMEM)]
        + [source_spec(block, index) for _, block, index in sources]
        + [per_slot(x.shape) for x in small]
        + [pl.BlockSpec(gain.shape, lambda j: (0, 0))]
        + [pl.BlockSpec(memory_space=pl.ANY)] * len(kept),
        out_specs=tuple(per_slot(o.shape) for o in out_shape),
        scratch_shapes=[pltpu.VMEM(shape, jnp.float32) for shape in scratch],
        input_output_aliases={first_kept + n: n for n in range(len(kept))},
        compiler_params=pltpu.CompilerParams(vmem_limit_bytes=32 * 1024 * 1024),
    )(live, *[x for x, _, _ in sources], *small, gain, *kept)


def exchange(cells):
    return lax.all_to_all(cells, ("group", "sub"), split_axis=0, concat_axis=0, tiled=True)


def with_spare(placed, states, small, gain, n_group):
    cells, live = pack(placed, states, n_group, True)
    heads, key_size, value_size = states.shape[1:]
    square = (key_size, value_size)
    arrived = exchange(cells)
    spare = arrived[:, heads]
    swap = [(n, n ^ 1) for n in range(SUBGROUPS)]
    other = lax.ppermute(spare, "sub", swap)
    by_source = arrived.reshape((n_group, SUBGROUPS, heads + 1) + square)
    other = other.reshape((n_group, SUBGROUPS) + square)
    firsts = (
        by_source,
        (SOURCES, SUBGROUPS, heads) + square,
        lambda group, slot: (group, 0, 0, 0, 0),
    )
    earlier = decode(
        live, [firsts], lambda n, i, x: [x[n, i, a] for a in range(heads)], 0, small, gain
    )
    own = (by_source, (SOURCES, SUBGROUPS, 1) + square, lambda group, slot: (group, 0, heads, 0, 0))
    theirs = (other, (SOURCES, SUBGROUPS) + square, lambda group, slot: (group, 0, 0, 0))

    def load(n, i, x, y):
        core = lax.axis_index("sub") % CORES
        return [jnp.where(core == a, x[n, i, 0], y[n, i]) for a in range(heads)]

    return decode(live, [own, theirs], load, 1, small, gain, earlier)


def without_spare(placed, states, small, gain, n_group):
    cells, live = pack(placed, states, n_group, False)
    heads, key_size, value_size = states.shape[1:]
    square = (key_size, value_size)
    arrived = exchange(cells).reshape((n_group, SUBGROUPS, SLOT_CAP, heads) + square)
    block = (SOURCES, SUBGROUPS, 1, heads) + square
    slots = (arrived, block, lambda group, slot: (group, 0, slot, 0, 0, 0))
    return decode(
        live, [slots], lambda n, i, x: [x[n, i, 0, a] for a in range(heads)], None, small, gain
    )


def local(states, placement, queries, key_vectors, value_vectors, gate_inputs, strength, decay, gain):
    n_group = lax.axis_size("group")
    placed = placement.reshape(placement.shape[0])
    chips = placed.reshape(n_group, -1, 1) // CORES
    named = chips == jnp.arange(n_group * SUBGROUPS // CORES, dtype=jnp.int32)
    fits = jnp.all(jnp.sum(named.astype(jnp.int32), axis=1) <= SLOT_CAP + 1)
    small = (queries, key_vectors, value_vectors, gate_inputs, strength, decay)
    gain = gain.reshape(1, gain.shape[0])
    return lax.cond(
        fits,
        lambda *x: with_spare(*x, n_group),
        lambda *x: without_spare(*x, n_group),
        placed,
        states,
        small,
        gain,
    )


def solution(mesh):
    n_group, n_head = mesh.devices.shape
    quads = Mesh(
        mesh.devices.reshape(n_group, n_head // SUBGROUPS, SUBGROUPS), ("group", "block", "sub")
    )
    spread = P("group", ("block", "sub"))
    return jax.shard_map(
        local,
        mesh=quads,
        in_specs=(spread, P(), spread, spread, spread, spread, spread, spread, P()),
        out_specs=(spread, spread),
        check_vma=False,
    )
```

```python
import math

import jax
import jax.numpy as jnp
from jax import lax
from jax.experimental import pallas as pl
from jax.experimental.pallas import tpu as pltpu
from jax.sharding import Mesh
from jax.sharding import PartitionSpec as P

SUBGROUPS = 4
SLOT_CAP = 2
CORES = 2
SOURCES = 2
EPS = 1e-06


def pack_kernel(n_group, reqs, spare, placed, states, cells, info, count, sent, sems):
    group = lax.axis_index("group")
    mine = group * SUBGROUPS + lax.axis_index("sub")
    heads = states.shape[1]
    dec_groups = n_group * SUBGROUPS

    def clear(d, carry):
        count[d] = 0
        return carry

    lax.fori_loop(0, dec_groups + dec_groups // CORES, clear, 0, unroll=8)

    def send(r, carry):
        d = placed[group * reqs + r]
        rank = count[d]
        count[d] = rank + 1
        if spare:
            chip = d // CORES
            used = count[dec_groups + chip]
            count[dec_groups + chip] = used + rank
            sent[r] = jnp.where(used * rank == 0, 1, 0)

            @pl.when(rank == 0)
            def _():
                pltpu.make_async_copy(
                    states.at[r], cells.at[d, pl.ds(0, heads)], sems.at[r]
                ).start()

            @pl.when(rank * (1 - used) > 0)
            def _():
                for a in range(heads):
                    pltpu.make_async_copy(
                        states.at[r, a], cells.at[chip * CORES + a, heads], sems.at[r]
                    ).start()

        else:
            pltpu.make_async_copy(states.at[r], cells.at[d, rank], sems.at[r]).start()
        return carry

    lax.fori_loop(0, reqs, send, 0, unroll=4)

    full = 0
    for s in range(n_group):

        def tally(r, sums, s=s):
            live, low, high = sums
            d = placed[s * reqs + r]
            chip = d // CORES
            one = lax.shift_left(1, 4 * (chip % 8))
            live = live + jnp.where(d == mine, 1, 0)
            return live, low + jnp.where(chip < 8, one, 0), high + jnp.where(chip < 8, 0, one)

        live, low, high = lax.fori_loop(0, reqs, tally, (0, 0, 0), unroll=8)
        info[s] = live
        full = full | ((low | high) & 0x44444444)
    info[n_group] = jnp.where(full == 0, 1, 0)

    def drain(r, carry):
        if spare:

            @pl.when(sent[r] > 0)
            def _():
                landed = cells.at[0, pl.ds(0, heads)]
                pltpu.make_async_copy(states.at[r], landed, sems.at[r]).wait()

        else:
            pltpu.make_async_copy(states.at[r], cells.at[0, 0], sems.at[r]).wait()
        return carry

    lax.fori_loop(0, reqs, drain, 0, unroll=4)


def pack(placed, states, n_group, spare):
    reqs, heads, key_size, value_size = states.shape
    cell = (heads + 1,) if spare else (SLOT_CAP, heads)
    dec_groups = n_group * SUBGROUPS
    cells = (dec_groups,) + cell + (key_size, value_size)
    return pl.pallas_call(
        lambda *refs: pack_kernel(n_group, reqs, spare, *refs),
        out_shape=(
            pltpu.VMEM(cells, states.dtype),
            jax.ShapeDtypeStruct((n_group + 1,), jnp.int32),
        ),
        in_specs=[
            pl.BlockSpec(memory_space=pltpu.SMEM),
            pl.BlockSpec(memory_space=pltpu.HBM),
        ],
        out_specs=(
            pl.BlockSpec(memory_space=pltpu.VMEM),
            pl.BlockSpec(memory_space=pltpu.SMEM),
        ),
        scratch_shapes=[
            pltpu.SMEM((dec_groups + dec_groups // CORES,), jnp.int32),
            pltpu.SMEM((reqs,), jnp.int32),
            pltpu.SemaphoreType.DMA((reqs,)),
        ],
        compiler_params=pltpu.CompilerParams(vmem_limit_bytes=32 * 1024 * 1024),
    )(placed, pltpu.with_memory_space_constraint(states, pltpu.HBM))


def split(x):
    high = x.astype(jnp.bfloat16)
    return high, (x - high.astype(jnp.float32)).astype(jnp.bfloat16)


def row_sums(parts):
    rows, lanes = parts[0].shape
    high, low = split(jnp.concatenate(parts, axis=0))
    sums = jnp.dot(
        jnp.concatenate([high, low], axis=1),
        jnp.ones((2 * lanes, lanes), jnp.bfloat16),
        preferred_element_type=jnp.float32,
    )
    return [sums[n * rows : (n + 1) * rows] for n in range(len(parts))]


def widen(columns, width):
    rows, count = columns.shape
    high, rest = split(columns)
    low = columns - high.astype(jnp.float32) - rest.astype(jnp.float32)
    parts = [high.astype(jnp.float32), rest.astype(jnp.float32), low]
    lane = lax.broadcasted_iota(jnp.int32, (count, count * width), 1)
    column = lax.broadcasted_iota(jnp.int32, (count, count * width), 0)
    wide = jnp.dot(
        jnp.concatenate(parts, axis=0).astype(jnp.bfloat16),
        jnp.where(lane // width == column, 1.0, 0.0).astype(jnp.bfloat16),
        preferred_element_type=jnp.float32,
    )
    return wide[:rows] + wide[rows : 2 * rows] + wide[2 * rows :]


def decode_kernel(
    load, chosen, slot, first, live, query, key, value, gate, strength, decay, gain, tokens, states,
    by_key, by_query, values, fades, writes, key_rows, query_rows, kept,
):
    size, width = states.shape[2:]
    heads = states.shape[1] // SUBGROUPS
    steps = key.shape[4]
    units = [(n, i) for n in range(SOURCES) for i in range(SUBGROUPS)]
    count = len(units)

    def keys(i):
        return slice(i * size, (i + 1) * size)

    def lanes(i):
        return slice(i * heads * width, (i + 1) * heads * width)

    def state_of(n, i):
        return jnp.concatenate(
            [states[first + n, heads * i + a] for a in range(heads)]
            if chosen
            else load(first + n, i),
            axis=1,
        )

    def rows(t):
        return slice(t * count, (t + 1) * count)

    def spread(ref, u, x):
        for a in range(heads):
            ref[a, pl.ds(u, steps, stride=count), :] = x[:, a * width : (a + 1) * width]

    def gather(ref, u):
        return jnp.concatenate(
            [ref[a, pl.ds(u, steps, stride=count), :] for a in range(heads)], axis=1
        )

    wide = widen(
        jnp.concatenate(
            [x[0, 0, first + n, slot] for x in (decay, strength) for n in range(SOURCES)], axis=0
        ),
        width,
    )
    for u, (n, i) in enumerate(units):
        key_f = key[0, 0, first + n, slot, :, keys(i)].astype(jnp.float32)
        query_f = query[0, 0, first + n, slot, :, keys(i)].astype(jnp.float32)
        both = jnp.concatenate([key_f, query_f], axis=0).astype(jnp.bfloat16)
        before = load(first + n, i)
        if chosen:
            for a in range(heads):
                states[first + n, heads * i + a] = before[a]
        high, low = split(jnp.concatenate(before, axis=1))
        product = jnp.dot(
            jnp.concatenate([both, both], axis=1),
            jnp.concatenate([high, low], axis=0),
            preferred_element_type=jnp.float32,
        )
        spread(by_key, u, product[:steps])
        spread(by_query, u, product[steps:])
        key_rows[pl.ds(u, steps, stride=count), :] = key_f
        query_rows[pl.ds(u, steps, stride=count), :] = query_f
        spread(values, u, value[0, 0, first + n, slot, :, lanes(i)].astype(jnp.float32))
        spread(fades, u, wide[n * steps : (n + 1) * steps, lanes(i)])
        spread(writes, u, wide[(SOURCES + n) * steps : (SOURCES + n + 1) * steps, lanes(i)])

    on_key = [[by_key[a, rows(t)] for a in range(heads)] for t in range(steps)]
    on_query = [[by_query[a, rows(t)] for a in range(heads)] for t in range(steps)]
    keyed = [key_rows[rows(t)] for t in range(steps)]
    asked = [query_rows[rows(t)] for t in range(steps)]
    pairs = [(l, t) for t in range(steps) for l in range(t, steps)]
    key_key = dict(zip(pairs, row_sums([keyed[l] * keyed[t] for l, t in pairs])))
    query_key = dict(zip(pairs, row_sums([asked[l] * keyed[t] for l, t in pairs])))
    query_norms = [lax.rsqrt(x + EPS) / math.sqrt(size) for x in row_sums([q * q for q in asked])]
    written, total = [], None
    for t in range(steps):
        fade = [fades[a, rows(t)] for a in range(heads)]
        total = fade if total is None else [x * f for x, f in zip(total, fade)]
        norm = lax.rsqrt(key_key[t, t] + EPS)
        write = []
        for a in range(heads):
            residual = values[a, rows(t)] - norm * (on_key[t][a] * fade[a])
            write.append(writes[a, rows(t)] * norm * residual)
        written = [[w * f for w, f in zip(old, fade)] for old in written] + [write]
        for later in range(t, steps):
            for on, dots in ((on_key, key_key), (on_query, query_key)):
                if on is on_query or later > t:
                    dot = dots[later, t]
                    on[later] = [x * f + dot * w for x, f, w in zip(on[later], fade, write)]
    kept[...] = jnp.concatenate(total, axis=1)
    readouts = [x * query_norms[t] for t in range(steps) for x in on_query[t]]
    squares = row_sums([x * x for x in readouts])
    for t in range(steps):
        for a in range(heads):
            by_key[a, rows(t)] = written[t][a]
            norm = lax.rsqrt(squares[t * heads + a] / width + EPS)
            by_query[a, rows(t)] = readouts[t * heads + a] * norm * gain[...]

    for u, (n, i) in enumerate(units):
        key_f = key[0, 0, first + n, slot, :, keys(i)].astype(jnp.float32)
        high, low = split(gather(by_key, u))
        update = lax.dot_general(
            jnp.concatenate([key_f, key_f], axis=0).astype(jnp.bfloat16),
            jnp.concatenate([high.astype(jnp.float32), low.astype(jnp.float32)], axis=0).astype(
                jnp.bfloat16
            ),
            (((0,), (0,)), ((), ())),
            preferred_element_type=jnp.float32,
        )
        state = kept[u : u + 1, :] * state_of(n, i) + update
        for a in range(heads):
            states[first + n, heads * i + a] = state[:, a * width : (a + 1) * width]
        opened = gate[0, 0, first + n, slot, :, lanes(i)].astype(jnp.float32)
        token = gather(by_query, u) * (opened * jax.nn.sigmoid(opened))
        tokens[first + n, :, lanes(i)] = token.astype(tokens.dtype)

    for n in range(SOURCES):

        @pl.when(live[first + n] <= slot)
        def _(n=n):
            tokens[first + n] = jnp.zeros(tokens.shape[1:], tokens.dtype)
            states[first + n] = jnp.zeros(states.shape[1:], states.dtype)


def decode(live, sources, load, slot, small, gain, earlier=None):
    queries, values = small[0], small[2]
    n_group, cap, steps = queries.shape[2:5]
    key_size, value_size = queries.shape[5] // SUBGROUPS, gain.shape[1]
    heads = values.shape[5] // (SUBGROUPS * value_size)
    block = (SUBGROUPS * heads, key_size, value_size)
    units = SOURCES * SUBGROUPS
    rows = steps * units
    by_step = (heads, rows, value_size)
    scratch = [by_step] * 5 + [(rows, key_size)] * 2 + [(units, heads * value_size)]
    kept = () if earlier is None else earlier

    def kernel(live, *refs):
        blocks, refs = refs[: len(sources)], refs[len(sources) :]
        ins, refs = refs[: len(small) + 1], refs[len(small) + 1 :]
        before, refs = refs[: len(kept)], refs[len(kept) :]
        tokens, finals, states, sems, *work = refs
        if kept:
            result, tokens = tokens, work.pop()

        def place(batch):
            span = pl.ds(batch * SOURCES, SOURCES)
            return pltpu.make_async_copy(
                states.at[span], finals.at[0, 0, span, slot], sems.at[batch]
            )

        def run(batch, carry):
            mine = tokens.at[0, 0, :, slot] if kept else tokens
            decode_kernel(
                lambda s, i: load(s, i, *blocks), len(sources) > 1, slot, batch * SOURCES, live,
                *ins, mine, states, *work,
            )
            place(batch).start()
            return carry

        lax.fori_loop(0, n_group // SOURCES, run, 0)
        if kept:
            for s in range(n_group):
                tokens[0, 0, s, 0] = before[0][s]
            copy = pltpu.make_async_copy(tokens, result, sems.at[n_group // SOURCES])
            copy.start()
            copy.wait()
        for batch in range(n_group // SOURCES):
            place(batch).wait()

    vmem, any_space = pl.BlockSpec(memory_space=pltpu.VMEM), pl.BlockSpec(memory_space=pl.ANY)
    in_vmem = [pltpu.with_memory_space_constraint(x, pltpu.VMEM) for x in sources]
    tokens_shape = values.shape if kept else (n_group,) + values.shape[4:]
    return pl.pallas_call(
        kernel,
        out_shape=(
            jax.ShapeDtypeStruct(tokens_shape, jnp.bfloat16),
            jax.ShapeDtypeStruct((1, 1, n_group, cap) + block, jnp.float32),
        ),
        in_specs=[pl.BlockSpec(memory_space=pltpu.SMEM)]
        + [vmem] * (len(sources) + len(small) + 1)
        + [vmem, any_space][: len(kept)],
        out_specs=(any_space if kept else vmem, any_space),
        scratch_shapes=[
            pltpu.VMEM((n_group,) + block, jnp.float32),
            pltpu.SemaphoreType.DMA((n_group // SOURCES + 1,)),
        ]
        + [pltpu.VMEM(shape, jnp.float32) for shape in scratch]
        + [pltpu.VMEM(tokens_shape, jnp.bfloat16)] * bool(kept),
        input_output_aliases={len(sources) + len(small) + 3: 1} if kept else {},
        compiler_params=pltpu.CompilerParams(vmem_limit_bytes=32 * 1024 * 1024),
    )(live, *in_vmem, *small, gain, *kept)


def exchange(cells):
    return lax.all_to_all(cells, ("group", "sub"), split_axis=0, concat_axis=0, tiled=True)


def with_spare(cells, live, placed, states, small, gain, n_group):
    heads, key_size, value_size = states.shape[1:]
    square = (key_size, value_size)
    arrived = exchange(cells)
    spare = arrived[:, heads]
    swap = [(n, n ^ 1) for n in range(SUBGROUPS)]
    other = lax.ppermute(spare, "sub", swap)
    by_source = arrived.reshape((n_group, SUBGROUPS, heads + 1) + square)
    other = other.reshape((n_group, SUBGROUPS) + square)
    earlier = decode(
        live, [by_source], lambda s, i, x: [x[s, i, a] for a in range(heads)], 0, small, gain
    )

    def load(s, i, x, y):
        core = lax.axis_index("sub") % CORES
        return [jnp.where(core == a, x[s, i, heads], y[s, i]) for a in range(heads)]

    return decode(live, [by_source, other], load, 1, small, gain, earlier)


def without_spare(cells, live, placed, states, small, gain, n_group):
    cells, live = pack(placed, states, n_group, False)
    heads, key_size, value_size = states.shape[1:]
    square = (key_size, value_size)
    arrived = exchange(cells).reshape((n_group, SUBGROUPS, SLOT_CAP, heads) + square)
    earlier = None
    for slot in range(SLOT_CAP):
        earlier = decode(
            live,
            [arrived],
            lambda s, i, x, slot=slot: [x[s, i, slot, a] for a in range(heads)],
            slot,
            small,
            gain,
            earlier,
        )
    return earlier


def local(states, placement, queries, key_vectors, value_vectors, gate_inputs, strength, decay, gain):
    n_group = lax.axis_size("group")
    placed = placement.reshape(placement.shape[0])
    cells, info = pack(placed, states, n_group, True)
    small = (queries, key_vectors, value_vectors, gate_inputs, strength, decay)
    gain = gain.reshape(1, gain.shape[0])
    return lax.cond(
        info[n_group] > 0,
        lambda *x: with_spare(*x, n_group),
        lambda *x: without_spare(*x, n_group),
        cells,
        info,
        placed,
        states,
        small,
        gain,
    )


def solution(mesh):
    n_group, n_head = mesh.devices.shape
    quads = Mesh(
        mesh.devices.reshape(n_group, n_head // SUBGROUPS, SUBGROUPS), ("group", "block", "sub")
    )
    spread = P("group", ("block", "sub"))
    return jax.shard_map(
        local,
        mesh=quads,
        in_specs=(spread, P(), spread, spread, spread, spread, spread, spread, P()),
        out_specs=(spread, spread),
        check_vma=False,
    )
```

```python
import math

import jax
import jax.numpy as jnp
from jax import lax
from jax.experimental import pallas as pl
from jax.experimental.pallas import tpu as pltpu
from jax.sharding import Mesh
from jax.sharding import PartitionSpec as P

SUBGROUPS = 4
SLOT_CAP = 2
CORES = 2
SOURCES = 2
EPS = 1e-06


def fits_kernel(dec_groups, reqs, placed, fits):
    lanes = placed.shape[1]
    chips = placed[...] // CORES
    named = [jnp.where(chips == chip, 1.0, 0.0) for chip in range(dec_groups // CORES)]
    lane = lax.broadcasted_iota(jnp.int32, (lanes, lanes), 0)
    group = lax.broadcasted_iota(jnp.int32, (lanes, lanes), 1)
    counts = jnp.dot(
        jnp.concatenate(named, axis=0).astype(jnp.bfloat16),
        jnp.where(lane // reqs == group, 1.0, 0.0).astype(jnp.bfloat16),
        preferred_element_type=jnp.float32,
    )
    fits[0] = jnp.where(jnp.max(counts) < SLOT_CAP + 1.5, 1, 0)


def cells_fit(placed, dec_groups, reqs):
    return pl.pallas_call(
        lambda *refs: fits_kernel(dec_groups, reqs, *refs),
        out_shape=jax.ShapeDtypeStruct((1,), jnp.int32),
        in_specs=[pl.BlockSpec(memory_space=pltpu.VMEM)],
        out_specs=pl.BlockSpec(memory_space=pltpu.SMEM),
    )(placed.reshape(-1, 128))


def pack_kernel(n_group, reqs, spare, placed, states, cells, live, count, sems):
    group = lax.axis_index("group")
    mine = group * SUBGROUPS + lax.axis_index("sub")
    heads = states.shape[1]

    def clear(d, carry):
        count[d] = 0
        return carry

    lax.fori_loop(0, n_group * SUBGROUPS, clear, 0, unroll=8)

    def send(r, carry):
        d = placed[group * reqs + r]
        rank = count[d]
        count[d] = rank + 1
        if spare:

            @pl.when(rank == 0)
            def _():
                pltpu.make_async_copy(
                    states.at[r], cells.at[d, pl.ds(0, heads)], sems.at[r]
                ).start()

            @pl.when(rank > 0)
            def _():
                for a in range(heads):
                    pltpu.make_async_copy(
                        states.at[r, a], cells.at[d // CORES * CORES + a, heads], sems.at[r]
                    ).start()

        else:
            pltpu.make_async_copy(states.at[r], cells.at[d, rank], sems.at[r]).start()
        return carry

    lax.fori_loop(0, reqs, send, 0, unroll=4)

    for s in range(n_group):

        def tally(r, total, s=s):
            return total + jnp.where(placed[s * reqs + r] == mine, 1, 0)

        live[s] = lax.fori_loop(0, reqs, tally, 0, unroll=8)

    def drain(r, carry):
        landed = cells.at[0, pl.ds(0, heads)] if spare else cells.at[0, 0]
        pltpu.make_async_copy(states.at[r], landed, sems.at[r]).wait()
        return carry

    lax.fori_loop(0, reqs, drain, 0, unroll=4)


def pack(placed, states, n_group, spare):
    reqs, heads, key_size, value_size = states.shape
    cell = (heads + 1,) if spare else (SLOT_CAP, heads)
    cells = (n_group * SUBGROUPS,) + cell + (key_size, value_size)
    return pl.pallas_call(
        lambda *refs: pack_kernel(n_group, reqs, spare, *refs),
        out_shape=(
            pltpu.VMEM(cells, states.dtype),
            jax.ShapeDtypeStruct((n_group,), jnp.int32),
        ),
        in_specs=[
            pl.BlockSpec(memory_space=pltpu.SMEM),
            pl.BlockSpec(memory_space=pltpu.HBM),
        ],
        out_specs=(
            pl.BlockSpec(memory_space=pltpu.VMEM),
            pl.BlockSpec(memory_space=pltpu.SMEM),
        ),
        scratch_shapes=[
            pltpu.SMEM((n_group * SUBGROUPS,), jnp.int32),
            pltpu.SemaphoreType.DMA((reqs,)),
        ],
        compiler_params=pltpu.CompilerParams(vmem_limit_bytes=32 * 1024 * 1024),
    )(placed, pltpu.with_memory_space_constraint(states, pltpu.HBM))


def split(x):
    high = x.astype(jnp.bfloat16)
    return high, (x - high.astype(jnp.float32)).astype(jnp.bfloat16)


def row_sums(parts):
    rows, lanes = parts[0].shape
    high, low = split(jnp.concatenate(parts, axis=0))
    sums = jnp.dot(
        jnp.concatenate([high, low], axis=1),
        jnp.ones((2 * lanes, lanes), jnp.bfloat16),
        preferred_element_type=jnp.float32,
    )
    return [sums[n * rows : (n + 1) * rows] for n in range(len(parts))]


def widen(columns, width):
    rows, count = columns.shape
    high, rest = split(columns)
    low = columns - high.astype(jnp.float32) - rest.astype(jnp.float32)
    parts = [high.astype(jnp.float32), rest.astype(jnp.float32), low]
    lane = lax.broadcasted_iota(jnp.int32, (count, count * width), 1)
    column = lax.broadcasted_iota(jnp.int32, (count, count * width), 0)
    wide = jnp.dot(
        jnp.concatenate(parts, axis=0).astype(jnp.bfloat16),
        jnp.where(lane // width == column, 1.0, 0.0).astype(jnp.bfloat16),
        preferred_element_type=jnp.float32,
    )
    return wide[:rows] + wide[rows : 2 * rows] + wide[2 * rows :]


def decode_kernel(
    load, chosen, slot, first, live, query, key, value, gate, strength, decay, gain, tokens, states,
    by_key, by_query, values, fades, writes, key_rows, query_rows, kept,
):
    size, width = states.shape[2:]
    heads = states.shape[1] // SUBGROUPS
    steps = key.shape[4]
    units = [(n, i) for n in range(SOURCES) for i in range(SUBGROUPS)]
    count = len(units)

    def keys(i):
        return slice(i * size, (i + 1) * size)

    def lanes(i):
        return slice(i * heads * width, (i + 1) * heads * width)

    def state_of(n, i):
        return jnp.concatenate(
            [states[first + n, heads * i + a] for a in range(heads)]
            if chosen
            else load(first + n, i),
            axis=1,
        )

    def rows(t):
        return slice(t * count, (t + 1) * count)

    def spread(ref, u, x):
        for a in range(heads):
            ref[a, pl.ds(u, steps, stride=count), :] = x[:, a * width : (a + 1) * width]

    def gather(ref, u):
        return jnp.concatenate(
            [ref[a, pl.ds(u, steps, stride=count), :] for a in range(heads)], axis=1
        )

    wide = widen(
        jnp.concatenate(
            [x[0, 0, first + n, slot] for x in (decay, strength) for n in range(SOURCES)], axis=0
        ),
        width,
    )
    for u, (n, i) in enumerate(units):
        key_f = key[0, 0, first + n, slot, :, keys(i)].astype(jnp.float32)
        query_f = query[0, 0, first + n, slot, :, keys(i)].astype(jnp.float32)
        both = jnp.concatenate([key_f, query_f], axis=0).astype(jnp.bfloat16)
        before = load(first + n, i)
        if chosen:
            for a in range(heads):
                states[first + n, heads * i + a] = before[a]
        high, low = split(jnp.concatenate(before, axis=1))
        product = jnp.dot(
            jnp.concatenate([both, both], axis=1),
            jnp.concatenate([high, low], axis=0),
            preferred_element_type=jnp.float32,
        )
        spread(by_key, u, product[:steps])
        spread(by_query, u, product[steps:])
        key_rows[pl.ds(u, steps, stride=count), :] = key_f
        query_rows[pl.ds(u, steps, stride=count), :] = query_f
        spread(values, u, value[0, 0, first + n, slot, :, lanes(i)].astype(jnp.float32))
        spread(fades, u, wide[n * steps : (n + 1) * steps, lanes(i)])
        spread(writes, u, wide[(SOURCES + n) * steps : (SOURCES + n + 1) * steps, lanes(i)])

    on_key = [[by_key[a, rows(t)] for a in range(heads)] for t in range(steps)]
    on_query = [[by_query[a, rows(t)] for a in range(heads)] for t in range(steps)]
    keyed = [key_rows[rows(t)] for t in range(steps)]
    asked = [query_rows[rows(t)] for t in range(steps)]
    pairs = [(l, t) for t in range(steps) for l in range(t, steps)]
    key_key = dict(zip(pairs, row_sums([keyed[l] * keyed[t] for l, t in pairs])))
    query_key = dict(zip(pairs, row_sums([asked[l] * keyed[t] for l, t in pairs])))
    query_norms = [lax.rsqrt(x + EPS) / math.sqrt(size) for x in row_sums([q * q for q in asked])]
    written, total = [], None
    for t in range(steps):
        fade = [fades[a, rows(t)] for a in range(heads)]
        total = fade if total is None else [x * f for x, f in zip(total, fade)]
        norm = lax.rsqrt(key_key[t, t] + EPS)
        write = []
        for a in range(heads):
            residual = values[a, rows(t)] - norm * (on_key[t][a] * fade[a])
            write.append(writes[a, rows(t)] * norm * residual)
        written = [[w * f for w, f in zip(old, fade)] for old in written] + [write]
        for later in range(t, steps):
            for on, dots in ((on_key, key_key), (on_query, query_key)):
                if on is on_query or later > t:
                    dot = dots[later, t]
                    on[later] = [x * f + dot * w for x, f, w in zip(on[later], fade, write)]
    kept[...] = jnp.concatenate(total, axis=1)
    readouts = [x * query_norms[t] for t in range(steps) for x in on_query[t]]
    squares = row_sums([x * x for x in readouts])
    for t in range(steps):
        for a in range(heads):
            by_key[a, rows(t)] = written[t][a]
            norm = lax.rsqrt(squares[t * heads + a] / width + EPS)
            by_query[a, rows(t)] = readouts[t * heads + a] * norm * gain[...]

    for u, (n, i) in enumerate(units):
        key_f = key[0, 0, first + n, slot, :, keys(i)].astype(jnp.float32)
        high, low = split(gather(by_key, u))
        update = lax.dot_general(
            jnp.concatenate([key_f, key_f], axis=0).astype(jnp.bfloat16),
            jnp.concatenate([high.astype(jnp.float32), low.astype(jnp.float32)], axis=0).astype(
                jnp.bfloat16
            ),
            (((0,), (0,)), ((), ())),
            preferred_element_type=jnp.float32,
        )
        state = kept[u : u + 1, :] * state_of(n, i) + update
        for a in range(heads):
            states[first + n, heads * i + a] = state[:, a * width : (a + 1) * width]
        opened = gate[0, 0, first + n, slot, :, lanes(i)].astype(jnp.float32)
        token = gather(by_query, u) * (opened * jax.nn.sigmoid(opened))
        tokens[first + n, :, lanes(i)] = token.astype(tokens.dtype)

    for n in range(SOURCES):

        @pl.when(live[first + n] <= slot)
        def _(n=n):
            tokens[first + n] = jnp.zeros(tokens.shape[1:], tokens.dtype)
            states[first + n] = jnp.zeros(states.shape[1:], states.dtype)


def decode(live, sources, load, slot, small, gain, earlier=None):
    queries, values = small[0], small[2]
    n_group, cap, steps = queries.shape[2:5]
    key_size, value_size = queries.shape[5] // SUBGROUPS, gain.shape[1]
    heads = values.shape[5] // (SUBGROUPS * value_size)
    block = (SUBGROUPS * heads, key_size, value_size)
    units = SOURCES * SUBGROUPS
    rows = steps * units
    by_step = (heads, rows, value_size)
    scratch = [by_step] * 5 + [(rows, key_size)] * 2 + [(units, heads * value_size)]
    kept = () if earlier is None else earlier

    def kernel(live, *refs):
        blocks, refs = refs[: len(sources)], refs[len(sources) :]
        ins, refs = refs[: len(small) + 1], refs[len(small) + 1 :]
        before, refs = refs[: len(kept)], refs[len(kept) :]
        tokens, finals, states, sems, *work = refs
        if kept:
            result, tokens = tokens, work.pop()

        def place(batch):
            span = pl.ds(batch * SOURCES, SOURCES)
            return pltpu.make_async_copy(
                states.at[span], finals.at[0, 0, span, slot], sems.at[batch]
            )

        def run(batch, carry):
            mine = tokens.at[0, 0, :, slot] if kept else tokens
            decode_kernel(
                lambda s, i: load(s, i, *blocks), len(sources) > 1, slot, batch * SOURCES, live,
                *ins, mine, states, *work,
            )
            place(batch).start()
            return carry

        lax.fori_loop(0, n_group // SOURCES, run, 0)
        if kept:
            for s in range(n_group):
                tokens[0, 0, s, 0] = before[0][s]
            copy = pltpu.make_async_copy(tokens, result, sems.at[n_group // SOURCES])
            copy.start()
            copy.wait()
        for batch in range(n_group // SOURCES):
            place(batch).wait()

    vmem, any_space = pl.BlockSpec(memory_space=pltpu.VMEM), pl.BlockSpec(memory_space=pl.ANY)
    in_vmem = [pltpu.with_memory_space_constraint(x, pltpu.VMEM) for x in sources]
    tokens_shape = values.shape if kept else (n_group,) + values.shape[4:]
    return pl.pallas_call(
        kernel,
        out_shape=(
            jax.ShapeDtypeStruct(tokens_shape, jnp.bfloat16),
            jax.ShapeDtypeStruct((1, 1, n_group, cap) + block, jnp.float32),
        ),
        in_specs=[pl.BlockSpec(memory_space=pltpu.SMEM)]
        + [vmem] * (len(sources) + len(small) + 1)
        + [vmem, any_space][: len(kept)],
        out_specs=(any_space if kept else vmem, any_space),
        scratch_shapes=[
            pltpu.VMEM((n_group,) + block, jnp.float32),
            pltpu.SemaphoreType.DMA((n_group // SOURCES + 1,)),
        ]
        + [pltpu.VMEM(shape, jnp.float32) for shape in scratch]
        + [pltpu.VMEM(tokens_shape, jnp.bfloat16)] * bool(kept),
        input_output_aliases={len(sources) + len(small) + 3: 1} if kept else {},
        compiler_params=pltpu.CompilerParams(vmem_limit_bytes=32 * 1024 * 1024),
    )(live, *in_vmem, *small, gain, *kept)


def exchange(cells):
    return lax.all_to_all(cells, ("group", "sub"), split_axis=0, concat_axis=0, tiled=True)


def with_spare(placed, states, small, gain, n_group):
    cells, live = pack(placed, states, n_group, True)
    heads, key_size, value_size = states.shape[1:]
    square = (key_size, value_size)
    arrived = exchange(cells)
    spare = arrived[:, heads]
    swap = [(n, n ^ 1) for n in range(SUBGROUPS)]
    other = lax.ppermute(spare, "sub", swap)
    by_source = arrived.reshape((n_group, SUBGROUPS, heads + 1) + square)
    other = other.reshape((n_group, SUBGROUPS) + square)
    earlier = decode(
        live, [by_source], lambda s, i, x: [x[s, i, a] for a in range(heads)], 0, small, gain
    )

    def load(s, i, x, y):
        core = lax.axis_index("sub") % CORES
        return [jnp.where(core == a, x[s, i, heads], y[s, i]) for a in range(heads)]

    return decode(live, [by_source, other], load, 1, small, gain, earlier)


def without_spare(placed, states, small, gain, n_group):
    cells, live = pack(placed, states, n_group, False)
    heads, key_size, value_size = states.shape[1:]
    square = (key_size, value_size)
    arrived = exchange(cells).reshape((n_group, SUBGROUPS, SLOT_CAP, heads) + square)
    earlier = None
    for slot in range(SLOT_CAP):
        earlier = decode(
            live,
            [arrived],
            lambda s, i, x, slot=slot: [x[s, i, slot, a] for a in range(heads)],
            slot,
            small,
            gain,
            earlier,
        )
    return earlier


def local(states, placement, queries, key_vectors, value_vectors, gate_inputs, strength, decay, gain):
    n_group = lax.axis_size("group")
    placed = placement.reshape(placement.shape[0])
    fits = cells_fit(placed, n_group * SUBGROUPS, states.shape[0])
    small = (queries, key_vectors, value_vectors, gate_inputs, strength, decay)
    gain = gain.reshape(1, gain.shape[0])
    return lax.cond(
        fits[0] > 0,
        lambda *x: with_spare(*x, n_group),
        lambda *x: without_spare(*x, n_group),
        placed,
        states,
        small,
        gain,
    )


def solution(mesh):
    n_group, n_head = mesh.devices.shape
    quads = Mesh(
        mesh.devices.reshape(n_group, n_head // SUBGROUPS, SUBGROUPS), ("group", "block", "sub")
    )
    spread = P("group", ("block", "sub"))
    return jax.shard_map(
        local,
        mesh=quads,
        in_specs=(spread, P(), spread, spread, spread, spread, spread, spread, P()),
        out_specs=(spread, spread),
        check_vma=False,
    )
```

```python
import math

import jax
import jax.numpy as jnp
from jax import lax
from jax.experimental import pallas as pl
from jax.experimental.pallas import tpu as pltpu
from jax.sharding import Mesh
from jax.sharding import PartitionSpec as P

SUBGROUPS = 4
SLOT_CAP = 2
CORES = 2
SOURCES = 2
EPS = 1e-06


def fits_kernel(dec_groups, reqs, placed, fits):
    lanes = placed.shape[1]
    chips = placed[...] // CORES
    named = [jnp.where(chips == chip, 1.0, 0.0) for chip in range(dec_groups // CORES)]
    lane = lax.broadcasted_iota(jnp.int32, (lanes, lanes), 0)
    group = lax.broadcasted_iota(jnp.int32, (lanes, lanes), 1)
    counts = jnp.dot(
        jnp.concatenate(named, axis=0).astype(jnp.bfloat16),
        jnp.where(lane // reqs == group, 1.0, 0.0).astype(jnp.bfloat16),
        preferred_element_type=jnp.float32,
    )
    fits[0] = jnp.where(jnp.max(counts) < SLOT_CAP + 1.5, 1, 0)


def cells_fit(placed, dec_groups, reqs):
    return pl.pallas_call(
        lambda *refs: fits_kernel(dec_groups, reqs, *refs),
        out_shape=jax.ShapeDtypeStruct((1,), jnp.int32),
        in_specs=[pl.BlockSpec(memory_space=pltpu.VMEM)],
        out_specs=pl.BlockSpec(memory_space=pltpu.SMEM),
    )(placed.reshape(-1, 128))


def pack_kernel(n_group, reqs, spare, placed, states, cells, live, count, sems):
    group = lax.axis_index("group")
    mine = group * SUBGROUPS + lax.axis_index("sub")
    heads = states.shape[1]

    def clear(d, carry):
        count[d] = 0
        return carry

    lax.fori_loop(0, n_group * SUBGROUPS, clear, 0, unroll=8)

    def send(r, carry):
        d = placed[group * reqs + r]
        rank = count[d]
        count[d] = rank + 1
        if spare:

            @pl.when(rank == 0)
            def _():
                pltpu.make_async_copy(
                    states.at[r], cells.at[d, pl.ds(0, heads)], sems.at[r]
                ).start()

            @pl.when(rank > 0)
            def _():
                for a in range(heads):
                    pltpu.make_async_copy(
                        states.at[r, a], cells.at[d // CORES * CORES + a, heads], sems.at[r]
                    ).start()

        else:
            pltpu.make_async_copy(states.at[r], cells.at[d, rank], sems.at[r]).start()
        return carry

    lax.fori_loop(0, reqs, send, 0, unroll=4)

    for s in range(n_group):

        def tally(r, total, s=s):
            return total + jnp.where(placed[s * reqs + r] == mine, 1, 0)

        live[s] = lax.fori_loop(0, reqs, tally, 0, unroll=8)

    def drain(r, carry):
        landed = cells.at[0, pl.ds(0, heads)] if spare else cells.at[0, 0]
        pltpu.make_async_copy(states.at[r], landed, sems.at[r]).wait()
        return carry

    lax.fori_loop(0, reqs, drain, 0, unroll=4)


def pack(placed, states, n_group, spare):
    reqs, heads, key_size, value_size = states.shape
    cell = (heads + 1,) if spare else (SLOT_CAP, heads)
    cells = (n_group * SUBGROUPS,) + cell + (key_size, value_size)
    return pl.pallas_call(
        lambda *refs: pack_kernel(n_group, reqs, spare, *refs),
        out_shape=(
            pltpu.VMEM(cells, states.dtype),
            jax.ShapeDtypeStruct((n_group,), jnp.int32),
        ),
        in_specs=[
            pl.BlockSpec(memory_space=pltpu.SMEM),
            pl.BlockSpec(memory_space=pltpu.HBM),
        ],
        out_specs=(
            pl.BlockSpec(memory_space=pltpu.VMEM),
            pl.BlockSpec(memory_space=pltpu.SMEM),
        ),
        scratch_shapes=[
            pltpu.SMEM((n_group * SUBGROUPS,), jnp.int32),
            pltpu.SemaphoreType.DMA((reqs,)),
        ],
        compiler_params=pltpu.CompilerParams(vmem_limit_bytes=32 * 1024 * 1024),
    )(placed, pltpu.with_memory_space_constraint(states, pltpu.HBM))


def split(x):
    high = x.astype(jnp.bfloat16)
    return high, (x - high.astype(jnp.float32)).astype(jnp.bfloat16)


def row_sums(parts):
    rows, lanes = parts[0].shape
    high, low = split(jnp.concatenate(parts, axis=0))
    sums = jnp.dot(
        jnp.concatenate([high, low], axis=1),
        jnp.ones((2 * lanes, lanes), jnp.bfloat16),
        preferred_element_type=jnp.float32,
    )
    return [sums[n * rows : (n + 1) * rows] for n in range(len(parts))]


def widen(columns, width):
    rows, count = columns.shape
    high, rest = split(columns)
    low = columns - high.astype(jnp.float32) - rest.astype(jnp.float32)
    parts = [high.astype(jnp.float32), rest.astype(jnp.float32), low]
    lane = lax.broadcasted_iota(jnp.int32, (count, count * width), 1)
    column = lax.broadcasted_iota(jnp.int32, (count, count * width), 0)
    wide = jnp.dot(
        jnp.concatenate(parts, axis=0).astype(jnp.bfloat16),
        jnp.where(lane // width == column, 1.0, 0.0).astype(jnp.bfloat16),
        preferred_element_type=jnp.float32,
    )
    return wide[:rows] + wide[rows : 2 * rows] + wide[2 * rows :]


def decode_kernel(
    load, chosen, slot, first, live, query, key, value, gate, strength, decay, gain, tokens, states,
    by_key, by_query, values, fades, writes, key_rows, query_rows, kept,
):
    size, width = states.shape[2:]
    heads = states.shape[1] // SUBGROUPS
    steps = key.shape[4]
    units = [(n, i) for n in range(SOURCES) for i in range(SUBGROUPS)]
    count = len(units)

    def keys(i):
        return slice(i * size, (i + 1) * size)

    def lanes(i):
        return slice(i * heads * width, (i + 1) * heads * width)

    def state_of(n, i):
        return jnp.concatenate(
            [states[first + n, heads * i + a] for a in range(heads)]
            if chosen
            else load(first + n, i),
            axis=1,
        )

    def rows(t):
        return slice(t * count, (t + 1) * count)

    def spread(ref, u, x):
        for a in range(heads):
            ref[a, pl.ds(u, steps, stride=count), :] = x[:, a * width : (a + 1) * width]

    def gather(ref, u):
        return jnp.concatenate(
            [ref[a, pl.ds(u, steps, stride=count), :] for a in range(heads)], axis=1
        )

    wide = widen(
        jnp.concatenate(
            [x[0, 0, first + n, slot] for x in (decay, strength) for n in range(SOURCES)], axis=0
        ),
        width,
    )
    for u, (n, i) in enumerate(units):
        key_f = key[0, 0, first + n, slot, :, keys(i)].astype(jnp.float32)
        query_f = query[0, 0, first + n, slot, :, keys(i)].astype(jnp.float32)
        both = jnp.concatenate([key_f, query_f], axis=0).astype(jnp.bfloat16)
        before = load(first + n, i)
        if chosen:
            for a in range(heads):
                states[first + n, heads * i + a] = before[a]
        high, low = split(jnp.concatenate(before, axis=1))
        product = jnp.dot(
            jnp.concatenate([both, both], axis=1),
            jnp.concatenate([high, low], axis=0),
            preferred_element_type=jnp.float32,
        )
        spread(by_key, u, product[:steps])
        spread(by_query, u, product[steps:])
        key_rows[pl.ds(u, steps, stride=count), :] = key_f
        query_rows[pl.ds(u, steps, stride=count), :] = query_f
        spread(values, u, value[0, 0, first + n, slot, :, lanes(i)].astype(jnp.float32))
        spread(fades, u, wide[n * steps : (n + 1) * steps, lanes(i)])
        spread(writes, u, wide[(SOURCES + n) * steps : (SOURCES + n + 1) * steps, lanes(i)])

    on_key = [[by_key[a, rows(t)] for a in range(heads)] for t in range(steps)]
    on_query = [[by_query[a, rows(t)] for a in range(heads)] for t in range(steps)]
    keyed = [key_rows[rows(t)] for t in range(steps)]
    asked = [query_rows[rows(t)] for t in range(steps)]
    pairs = [(l, t) for t in range(steps) for l in range(t, steps)]
    key_key = dict(zip(pairs, row_sums([keyed[l] * keyed[t] for l, t in pairs])))
    query_key = dict(zip(pairs, row_sums([asked[l] * keyed[t] for l, t in pairs])))
    query_norms = [lax.rsqrt(x + EPS) / math.sqrt(size) for x in row_sums([q * q for q in asked])]
    written, total = [], None
    for t in range(steps):
        fade = [fades[a, rows(t)] for a in range(heads)]
        total = fade if total is None else [x * f for x, f in zip(total, fade)]
        norm = lax.rsqrt(key_key[t, t] + EPS)
        write = []
        for a in range(heads):
            residual = values[a, rows(t)] - norm * (on_key[t][a] * fade[a])
            write.append(writes[a, rows(t)] * norm * residual)
        written = [[w * f for w, f in zip(old, fade)] for old in written] + [write]
        for later in range(t, steps):
            for on, dots in ((on_key, key_key), (on_query, query_key)):
                if on is on_query or later > t:
                    dot = dots[later, t]
                    on[later] = [x * f + dot * w for x, f, w in zip(on[later], fade, write)]
    kept[...] = jnp.concatenate(total, axis=1)
    readouts = [x * query_norms[t] for t in range(steps) for x in on_query[t]]
    squares = row_sums([x * x for x in readouts])
    for t in range(steps):
        for a in range(heads):
            by_key[a, rows(t)] = written[t][a]
            norm = lax.rsqrt(squares[t * heads + a] / width + EPS)
            by_query[a, rows(t)] = readouts[t * heads + a] * norm * gain[...]

    for u, (n, i) in enumerate(units):
        key_f = key[0, 0, first + n, slot, :, keys(i)].astype(jnp.float32)
        high, low = split(gather(by_key, u))
        update = lax.dot_general(
            jnp.concatenate([key_f, key_f], axis=0).astype(jnp.bfloat16),
            jnp.concatenate([high.astype(jnp.float32), low.astype(jnp.float32)], axis=0).astype(
                jnp.bfloat16
            ),
            (((0,), (0,)), ((), ())),
            preferred_element_type=jnp.float32,
        )
        state = kept[u : u + 1, :] * state_of(n, i) + update
        for a in range(heads):
            states[first + n, heads * i + a] = state[:, a * width : (a + 1) * width]
        opened = gate[0, 0, first + n, slot, :, lanes(i)].astype(jnp.float32)
        token = gather(by_query, u) * (opened * jax.nn.sigmoid(opened))
        tokens[first + n, :, lanes(i)] = token.astype(tokens.dtype)

    for n in range(SOURCES):

        @pl.when(live[first + n] <= slot)
        def _(n=n):
            tokens[first + n] = jnp.zeros(tokens.shape[1:], tokens.dtype)
            states[first + n] = jnp.zeros(states.shape[1:], states.dtype)


def decode(live, sources, load, slot, small, gain, earlier=None):
    queries, values = small[0], small[2]
    n_group, cap, steps = queries.shape[2:5]
    key_size, value_size = queries.shape[5] // SUBGROUPS, gain.shape[1]
    heads = values.shape[5] // (SUBGROUPS * value_size)
    block = (SUBGROUPS * heads, key_size, value_size)
    units = SOURCES * SUBGROUPS
    rows = steps * units
    by_step = (heads, rows, value_size)
    scratch = [by_step] * 5 + [(rows, key_size)] * 2 + [(units, heads * value_size)]
    kept = () if earlier is None else earlier

    def kernel(live, *refs):
        blocks, refs = refs[: len(sources)], refs[len(sources) :]
        ins, refs = refs[: len(small) + 1], refs[len(small) + 1 :]
        before, refs = refs[: len(kept)], refs[len(kept) :]
        tokens, finals, states, sems, *work = refs
        if kept:
            result, tokens = tokens, work.pop()
            tokens[0, 0, :, slot] = jnp.zeros((n_group,) + values.shape[4:], jnp.bfloat16)
        else:
            blank = work.pop()
            blank[...] = jnp.zeros(block, jnp.float32)

        def erase(group):
            return pltpu.make_async_copy(
                blank, finals.at[0, 0, group, cap - 1], sems.at[n_group + group]
            )

        def place(group):
            return pltpu.make_async_copy(
                states.at[group], finals.at[0, 0, group, slot], sems.at[group]
            )

        def run(batch, carry):
            first = batch * SOURCES

            def compute():
                decode_kernel(
                    lambda s, i: load(s, i, *blocks), len(sources) > 1, slot, first, live, *ins,
                    tokens.at[0, 0, :, slot] if kept else tokens, states, *work,
                )

            if kept:
                some = live[first] > slot
                for n in range(1, SOURCES):
                    some = some | (live[first + n] > slot)
                pl.when(some)(compute)
                for n in range(SOURCES):
                    pl.when(live[first + n] > slot)(lambda n=n: place(first + n).start())
            else:
                compute()
                for n in range(SOURCES):
                    place(first + n).start()
            return carry

        if not kept:
            for group in range(n_group):
                pl.when(live[group] < cap)(lambda group=group: erase(group).start())
        lax.fori_loop(0, n_group // SOURCES, run, 0)
        if kept:
            tokens[0, 0, :, 0] = before[0][...]
            copy = pltpu.make_async_copy(tokens, result, sems.at[n_group])
            copy.start()
            copy.wait()
            for group in range(n_group):
                pl.when(live[group] > slot)(lambda group=group: place(group).wait())
        else:
            for group in range(n_group):
                place(group).wait()
                pl.when(live[group] < cap)(lambda group=group: erase(group).wait())

    vmem, any_space = pl.BlockSpec(memory_space=pltpu.VMEM), pl.BlockSpec(memory_space=pl.ANY)
    in_vmem = [pltpu.with_memory_space_constraint(x, pltpu.VMEM) for x in sources]
    tokens_shape = values.shape if kept else (n_group,) + values.shape[4:]
    return pl.pallas_call(
        kernel,
        out_shape=(
            jax.ShapeDtypeStruct(tokens_shape, jnp.bfloat16),
            jax.ShapeDtypeStruct((1, 1, n_group, cap) + block, jnp.float32),
        ),
        in_specs=[pl.BlockSpec(memory_space=pltpu.SMEM)]
        + [vmem] * (len(sources) + len(small) + 1)
        + [vmem, any_space][: len(kept)],
        out_specs=(any_space if kept else vmem, any_space),
        scratch_shapes=[
            pltpu.VMEM((n_group,) + block, jnp.float32),
            pltpu.SemaphoreType.DMA((2 * n_group,)),
        ]
        + [pltpu.VMEM(shape, jnp.float32) for shape in scratch]
        + [pltpu.VMEM(tokens_shape, jnp.bfloat16) if kept else pltpu.VMEM(block, jnp.float32)],
        input_output_aliases={len(sources) + len(small) + 3: 1} if kept else {},
        compiler_params=pltpu.CompilerParams(vmem_limit_bytes=32 * 1024 * 1024),
    )(live, *in_vmem, *small, gain, *kept)


def exchange(cells):
    return lax.all_to_all(cells, ("group", "sub"), split_axis=0, concat_axis=0, tiled=True)


def with_spare(placed, states, small, gain, n_group):
    cells, live = pack(placed, states, n_group, True)
    heads, key_size, value_size = states.shape[1:]
    square = (key_size, value_size)
    arrived = exchange(cells)
    spare = arrived[:, heads]
    swap = [(n, n ^ 1) for n in range(SUBGROUPS)]
    other = lax.ppermute(spare, "sub", swap)
    by_source = arrived.reshape((n_group, SUBGROUPS, heads + 1) + square)
    other = other.reshape((n_group, SUBGROUPS) + square)
    earlier = decode(
        live, [by_source], lambda s, i, x: [x[s, i, a] for a in range(heads)], 0, small, gain
    )

    def load(s, i, x, y):
        core = lax.axis_index("sub") % CORES
        return [jnp.where(core == a, x[s, i, heads], y[s, i]) for a in range(heads)]

    return decode(live, [by_source, other], load, 1, small, gain, earlier)


def without_spare(placed, states, small, gain, n_group):
    cells, live = pack(placed, states, n_group, False)
    heads, key_size, value_size = states.shape[1:]
    square = (key_size, value_size)
    arrived = exchange(cells).reshape((n_group, SUBGROUPS, SLOT_CAP, heads) + square)
    earlier = None
    for slot in range(SLOT_CAP):
        earlier = decode(
            live,
            [arrived],
            lambda s, i, x, slot=slot: [x[s, i, slot, a] for a in range(heads)],
            slot,
            small,
            gain,
            earlier,
        )
    return earlier


def local(states, placement, queries, key_vectors, value_vectors, gate_inputs, strength, decay, gain):
    n_group = lax.axis_size("group")
    placed = placement.reshape(placement.shape[0])
    fits = cells_fit(placed, n_group * SUBGROUPS, states.shape[0])
    small = (queries, key_vectors, value_vectors, gate_inputs, strength, decay)
    gain = gain.reshape(1, gain.shape[0])
    return lax.switch(
        fits[0],
        [lambda *x: without_spare(*x, n_group), lambda *x: with_spare(*x, n_group)],
        placed,
        states,
        small,
        gain,
    )


def solution(mesh):
    n_group, n_head = mesh.devices.shape
    quads = Mesh(
        mesh.devices.reshape(n_group, n_head // SUBGROUPS, SUBGROUPS), ("group", "block", "sub")
    )
    spread = P("group", ("block", "sub"))
    return jax.shard_map(
        local,
        mesh=quads,
        in_specs=(spread, P(), spread, spread, spread, spread, spread, spread, P()),
        out_specs=(spread, spread),
        check_vma=False,
    )
```

```python
import math

import jax
import jax.numpy as jnp
from jax import lax
from jax.experimental import pallas as pl
from jax.experimental.pallas import tpu as pltpu
from jax.sharding import Mesh
from jax.sharding import PartitionSpec as P

SUBGROUPS = 4
SLOT_CAP = 2
CORES = 2
SOURCES = 2
EPS = 1e-06


def fits_kernel(dec_groups, reqs, placed, fits):
    lanes = placed.shape[1]
    chips = placed[...] // CORES
    named = [jnp.where(chips == chip, 1.0, 0.0) for chip in range(dec_groups // CORES)]
    lane = lax.broadcasted_iota(jnp.int32, (lanes, lanes), 0)
    group = lax.broadcasted_iota(jnp.int32, (lanes, lanes), 1)
    counts = jnp.dot(
        jnp.concatenate(named, axis=0).astype(jnp.bfloat16),
        jnp.where(lane // reqs == group, 1.0, 0.0).astype(jnp.bfloat16),
        preferred_element_type=jnp.float32,
    )
    fits[0] = jnp.where(jnp.max(counts) < SLOT_CAP + 1.5, 1, 0)


def cells_fit(placed, dec_groups, reqs):
    return pl.pallas_call(
        lambda *refs: fits_kernel(dec_groups, reqs, *refs),
        out_shape=jax.ShapeDtypeStruct((1,), jnp.int32),
        in_specs=[pl.BlockSpec(memory_space=pltpu.VMEM)],
        out_specs=pl.BlockSpec(memory_space=pltpu.SMEM),
    )(placed.reshape(-1, 128))


def pack_kernel(n_group, reqs, spare, placed, states, cells, live, count, sems):
    group = lax.axis_index("group")
    mine = group * SUBGROUPS + lax.axis_index("sub")
    heads = states.shape[1]

    def clear(d, carry):
        count[d] = 0
        return carry

    lax.fori_loop(0, n_group * SUBGROUPS, clear, 0, unroll=8)

    def send(r, carry):
        d = placed[group * reqs + r]
        rank = count[d]
        count[d] = rank + 1
        if spare:

            @pl.when(rank == 0)
            def _():
                pltpu.make_async_copy(
                    states.at[r], cells.at[d, pl.ds(0, heads)], sems.at[r]
                ).start()

            @pl.when(rank > 0)
            def _():
                for a in range(heads):
                    pltpu.make_async_copy(
                        states.at[r, a], cells.at[d // CORES * CORES + a, heads], sems.at[r]
                    ).start()

        else:
            pltpu.make_async_copy(states.at[r], cells.at[d, rank], sems.at[r]).start()
        return carry

    lax.fori_loop(0, reqs, send, 0, unroll=4)

    for s in range(n_group):

        def tally(r, total, s=s):
            return total + jnp.where(placed[s * reqs + r] == mine, 1, 0)

        live[s] = lax.fori_loop(0, reqs, tally, 0, unroll=8)

    def drain(r, carry):
        landed = cells.at[0, pl.ds(0, heads)] if spare else cells.at[0, 0]
        pltpu.make_async_copy(states.at[r], landed, sems.at[r]).wait()
        return carry

    lax.fori_loop(0, reqs, drain, 0, unroll=4)


def pack(placed, states, n_group, spare):
    reqs, heads, key_size, value_size = states.shape
    cell = (heads + 1,) if spare else (SLOT_CAP, heads)
    cells = (n_group * SUBGROUPS,) + cell + (key_size, value_size)
    return pl.pallas_call(
        lambda *refs: pack_kernel(n_group, reqs, spare, *refs),
        out_shape=(
            pltpu.VMEM(cells, states.dtype),
            jax.ShapeDtypeStruct((n_group,), jnp.int32),
        ),
        in_specs=[
            pl.BlockSpec(memory_space=pltpu.SMEM),
            pl.BlockSpec(memory_space=pltpu.HBM),
        ],
        out_specs=(
            pl.BlockSpec(memory_space=pltpu.VMEM),
            pl.BlockSpec(memory_space=pltpu.SMEM),
        ),
        scratch_shapes=[
            pltpu.SMEM((n_group * SUBGROUPS,), jnp.int32),
            pltpu.SemaphoreType.DMA((reqs,)),
        ],
        compiler_params=pltpu.CompilerParams(vmem_limit_bytes=32 * 1024 * 1024),
    )(placed, pltpu.with_memory_space_constraint(states, pltpu.HBM))


def split(x):
    high = x.astype(jnp.bfloat16)
    return high, (x - high.astype(jnp.float32)).astype(jnp.bfloat16)


def row_sums(parts):
    rows, lanes = parts[0].shape
    high, low = split(jnp.concatenate(parts, axis=0))
    sums = jnp.dot(
        jnp.concatenate([high, low], axis=1),
        jnp.ones((2 * lanes, lanes), jnp.bfloat16),
        preferred_element_type=jnp.float32,
    )
    return [sums[n * rows : (n + 1) * rows] for n in range(len(parts))]


def widen(columns, width):
    rows, count = columns.shape
    high, rest = split(columns)
    low = columns - high.astype(jnp.float32) - rest.astype(jnp.float32)
    parts = [high.astype(jnp.float32), rest.astype(jnp.float32), low]
    lane = lax.broadcasted_iota(jnp.int32, (count, count * width), 1)
    column = lax.broadcasted_iota(jnp.int32, (count, count * width), 0)
    wide = jnp.dot(
        jnp.concatenate(parts, axis=0).astype(jnp.bfloat16),
        jnp.where(lane // width == column, 1.0, 0.0).astype(jnp.bfloat16),
        preferred_element_type=jnp.float32,
    )
    return wide[:rows] + wide[rows : 2 * rows] + wide[2 * rows :]


def decode_kernel(
    load, chosen, slot, first, live, query, key, value, gate, strength, decay, gain, tokens, states,
    by_key, by_query, values, fades, writes, key_rows, query_rows, kept,
):
    size, width = states.shape[2:]
    heads = states.shape[1] // SUBGROUPS
    steps = key.shape[4]
    units = [(n, i) for n in range(SOURCES) for i in range(SUBGROUPS)]
    count = len(units)

    def keys(i):
        return slice(i * size, (i + 1) * size)

    def lanes(i):
        return slice(i * heads * width, (i + 1) * heads * width)

    def state_of(n, i):
        return jnp.concatenate(
            [states[first + n, heads * i + a] for a in range(heads)]
            if chosen
            else load(first + n, i),
            axis=1,
        )

    def rows(t):
        return slice(t * count, (t + 1) * count)

    def spread(ref, u, x):
        for a in range(heads):
            ref[a, pl.ds(u, steps, stride=count), :] = x[:, a * width : (a + 1) * width]

    def gather(ref, u):
        return jnp.concatenate(
            [ref[a, pl.ds(u, steps, stride=count), :] for a in range(heads)], axis=1
        )

    wide = widen(
        jnp.concatenate(
            [x[0, 0, first + n, slot] for x in (decay, strength) for n in range(SOURCES)], axis=0
        ),
        width,
    )
    for u, (n, i) in enumerate(units):
        key_f = key[0, 0, first + n, slot, :, keys(i)].astype(jnp.float32)
        query_f = query[0, 0, first + n, slot, :, keys(i)].astype(jnp.float32)
        both = jnp.concatenate([key_f, query_f], axis=0).astype(jnp.bfloat16)
        before = load(first + n, i)
        if chosen:
            for a in range(heads):
                states[first + n, heads * i + a] = before[a]
        high, low = split(jnp.concatenate(before, axis=1))
        product = jnp.dot(
            jnp.concatenate([both, both], axis=1),
            jnp.concatenate([high, low], axis=0),
            preferred_element_type=jnp.float32,
        )
        spread(by_key, u, product[:steps])
        spread(by_query, u, product[steps:])
        key_rows[pl.ds(u, steps, stride=count), :] = key_f
        query_rows[pl.ds(u, steps, stride=count), :] = query_f
        spread(values, u, value[0, 0, first + n, slot, :, lanes(i)].astype(jnp.float32))
        spread(fades, u, wide[n * steps : (n + 1) * steps, lanes(i)])
        spread(writes, u, wide[(SOURCES + n) * steps : (SOURCES + n + 1) * steps, lanes(i)])

    on_key = [[by_key[a, rows(t)] for a in range(heads)] for t in range(steps)]
    on_query = [[by_query[a, rows(t)] for a in range(heads)] for t in range(steps)]
    keyed = [key_rows[rows(t)] for t in range(steps)]
    asked = [query_rows[rows(t)] for t in range(steps)]
    pairs = [(l, t) for t in range(steps) for l in range(t, steps)]
    key_key = dict(zip(pairs, row_sums([keyed[l] * keyed[t] for l, t in pairs])))
    query_key = dict(zip(pairs, row_sums([asked[l] * keyed[t] for l, t in pairs])))
    query_norms = [lax.rsqrt(x + EPS) / math.sqrt(size) for x in row_sums([q * q for q in asked])]
    written, total = [], None
    for t in range(steps):
        fade = [fades[a, rows(t)] for a in range(heads)]
        total = fade if total is None else [x * f for x, f in zip(total, fade)]
        norm = lax.rsqrt(key_key[t, t] + EPS)
        write = []
        for a in range(heads):
            residual = values[a, rows(t)] - norm * (on_key[t][a] * fade[a])
            write.append(writes[a, rows(t)] * norm * residual)
        written = [[w * f for w, f in zip(old, fade)] for old in written] + [write]
        for later in range(t, steps):
            for on, dots in ((on_key, key_key), (on_query, query_key)):
                if on is on_query or later > t:
                    dot = dots[later, t]
                    on[later] = [x * f + dot * w for x, f, w in zip(on[later], fade, write)]
    kept[...] = jnp.concatenate(total, axis=1)
    readouts = [x * query_norms[t] for t in range(steps) for x in on_query[t]]
    squares = row_sums([x * x for x in readouts])
    for t in range(steps):
        for a in range(heads):
            by_key[a, rows(t)] = written[t][a]
            norm = lax.rsqrt(squares[t * heads + a] / width + EPS)
            by_query[a, rows(t)] = readouts[t * heads + a] * norm * gain[...]

    for u, (n, i) in enumerate(units):
        key_f = key[0, 0, first + n, slot, :, keys(i)].astype(jnp.float32)
        high, low = split(gather(by_key, u))
        update = lax.dot_general(
            jnp.concatenate([key_f, key_f], axis=0).astype(jnp.bfloat16),
            jnp.concatenate([high.astype(jnp.float32), low.astype(jnp.float32)], axis=0).astype(
                jnp.bfloat16
            ),
            (((0,), (0,)), ((), ())),
            preferred_element_type=jnp.float32,
        )
        state = kept[u : u + 1, :] * state_of(n, i) + update
        for a in range(heads):
            states[first + n, heads * i + a] = state[:, a * width : (a + 1) * width]
        opened = gate[0, 0, first + n, slot, :, lanes(i)].astype(jnp.float32)
        token = gather(by_query, u) * (opened * jax.nn.sigmoid(opened))
        tokens[first + n, :, lanes(i)] = token.astype(tokens.dtype)

    for n in range(SOURCES):

        @pl.when(live[first + n] <= slot)
        def _(n=n):
            tokens[first + n] = jnp.zeros(tokens.shape[1:], tokens.dtype)
            states[first + n] = jnp.zeros(states.shape[1:], states.dtype)


def decode(live, sources, load, slot, small, gain, earlier=None):
    queries, values = small[0], small[2]
    n_group, cap, steps = queries.shape[2:5]
    key_size, value_size = queries.shape[5] // SUBGROUPS, gain.shape[1]
    heads = values.shape[5] // (SUBGROUPS * value_size)
    block = (SUBGROUPS * heads, key_size, value_size)
    units = SOURCES * SUBGROUPS
    rows = steps * units
    by_step = (heads, rows, value_size)
    scratch = [by_step] * 5 + [(rows, key_size)] * 2 + [(units, heads * value_size)]
    kept = () if earlier is None else earlier

    def kernel(live, *refs):
        blocks, refs = refs[: len(sources)], refs[len(sources) :]
        ins, refs = refs[: len(small) + 1], refs[len(small) + 1 :]
        before, refs = refs[: len(kept)], refs[len(kept) :]
        result, finals, states, sems, *work = refs
        tokens, blank = work.pop(), work.pop()
        n_sem = 2 * n_group

        def erase(group):
            return pltpu.make_async_copy(
                blank, finals.at[0, 0, group, cap - 1], sems.at[n_group + group]
            )

        def place(group):
            return pltpu.make_async_copy(
                states.at[group], finals.at[0, 0, group, slot], sems.at[group]
            )

        def run(batch, carry):
            first = batch * SOURCES

            def compute():
                decode_kernel(
                    lambda s, i: load(s, i, *blocks), len(sources) > 1, slot, first, live, *ins,
                    tokens.at[0, 0, :, slot], states, *work,
                )

            if kept:
                some = live[first] > slot
                for n in range(1, SOURCES):
                    some = some | (live[first + n] > slot)
                pl.when(some)(compute)
                for n in range(SOURCES):
                    pl.when(live[first + n] > slot)(lambda n=n: place(first + n).start())
            else:
                compute()
                for n in range(SOURCES):
                    place(first + n).start()
            return carry

        def add_slot():
            copy = pltpu.make_async_copy(result, tokens, sems.at[n_sem])
            copy.start()
            copy.wait()
            lax.fori_loop(0, n_group // SOURCES, run, 0)
            copy = pltpu.make_async_copy(tokens, result, sems.at[n_sem])
            copy.start()
            for group in range(n_group):
                pl.when(live[group] > slot)(lambda group=group: place(group).wait())
            copy.wait()

        if kept:
            some = live[0] > slot
            for group in range(1, n_group):
                some = some | (live[group] > slot)
            pl.when(some)(add_slot)
        else:
            blank[...] = jnp.zeros(block, jnp.float32)
            for group in range(n_group):
                pl.when(live[group] < cap)(lambda group=group: erase(group).start())
            tokens[0, 0, :, cap - 1] = jnp.zeros((n_group,) + values.shape[4:], jnp.bfloat16)
            lax.fori_loop(0, n_group // SOURCES, run, 0)
            copy = pltpu.make_async_copy(tokens, result, sems.at[n_sem])
            copy.start()
            for group in range(n_group):
                place(group).wait()
                pl.when(live[group] < cap)(lambda group=group: erase(group).wait())
            copy.wait()

    vmem, any_space = pl.BlockSpec(memory_space=pltpu.VMEM), pl.BlockSpec(memory_space=pl.ANY)
    in_vmem = [pltpu.with_memory_space_constraint(x, pltpu.VMEM) for x in sources]
    return pl.pallas_call(
        kernel,
        out_shape=(
            jax.ShapeDtypeStruct(values.shape, jnp.bfloat16),
            jax.ShapeDtypeStruct((1, 1, n_group, cap) + block, jnp.float32),
        ),
        in_specs=[pl.BlockSpec(memory_space=pltpu.SMEM)]
        + [vmem] * (len(sources) + len(small) + 1)
        + [any_space] * len(kept),
        out_specs=(any_space, any_space),
        scratch_shapes=[
            pltpu.VMEM((n_group,) + block, jnp.float32),
            pltpu.SemaphoreType.DMA((2 * n_group + 1,)),
        ]
        + [pltpu.VMEM(shape, jnp.float32) for shape in scratch]
        + [pltpu.VMEM(block, jnp.float32), pltpu.VMEM(values.shape, jnp.bfloat16)],
        input_output_aliases={len(sources) + len(small) + 2 + n: n for n in range(len(kept))},
        compiler_params=pltpu.CompilerParams(vmem_limit_bytes=32 * 1024 * 1024),
    )(live, *in_vmem, *small, gain, *kept)


def exchange(cells):
    return lax.all_to_all(cells, ("group", "sub"), split_axis=0, concat_axis=0, tiled=True)


def with_spare(placed, states, small, gain, n_group):
    cells, live = pack(placed, states, n_group, True)
    heads, key_size, value_size = states.shape[1:]
    square = (key_size, value_size)
    arrived = exchange(cells)
    spare = arrived[:, heads]
    swap = [(n, n ^ 1) for n in range(SUBGROUPS)]
    other = lax.ppermute(spare, "sub", swap)
    by_source = arrived.reshape((n_group, SUBGROUPS, heads + 1) + square)
    other = other.reshape((n_group, SUBGROUPS) + square)
    earlier = decode(
        live, [by_source], lambda s, i, x: [x[s, i, a] for a in range(heads)], 0, small, gain
    )

    def load(s, i, x, y):
        core = lax.axis_index("sub") % CORES
        return [jnp.where(core == a, x[s, i, heads], y[s, i]) for a in range(heads)]

    return decode(live, [by_source, other], load, 1, small, gain, earlier)


def without_spare(placed, states, small, gain, n_group):
    cells, live = pack(placed, states, n_group, False)
    heads, key_size, value_size = states.shape[1:]
    square = (key_size, value_size)
    arrived = exchange(cells).reshape((n_group, SUBGROUPS, SLOT_CAP, heads) + square)
    earlier = None
    for slot in range(SLOT_CAP):
        earlier = decode(
            live,
            [arrived],
            lambda s, i, x, slot=slot: [x[s, i, slot, a] for a in range(heads)],
            slot,
            small,
            gain,
            earlier,
        )
    return earlier


def local(states, placement, queries, key_vectors, value_vectors, gate_inputs, strength, decay, gain):
    n_group = lax.axis_size("group")
    placed = placement.reshape(placement.shape[0])
    fits = cells_fit(placed, n_group * SUBGROUPS, states.shape[0])
    small = (queries, key_vectors, value_vectors, gate_inputs, strength, decay)
    gain = gain.reshape(1, gain.shape[0])
    return lax.switch(
        fits[0],
        [lambda *x: without_spare(*x, n_group), lambda *x: with_spare(*x, n_group)],
        placed,
        states,
        small,
        gain,
    )


def solution(mesh):
    n_group, n_head = mesh.devices.shape
    quads = Mesh(
        mesh.devices.reshape(n_group, n_head // SUBGROUPS, SUBGROUPS), ("group", "block", "sub")
    )
    spread = P("group", ("block", "sub"))
    return jax.shard_map(
        local,
        mesh=quads,
        in_specs=(spread, P(), spread, spread, spread, spread, spread, spread, P()),
        out_specs=(spread, spread),
        check_vma=False,
    )
```

```python
import math

import jax
import jax.numpy as jnp
from jax import lax
from jax.experimental import pallas as pl
from jax.experimental.pallas import tpu as pltpu
from jax.sharding import Mesh
from jax.sharding import PartitionSpec as P

SUBGROUPS = 4
SLOT_CAP = 2
CORES = 2
SOURCES = 2
EPS = 1e-06


def fits_kernel(dec_groups, reqs, placed, fits):
    lanes = placed.shape[1]
    chips = placed[...] // CORES
    named = [jnp.where(chips == chip, 1.0, 0.0) for chip in range(dec_groups // CORES)]
    lane = lax.broadcasted_iota(jnp.int32, (lanes, lanes), 0)
    group = lax.broadcasted_iota(jnp.int32, (lanes, lanes), 1)
    counts = jnp.dot(
        jnp.concatenate(named, axis=0).astype(jnp.bfloat16),
        jnp.where(lane // reqs == group, 1.0, 0.0).astype(jnp.bfloat16),
        preferred_element_type=jnp.float32,
    )
    fits[0] = jnp.where(jnp.max(counts) < SLOT_CAP + 1.5, 1, 0)


def cells_fit(placed, dec_groups, reqs):
    return pl.pallas_call(
        lambda *refs: fits_kernel(dec_groups, reqs, *refs),
        out_shape=jax.ShapeDtypeStruct((1,), jnp.int32),
        in_specs=[pl.BlockSpec(memory_space=pltpu.VMEM)],
        out_specs=pl.BlockSpec(memory_space=pltpu.SMEM),
    )(placed.reshape(-1, 128))


def pack_kernel(n_group, reqs, spare, placed, states, cells, live, count, sems):
    group = lax.axis_index("group")
    mine = group * SUBGROUPS + lax.axis_index("sub")
    heads = states.shape[1]

    def clear(d, carry):
        count[d] = 0
        return carry

    lax.fori_loop(0, n_group * SUBGROUPS, clear, 0, unroll=8)

    def send(r, carry):
        d = placed[group * reqs + r]
        rank = count[d]
        count[d] = rank + 1
        if spare:

            @pl.when(rank == 0)
            def _():
                pltpu.make_async_copy(
                    states.at[r], cells.at[d, pl.ds(0, heads)], sems.at[r]
                ).start()

            @pl.when(rank > 0)
            def _():
                for a in range(heads):
                    pltpu.make_async_copy(
                        states.at[r, a], cells.at[d // CORES * CORES + a, heads], sems.at[r]
                    ).start()

        else:
            pltpu.make_async_copy(states.at[r], cells.at[d, rank], sems.at[r]).start()
        return carry

    lax.fori_loop(0, reqs, send, 0, unroll=4)

    for s in range(n_group):

        def tally(r, total, s=s):
            return total + jnp.where(placed[s * reqs + r] == mine, 1, 0)

        live[s] = lax.fori_loop(0, reqs, tally, 0, unroll=8)

    def drain(r, carry):
        landed = cells.at[0, pl.ds(0, heads)] if spare else cells.at[0, 0]
        pltpu.make_async_copy(states.at[r], landed, sems.at[r]).wait()
        return carry

    lax.fori_loop(0, reqs, drain, 0, unroll=4)


def pack(placed, states, n_group, spare):
    reqs, heads, key_size, value_size = states.shape
    cell = (heads + 1,) if spare else (SLOT_CAP, heads)
    cells = (n_group * SUBGROUPS,) + cell + (key_size, value_size)
    return pl.pallas_call(
        lambda *refs: pack_kernel(n_group, reqs, spare, *refs),
        out_shape=(
            pltpu.VMEM(cells, states.dtype),
            jax.ShapeDtypeStruct((n_group,), jnp.int32),
        ),
        in_specs=[
            pl.BlockSpec(memory_space=pltpu.SMEM),
            pl.BlockSpec(memory_space=pltpu.HBM),
        ],
        out_specs=(
            pl.BlockSpec(memory_space=pltpu.VMEM),
            pl.BlockSpec(memory_space=pltpu.SMEM),
        ),
        scratch_shapes=[
            pltpu.SMEM((n_group * SUBGROUPS,), jnp.int32),
            pltpu.SemaphoreType.DMA((reqs,)),
        ],
        compiler_params=pltpu.CompilerParams(vmem_limit_bytes=32 * 1024 * 1024),
    )(placed, pltpu.with_memory_space_constraint(states, pltpu.HBM))


def split(x):
    high = x.astype(jnp.bfloat16)
    return high, (x - high.astype(jnp.float32)).astype(jnp.bfloat16)


def row_sums(parts):
    rows, lanes = parts[0].shape
    high, low = split(jnp.concatenate(parts, axis=0))
    sums = jnp.dot(
        jnp.concatenate([high, low], axis=1),
        jnp.ones((2 * lanes, lanes), jnp.bfloat16),
        preferred_element_type=jnp.float32,
    )
    return [sums[n * rows : (n + 1) * rows] for n in range(len(parts))]


def widen(columns, width):
    rows, count = columns.shape
    high, rest = split(columns)
    low = columns - high.astype(jnp.float32) - rest.astype(jnp.float32)
    parts = [high.astype(jnp.float32), rest.astype(jnp.float32), low]
    lane = lax.broadcasted_iota(jnp.int32, (count, count * width), 1)
    column = lax.broadcasted_iota(jnp.int32, (count, count * width), 0)
    wide = jnp.dot(
        jnp.concatenate(parts, axis=0).astype(jnp.bfloat16),
        jnp.where(lane // width == column, 1.0, 0.0).astype(jnp.bfloat16),
        preferred_element_type=jnp.float32,
    )
    return wide[:rows] + wide[rows : 2 * rows] + wide[2 * rows :]


def decode_kernel(
    load, chosen, sources, slot, first, live, query, key, value, gate, strength, decay, gain, tokens, states,
    by_key, by_query, values, fades, writes, key_rows, query_rows, kept,
):
    size, width = states.shape[2:]
    heads = states.shape[1] // SUBGROUPS
    steps = key.shape[4]
    units = [(n, i) for n in range(sources) for i in range(SUBGROUPS)]
    count = len(units)

    def keys(i):
        return slice(i * size, (i + 1) * size)

    def lanes(i):
        return slice(i * heads * width, (i + 1) * heads * width)

    def state_of(n, i):
        return jnp.concatenate(
            [states[first + n, heads * i + a] for a in range(heads)]
            if chosen
            else load(first + n, i),
            axis=1,
        )

    def rows(t):
        return slice(t * count, (t + 1) * count)

    def spread(ref, u, x):
        for a in range(heads):
            ref[a, pl.ds(u, steps, stride=count), :] = x[:, a * width : (a + 1) * width]

    def gather(ref, u):
        return jnp.concatenate(
            [ref[a, pl.ds(u, steps, stride=count), :] for a in range(heads)], axis=1
        )

    for u, (n, i) in enumerate(units):
        for ref, x in ((key_rows, key), (query_rows, query)):
            part = x[0, 0, first + n, slot, :, keys(i)]
            ref[pl.ds(u, steps, stride=count), :] = part.astype(jnp.float32)
    wide = widen(
        jnp.concatenate(
            [x[0, 0, first + n, slot] for x in (decay, strength) for n in range(sources)], axis=0
        ),
        width,
    )
    for u, (n, i) in enumerate(units):
        key_f = key[0, 0, first + n, slot, :, keys(i)].astype(jnp.float32)
        query_f = query[0, 0, first + n, slot, :, keys(i)].astype(jnp.float32)
        both = jnp.concatenate([key_f, query_f], axis=0).astype(jnp.bfloat16)
        before = load(first + n, i)
        if chosen:
            for a in range(heads):
                states[first + n, heads * i + a] = before[a]
        high, low = split(jnp.concatenate(before, axis=1))
        product = jnp.dot(
            jnp.concatenate([both, both], axis=1),
            jnp.concatenate([high, low], axis=0),
            preferred_element_type=jnp.float32,
        )
        spread(by_key, u, product[:steps])
        spread(by_query, u, product[steps:])
        spread(values, u, value[0, 0, first + n, slot, :, lanes(i)].astype(jnp.float32))
        spread(fades, u, wide[n * steps : (n + 1) * steps, lanes(i)])
        spread(writes, u, wide[(sources + n) * steps : (sources + n + 1) * steps, lanes(i)])

    on_key = [[by_key[a, rows(t)] for a in range(heads)] for t in range(steps)]
    on_query = [[by_query[a, rows(t)] for a in range(heads)] for t in range(steps)]
    keyed = [key_rows[rows(t)] for t in range(steps)]
    asked = [query_rows[rows(t)] for t in range(steps)]
    pairs = [(l, t) for t in range(steps) for l in range(t, steps)]
    key_key = dict(zip(pairs, row_sums([keyed[l] * keyed[t] for l, t in pairs])))
    query_key = dict(zip(pairs, row_sums([asked[l] * keyed[t] for l, t in pairs])))
    query_norms = [lax.rsqrt(x + EPS) / math.sqrt(size) for x in row_sums([q * q for q in asked])]
    written, total = [], None
    for t in range(steps):
        fade = [fades[a, rows(t)] for a in range(heads)]
        total = fade if total is None else [x * f for x, f in zip(total, fade)]
        norm = lax.rsqrt(key_key[t, t] + EPS)
        write = []
        for a in range(heads):
            residual = values[a, rows(t)] - norm * (on_key[t][a] * fade[a])
            write.append(writes[a, rows(t)] * norm * residual)
        written = [[w * f for w, f in zip(old, fade)] for old in written] + [write]
        for later in range(t, steps):
            for on, dots in ((on_key, key_key), (on_query, query_key)):
                if on is on_query or later > t:
                    dot = dots[later, t]
                    on[later] = [x * f + dot * w for x, f, w in zip(on[later], fade, write)]
    kept[...] = jnp.concatenate(total, axis=1)
    readouts = [x * query_norms[t] for t in range(steps) for x in on_query[t]]
    squares = row_sums([x * x for x in readouts])
    for t in range(steps):
        for a in range(heads):
            by_key[a, rows(t)] = written[t][a]
            norm = lax.rsqrt(squares[t * heads + a] / width + EPS)
            by_query[a, rows(t)] = readouts[t * heads + a] * norm * gain[...]

    for u, (n, i) in enumerate(units):
        key_f = key[0, 0, first + n, slot, :, keys(i)].astype(jnp.float32)
        high, low = split(gather(by_key, u))
        update = lax.dot_general(
            jnp.concatenate([key_f, key_f], axis=0).astype(jnp.bfloat16),
            jnp.concatenate([high.astype(jnp.float32), low.astype(jnp.float32)], axis=0).astype(
                jnp.bfloat16
            ),
            (((0,), (0,)), ((), ())),
            preferred_element_type=jnp.float32,
        )
        state = kept[u : u + 1, :] * state_of(n, i) + update
        for a in range(heads):
            states[first + n, heads * i + a] = state[:, a * width : (a + 1) * width]
        opened = gate[0, 0, first + n, slot, :, lanes(i)].astype(jnp.float32)
        token = gather(by_query, u) * (opened * jax.nn.sigmoid(opened))
        tokens[first + n, :, lanes(i)] = token.astype(tokens.dtype)

    for n in range(sources):

        @pl.when(live[first + n] <= slot)
        def _(n=n):
            tokens[first + n] = jnp.zeros(tokens.shape[1:], tokens.dtype)
            states[first + n] = jnp.zeros(states.shape[1:], states.dtype)


def decode(live, sources, load, slot, small, gain, earlier=None):
    queries, values = small[0], small[2]
    n_group, cap, steps = queries.shape[2:5]
    key_size, value_size = queries.shape[5] // SUBGROUPS, gain.shape[1]
    heads = values.shape[5] // (SUBGROUPS * value_size)
    block = (SUBGROUPS * heads, key_size, value_size)
    batch_size = SOURCES * 2 if earlier else SOURCES
    units = batch_size * SUBGROUPS
    rows = steps * units
    by_step = (heads, rows, value_size)
    scratch = [by_step] * 5 + [(rows, key_size)] * 2 + [(units, heads * value_size)]
    kept = () if earlier is None else (earlier[2], *earlier[:2])

    def kernel(live, *refs):
        blocks, refs = refs[: len(sources)], refs[len(sources) :]
        ins, refs = refs[: len(small) + 1], refs[len(small) + 1 :]
        before, refs = refs[: len(kept)], refs[len(kept) :]
        result, finals, *refs = refs
        handed, refs = refs[: 0 if kept else 1], refs[0 if kept else 1 :]
        states, sems, *work = refs
        tokens, blank = work.pop(), work.pop()
        n_sem = 2 * n_group

        def erase(group):
            return pltpu.make_async_copy(
                blank, finals.at[0, 0, group, cap - 1], sems.at[n_group + group]
            )

        def place(group):
            return pltpu.make_async_copy(
                states.at[group], finals.at[0, 0, group, slot], sems.at[group]
            )

        def run(batch, carry):
            first = batch * batch_size

            def compute():
                decode_kernel(
                    lambda s, i: load(s, i, *blocks), len(sources) > 1, batch_size, slot, first,
                    live, *ins, tokens.at[0, 0, :, slot], states, *work,
                )

            if kept:
                some = live[first] > slot
                for n in range(1, batch_size):
                    some = some | (live[first + n] > slot)
                pl.when(some)(compute)
                for n in range(batch_size):
                    pl.when(live[first + n] > slot)(lambda n=n: place(first + n).start())
            else:
                compute()
                for n in range(batch_size):
                    place(first + n).start()
            return carry

        def add_slot():
            lax.fori_loop(0, n_group // batch_size, run, 0)
            tokens[0, 0, :, 0] = before[0][...]
            copy = pltpu.make_async_copy(tokens, result, sems.at[n_sem])
            copy.start()
            for group in range(n_group):
                pl.when(live[group] > slot)(lambda group=group: place(group).wait())
            copy.wait()

        if kept:
            tokens[0, 0, :, slot] = jnp.zeros((n_group,) + values.shape[4:], jnp.bfloat16)
            some = live[0] > slot
            for group in range(1, n_group):
                some = some | (live[group] > slot)
            pl.when(some)(add_slot)
        else:
            blank[...] = jnp.zeros(block, jnp.float32)
            for group in range(n_group):
                pl.when(live[group] < cap)(lambda group=group: erase(group).start())
            tokens[0, 0, :, cap - 1] = jnp.zeros((n_group,) + values.shape[4:], jnp.bfloat16)
            lax.fori_loop(0, n_group // batch_size, run, 0)
            handed[0][...] = tokens[0, 0, :, slot]
            copy = pltpu.make_async_copy(tokens, result, sems.at[n_sem])
            copy.start()
            for group in range(n_group):
                place(group).wait()
                pl.when(live[group] < cap)(lambda group=group: erase(group).wait())
            copy.wait()

    vmem, any_space = pl.BlockSpec(memory_space=pltpu.VMEM), pl.BlockSpec(memory_space=pl.ANY)
    in_vmem = [pltpu.with_memory_space_constraint(x, pltpu.VMEM) for x in sources]
    return pl.pallas_call(
        kernel,
        out_shape=(
            jax.ShapeDtypeStruct(values.shape, jnp.bfloat16),
            jax.ShapeDtypeStruct((1, 1, n_group, cap) + block, jnp.float32),
        )
        + (() if kept else (jax.ShapeDtypeStruct((n_group,) + values.shape[4:], jnp.bfloat16),)),
        in_specs=[pl.BlockSpec(memory_space=pltpu.SMEM)]
        + [vmem] * (len(sources) + len(small) + 1)
        + [vmem, any_space, any_space][: len(kept)],
        out_specs=(any_space, any_space) + (() if kept else (vmem,)),
        scratch_shapes=[
            pltpu.VMEM((n_group,) + block, jnp.float32),
            pltpu.SemaphoreType.DMA((2 * n_group + 1,)),
        ]
        + [pltpu.VMEM(shape, jnp.float32) for shape in scratch]
        + [pltpu.VMEM(block, jnp.float32), pltpu.VMEM(values.shape, jnp.bfloat16)],
        input_output_aliases={len(sources) + len(small) + 3 + n: n for n in range(2)}
        if kept
        else {},
        compiler_params=pltpu.CompilerParams(vmem_limit_bytes=32 * 1024 * 1024),
    )(live, *in_vmem, *small, gain, *kept)


def exchange(cells):
    return lax.all_to_all(cells, ("group", "sub"), split_axis=0, concat_axis=0, tiled=True)


def with_spare(placed, states, small, gain, n_group):
    cells, live = pack(placed, states, n_group, True)
    heads, key_size, value_size = states.shape[1:]
    square = (key_size, value_size)
    arrived = exchange(cells)
    spare = arrived[:, heads]
    swap = [(n, n ^ 1) for n in range(SUBGROUPS)]
    other = lax.ppermute(spare, "sub", swap)
    by_source = arrived.reshape((n_group, SUBGROUPS, heads + 1) + square)
    other = other.reshape((n_group, SUBGROUPS) + square)
    earlier = decode(
        live, [by_source], lambda s, i, x: [x[s, i, a] for a in range(heads)], 0, small, gain
    )

    def load(s, i, x, y):
        core = lax.axis_index("sub") % CORES
        return [jnp.where(core == a, x[s, i, heads], y[s, i]) for a in range(heads)]

    return decode(live, [by_source, other], load, 1, small, gain, earlier)


def without_spare(placed, states, small, gain, n_group):
    cells, live = pack(placed, states, n_group, False)
    heads, key_size, value_size = states.shape[1:]
    square = (key_size, value_size)
    arrived = exchange(cells).reshape((n_group, SUBGROUPS, SLOT_CAP, heads) + square)
    earlier = None
    for slot in range(SLOT_CAP):
        earlier = decode(
            live,
            [arrived],
            lambda s, i, x, slot=slot: [x[s, i, slot, a] for a in range(heads)],
            slot,
            small,
            gain,
            earlier,
        )
    return earlier


def local(states, placement, queries, key_vectors, value_vectors, gate_inputs, strength, decay, gain):
    n_group = lax.axis_size("group")
    placed = placement.reshape(placement.shape[0])
    fits = cells_fit(placed, n_group * SUBGROUPS, states.shape[0])
    small = (queries, key_vectors, value_vectors, gate_inputs, strength, decay)
    gain = gain.reshape(1, gain.shape[0])
    return lax.switch(
        fits[0],
        [lambda *x: without_spare(*x, n_group), lambda *x: with_spare(*x, n_group)],
        placed,
        states,
        small,
        gain,
    )


def solution(mesh):
    n_group, n_head = mesh.devices.shape
    quads = Mesh(
        mesh.devices.reshape(n_group, n_head // SUBGROUPS, SUBGROUPS), ("group", "block", "sub")
    )
    spread = P("group", ("block", "sub"))
    return jax.shard_map(
        local,
        mesh=quads,
        in_specs=(spread, P(), spread, spread, spread, spread, spread, spread, P()),
        out_specs=(spread, spread),
        check_vma=False,
    )
```

```python
import math

import jax
import jax.numpy as jnp
from jax import lax
from jax.experimental import pallas as pl
from jax.experimental.pallas import tpu as pltpu
from jax.sharding import Mesh
from jax.sharding import PartitionSpec as P

SUBGROUPS = 4
SLOT_CAP = 2
CORES = 2
SOURCES = 2
EPS = 1e-06


def fits_kernel(dec_groups, reqs, placed, fits):
    lanes = placed.shape[1]
    chips = placed[...] // CORES
    named = [jnp.where(chips == chip, 1.0, 0.0) for chip in range(dec_groups // CORES)]
    lane = lax.broadcasted_iota(jnp.int32, (lanes, lanes), 0)
    group = lax.broadcasted_iota(jnp.int32, (lanes, lanes), 1)
    counts = jnp.dot(
        jnp.concatenate(named, axis=0).astype(jnp.bfloat16),
        jnp.where(lane // reqs == group, 1.0, 0.0).astype(jnp.bfloat16),
        preferred_element_type=jnp.float32,
    )
    fits[0] = jnp.where(jnp.max(counts) < SLOT_CAP + 1.5, 1, 0)


def cells_fit(placed, dec_groups, reqs):
    return pl.pallas_call(
        lambda *refs: fits_kernel(dec_groups, reqs, *refs),
        out_shape=jax.ShapeDtypeStruct((1,), jnp.int32),
        in_specs=[pl.BlockSpec(memory_space=pltpu.VMEM)],
        out_specs=pl.BlockSpec(memory_space=pltpu.SMEM),
    )(placed.reshape(-1, 128))


def pack_kernel(n_group, reqs, spare, placed, states, cells, live, count, sems):
    group = lax.axis_index("group")
    mine = group * SUBGROUPS + lax.axis_index("sub")
    heads = states.shape[1]

    def clear(d, carry):
        count[d] = 0
        return carry

    lax.fori_loop(0, n_group * SUBGROUPS, clear, 0, unroll=8)

    def send(r, carry):
        d = placed[group * reqs + r]
        rank = count[d]
        count[d] = rank + 1
        if spare:

            @pl.when(rank == 0)
            def _():
                pltpu.make_async_copy(
                    states.at[r], cells.at[d, pl.ds(0, heads)], sems.at[r]
                ).start()

            @pl.when(rank > 0)
            def _():
                for a in range(heads):
                    pltpu.make_async_copy(
                        states.at[r, a], cells.at[d // CORES * CORES + a, heads], sems.at[r]
                    ).start()

        else:
            pltpu.make_async_copy(states.at[r], cells.at[d, rank], sems.at[r]).start()
        return carry

    lax.fori_loop(0, reqs, send, 0, unroll=4)

    for s in range(n_group):

        def tally(r, total, s=s):
            return total + jnp.where(placed[s * reqs + r] == mine, 1, 0)

        live[s] = lax.fori_loop(0, reqs, tally, 0, unroll=8)

    def drain(r, carry):
        landed = cells.at[0, pl.ds(0, heads)] if spare else cells.at[0, 0]
        pltpu.make_async_copy(states.at[r], landed, sems.at[r]).wait()
        return carry

    lax.fori_loop(0, reqs, drain, 0, unroll=4)


def pack(placed, states, n_group, spare):
    reqs, heads, key_size, value_size = states.shape
    cell = (heads + 1,) if spare else (SLOT_CAP, heads)
    cells = (n_group * SUBGROUPS,) + cell + (key_size, value_size)
    return pl.pallas_call(
        lambda *refs: pack_kernel(n_group, reqs, spare, *refs),
        out_shape=(
            pltpu.VMEM(cells, states.dtype),
            jax.ShapeDtypeStruct((n_group,), jnp.int32),
        ),
        in_specs=[
            pl.BlockSpec(memory_space=pltpu.SMEM),
            pl.BlockSpec(memory_space=pltpu.HBM),
        ],
        out_specs=(
            pl.BlockSpec(memory_space=pltpu.VMEM),
            pl.BlockSpec(memory_space=pltpu.SMEM),
        ),
        scratch_shapes=[
            pltpu.SMEM((n_group * SUBGROUPS,), jnp.int32),
            pltpu.SemaphoreType.DMA((reqs,)),
        ],
        compiler_params=pltpu.CompilerParams(vmem_limit_bytes=32 * 1024 * 1024),
    )(placed, pltpu.with_memory_space_constraint(states, pltpu.HBM))


def split(x):
    high = x.astype(jnp.bfloat16)
    return high, (x - high.astype(jnp.float32)).astype(jnp.bfloat16)


def row_sums(parts):
    rows, lanes = parts[0].shape
    high, low = split(jnp.concatenate(parts, axis=0))
    sums = jnp.dot(
        jnp.concatenate([high, low], axis=1),
        jnp.ones((2 * lanes, lanes), jnp.bfloat16),
        preferred_element_type=jnp.float32,
    )
    return [sums[n * rows : (n + 1) * rows] for n in range(len(parts))]


def widen(columns, width):
    rows, count = columns.shape
    high, rest = split(columns)
    low = columns - high.astype(jnp.float32) - rest.astype(jnp.float32)
    parts = [high.astype(jnp.float32), rest.astype(jnp.float32), low]
    lane = lax.broadcasted_iota(jnp.int32, (count, count * width), 1)
    column = lax.broadcasted_iota(jnp.int32, (count, count * width), 0)
    wide = jnp.dot(
        jnp.concatenate(parts, axis=0).astype(jnp.bfloat16),
        jnp.where(lane // width == column, 1.0, 0.0).astype(jnp.bfloat16),
        preferred_element_type=jnp.float32,
    )
    return wide[:rows] + wide[rows : 2 * rows] + wide[2 * rows :]


def decode_kernel(
    load, sources, slot, first, live, query, key, value, gate, strength, decay, gain, tokens, states,
    by_key, by_query, values, fades, writes, key_rows, query_rows, kept,
):
    size, width = states.shape[2:]
    heads = states.shape[1] // SUBGROUPS
    steps = key.shape[4]
    units = [(n, i) for n in range(sources) for i in range(SUBGROUPS)]
    count = len(units)

    def keys(i):
        return slice(i * size, (i + 1) * size)

    def lanes(i):
        return slice(i * heads * width, (i + 1) * heads * width)

    def state_of(n, i):
        return jnp.concatenate(load(first + n, i), axis=1)

    def rows(t):
        return slice(t * count, (t + 1) * count)

    def spread(ref, u, x):
        for a in range(heads):
            ref[a, pl.ds(u, steps, stride=count), :] = x[:, a * width : (a + 1) * width]

    def gather(ref, u):
        return jnp.concatenate(
            [ref[a, pl.ds(u, steps, stride=count), :] for a in range(heads)], axis=1
        )

    for u, (n, i) in enumerate(units):
        for ref, x in ((key_rows, key), (query_rows, query)):
            part = x[0, 0, first + n, slot, :, keys(i)]
            ref[pl.ds(u, steps, stride=count), :] = part.astype(jnp.float32)
    wide = widen(
        jnp.concatenate(
            [x[0, 0, first + n, slot] for x in (decay, strength) for n in range(sources)], axis=0
        ),
        width,
    )
    for u, (n, i) in enumerate(units):
        key_f = key[0, 0, first + n, slot, :, keys(i)].astype(jnp.float32)
        query_f = query[0, 0, first + n, slot, :, keys(i)].astype(jnp.float32)
        both = jnp.concatenate([key_f, query_f], axis=0).astype(jnp.bfloat16)
        high, low = split(state_of(n, i))
        product = jnp.dot(
            jnp.concatenate([both, both], axis=1),
            jnp.concatenate([high, low], axis=0),
            preferred_element_type=jnp.float32,
        )
        spread(by_key, u, product[:steps])
        spread(by_query, u, product[steps:])
        spread(values, u, value[0, 0, first + n, slot, :, lanes(i)].astype(jnp.float32))
        spread(fades, u, wide[n * steps : (n + 1) * steps, lanes(i)])
        spread(writes, u, wide[(sources + n) * steps : (sources + n + 1) * steps, lanes(i)])

    on_key = [[by_key[a, rows(t)] for a in range(heads)] for t in range(steps)]
    on_query = [[by_query[a, rows(t)] for a in range(heads)] for t in range(steps)]
    keyed = [key_rows[rows(t)] for t in range(steps)]
    asked = [query_rows[rows(t)] for t in range(steps)]
    pairs = [(l, t) for t in range(steps) for l in range(t, steps)]
    key_key = dict(zip(pairs, row_sums([keyed[l] * keyed[t] for l, t in pairs])))
    query_key = dict(zip(pairs, row_sums([asked[l] * keyed[t] for l, t in pairs])))
    query_norms = [lax.rsqrt(x + EPS) / math.sqrt(size) for x in row_sums([q * q for q in asked])]
    written, total = [], None
    for t in range(steps):
        fade = [fades[a, rows(t)] for a in range(heads)]
        total = fade if total is None else [x * f for x, f in zip(total, fade)]
        norm = lax.rsqrt(key_key[t, t] + EPS)
        write = []
        for a in range(heads):
            residual = values[a, rows(t)] - norm * (on_key[t][a] * fade[a])
            write.append(writes[a, rows(t)] * norm * residual)
        written = [[w * f for w, f in zip(old, fade)] for old in written] + [write]
        for later in range(t, steps):
            for on, dots in ((on_key, key_key), (on_query, query_key)):
                if on is on_query or later > t:
                    dot = dots[later, t]
                    on[later] = [x * f + dot * w for x, f, w in zip(on[later], fade, write)]
    kept[...] = jnp.concatenate(total, axis=1)
    readouts = [x * query_norms[t] for t in range(steps) for x in on_query[t]]
    squares = row_sums([x * x for x in readouts])
    for t in range(steps):
        for a in range(heads):
            by_key[a, rows(t)] = written[t][a]
            norm = lax.rsqrt(squares[t * heads + a] / width + EPS)
            by_query[a, rows(t)] = readouts[t * heads + a] * norm * gain[...]

    for u, (n, i) in enumerate(units):
        key_f = key[0, 0, first + n, slot, :, keys(i)].astype(jnp.float32)
        high, low = split(gather(by_key, u))
        update = lax.dot_general(
            jnp.concatenate([key_f, key_f], axis=0).astype(jnp.bfloat16),
            jnp.concatenate([high.astype(jnp.float32), low.astype(jnp.float32)], axis=0).astype(
                jnp.bfloat16
            ),
            (((0,), (0,)), ((), ())),
            preferred_element_type=jnp.float32,
        )
        state = kept[u : u + 1, :] * state_of(n, i) + update
        for a in range(heads):
            states[first + n, heads * i + a] = state[:, a * width : (a + 1) * width]
        opened = gate[0, 0, first + n, slot, :, lanes(i)].astype(jnp.float32)
        token = gather(by_query, u) * (opened * jax.nn.sigmoid(opened))
        tokens[first + n, :, lanes(i)] = token.astype(tokens.dtype)

    for n in range(sources):

        @pl.when(live[first + n] <= slot)
        def _(n=n):
            tokens[first + n] = jnp.zeros(tokens.shape[1:], tokens.dtype)
            states[first + n] = jnp.zeros(states.shape[1:], states.dtype)


def decode(live, sources, load, slot, small, gain, earlier=None):
    queries, values = small[0], small[2]
    n_group, cap, steps = queries.shape[2:5]
    key_size, value_size = queries.shape[5] // SUBGROUPS, gain.shape[1]
    heads = values.shape[5] // (SUBGROUPS * value_size)
    block = (SUBGROUPS * heads, key_size, value_size)
    batch_size = SOURCES * 2 if earlier else SOURCES
    units = batch_size * SUBGROUPS
    rows = steps * units
    by_step = (heads, rows, value_size)
    scratch = [by_step] * 5 + [(rows, key_size)] * 2 + [(units, heads * value_size)]
    kept = () if earlier is None else (earlier[2], *earlier[:2])

    def kernel(live, *refs):
        blocks, refs = refs[: len(sources)], refs[len(sources) :]
        ins, refs = refs[: len(small) + 1], refs[len(small) + 1 :]
        before, refs = refs[: len(kept)], refs[len(kept) :]
        result, finals, *refs = refs
        handed, refs = refs[: 0 if kept else 1], refs[0 if kept else 1 :]
        states, sems, *work = refs
        tokens, blank = work.pop(), work.pop()
        n_sem = 2 * n_group

        def erase(group):
            return pltpu.make_async_copy(
                blank, finals.at[0, 0, group, cap - 1], sems.at[n_group + group]
            )

        def place(group):
            return pltpu.make_async_copy(
                states.at[group], finals.at[0, 0, group, slot], sems.at[group]
            )

        def run(batch, carry):
            first = batch * batch_size

            def compute(core):
                decode_kernel(
                    lambda s, i: load(s, i, core, *blocks), batch_size, slot, first, live, *ins,
                    tokens.at[0, 0, :, slot], states, *work,
                )

            if kept:
                some = live[first] > slot
                for n in range(1, batch_size):
                    some = some | (live[first + n] > slot)
                if len(sources) > 1:
                    me = lax.axis_index("sub") % CORES
                    for core in range(CORES):
                        pl.when(some & (me == core))(lambda core=core: compute(core))
                else:
                    pl.when(some)(lambda: compute(0))
                for n in range(batch_size):
                    pl.when(live[first + n] > slot)(lambda n=n: place(first + n).start())
            else:
                compute(0)
                for n in range(batch_size):
                    place(first + n).start()
            return carry

        def add_slot():
            lax.fori_loop(0, n_group // batch_size, run, 0)
            tokens[0, 0, :, 0] = before[0][...]
            copy = pltpu.make_async_copy(tokens, result, sems.at[n_sem])
            copy.start()
            for group in range(n_group):
                pl.when(live[group] > slot)(lambda group=group: place(group).wait())
            copy.wait()

        if kept:
            tokens[0, 0, :, slot] = jnp.zeros((n_group,) + values.shape[4:], jnp.bfloat16)
            some = live[0] > slot
            for group in range(1, n_group):
                some = some | (live[group] > slot)
            pl.when(some)(add_slot)
        else:
            blank[...] = jnp.zeros(block, jnp.float32)
            for group in range(n_group):
                pl.when(live[group] < cap)(lambda group=group: erase(group).start())
            tokens[0, 0, :, cap - 1] = jnp.zeros((n_group,) + values.shape[4:], jnp.bfloat16)
            lax.fori_loop(0, n_group // batch_size, run, 0)
            handed[0][...] = tokens[0, 0, :, slot]
            copy = pltpu.make_async_copy(tokens, result, sems.at[n_sem])
            copy.start()
            for group in range(n_group):
                place(group).wait()
                pl.when(live[group] < cap)(lambda group=group: erase(group).wait())
            copy.wait()

    vmem, any_space = pl.BlockSpec(memory_space=pltpu.VMEM), pl.BlockSpec(memory_space=pl.ANY)
    in_vmem = [pltpu.with_memory_space_constraint(x, pltpu.VMEM) for x in sources]
    return pl.pallas_call(
        kernel,
        out_shape=(
            jax.ShapeDtypeStruct(values.shape, jnp.bfloat16),
            jax.ShapeDtypeStruct((1, 1, n_group, cap) + block, jnp.float32),
        )
        + (() if kept else (jax.ShapeDtypeStruct((n_group,) + values.shape[4:], jnp.bfloat16),)),
        in_specs=[pl.BlockSpec(memory_space=pltpu.SMEM)]
        + [vmem] * (len(sources) + len(small) + 1)
        + [vmem, any_space, any_space][: len(kept)],
        out_specs=(any_space, any_space) + (() if kept else (vmem,)),
        scratch_shapes=[
            pltpu.VMEM((n_group,) + block, jnp.float32),
            pltpu.SemaphoreType.DMA((2 * n_group + 1,)),
        ]
        + [pltpu.VMEM(shape, jnp.float32) for shape in scratch]
        + [pltpu.VMEM(block, jnp.float32), pltpu.VMEM(values.shape, jnp.bfloat16)],
        input_output_aliases={len(sources) + len(small) + 3 + n: n for n in range(2)}
        if kept
        else {},
        compiler_params=pltpu.CompilerParams(vmem_limit_bytes=32 * 1024 * 1024),
    )(live, *in_vmem, *small, gain, *kept)


def exchange(cells):
    return lax.all_to_all(cells, ("group", "sub"), split_axis=0, concat_axis=0, tiled=True)


def with_spare(placed, states, small, gain, n_group):
    cells, live = pack(placed, states, n_group, True)
    heads, key_size, value_size = states.shape[1:]
    square = (key_size, value_size)
    arrived = exchange(cells)
    spare = arrived[:, heads]
    swap = [(n, n ^ 1) for n in range(SUBGROUPS)]
    other = lax.ppermute(spare, "sub", swap)
    by_source = arrived.reshape((n_group, SUBGROUPS, heads + 1) + square)
    other = other.reshape((n_group, SUBGROUPS) + square)
    earlier = decode(
        live, [by_source], lambda s, i, _, x: [x[s, i, a] for a in range(heads)], 0, small, gain
    )

    def load(s, i, core, x, y):
        return [x[s, i, heads] if core == a else y[s, i] for a in range(heads)]

    return decode(live, [by_source, other], load, 1, small, gain, earlier)


def without_spare(placed, states, small, gain, n_group):
    cells, live = pack(placed, states, n_group, False)
    heads, key_size, value_size = states.shape[1:]
    square = (key_size, value_size)
    arrived = exchange(cells).reshape((n_group, SUBGROUPS, SLOT_CAP, heads) + square)
    earlier = None
    for slot in range(SLOT_CAP):
        earlier = decode(
            live,
            [arrived],
            lambda s, i, _, x, slot=slot: [x[s, i, slot, a] for a in range(heads)],
            slot,
            small,
            gain,
            earlier,
        )
    return earlier


def local(states, placement, queries, key_vectors, value_vectors, gate_inputs, strength, decay, gain):
    n_group = lax.axis_size("group")
    placed = placement.reshape(placement.shape[0])
    fits = cells_fit(placed, n_group * SUBGROUPS, states.shape[0])
    small = (queries, key_vectors, value_vectors, gate_inputs, strength, decay)
    gain = gain.reshape(1, gain.shape[0])
    return lax.switch(
        fits[0],
        [lambda *x: without_spare(*x, n_group), lambda *x: with_spare(*x, n_group)],
        placed,
        states,
        small,
        gain,
    )


def solution(mesh):
    n_group, n_head = mesh.devices.shape
    quads = Mesh(
        mesh.devices.reshape(n_group, n_head // SUBGROUPS, SUBGROUPS), ("group", "block", "sub")
    )
    spread = P("group", ("block", "sub"))
    return jax.shard_map(
        local,
        mesh=quads,
        in_specs=(spread, P(), spread, spread, spread, spread, spread, spread, P()),
        out_specs=(spread, spread),
        check_vma=False,
    )
```

```python
import math

import jax
import jax.numpy as jnp
from jax import lax
from jax.experimental import pallas as pl
from jax.experimental.pallas import tpu as pltpu
from jax.sharding import Mesh
from jax.sharding import PartitionSpec as P

SUBGROUPS = 4
SLOT_CAP = 2
CORES = 2
SOURCES = 2
EPS = 1e-06


def fits_kernel(dec_groups, reqs, placed, fits):
    lanes = placed.shape[1]
    chips = placed[...] // CORES
    named = [jnp.where(chips == chip, 1.0, 0.0) for chip in range(dec_groups // CORES)]
    lane = lax.broadcasted_iota(jnp.int32, (lanes, lanes), 0)
    group = lax.broadcasted_iota(jnp.int32, (lanes, lanes), 1)
    counts = jnp.dot(
        jnp.concatenate(named, axis=0).astype(jnp.bfloat16),
        jnp.where(lane // reqs == group, 1.0, 0.0).astype(jnp.bfloat16),
        preferred_element_type=jnp.float32,
    )
    fits[0] = jnp.where(jnp.max(counts) < SLOT_CAP + 1.5, 1, 0)


def cells_fit(placed, dec_groups, reqs):
    return pl.pallas_call(
        lambda *refs: fits_kernel(dec_groups, reqs, *refs),
        out_shape=jax.ShapeDtypeStruct((1,), jnp.int32),
        in_specs=[pl.BlockSpec(memory_space=pltpu.VMEM)],
        out_specs=pl.BlockSpec(memory_space=pltpu.SMEM),
    )(placed.reshape(-1, 128))


def pack_kernel(n_group, reqs, spare, placed, states, cells, live, count, sems):
    group = lax.axis_index("group")
    mine = group * SUBGROUPS + lax.axis_index("sub")
    heads = states.shape[1]

    def clear(d, carry):
        count[d] = 0
        return carry

    lax.fori_loop(0, n_group * SUBGROUPS, clear, 0, unroll=8)

    def send(r, carry):
        d = placed[group * reqs + r]
        rank = count[d]
        count[d] = rank + 1
        if spare:

            @pl.when(rank == 0)
            def _():
                pltpu.make_async_copy(
                    states.at[r], cells.at[d, pl.ds(0, heads)], sems.at[r]
                ).start()

            @pl.when(rank > 0)
            def _():
                for a in range(heads):
                    pltpu.make_async_copy(
                        states.at[r, a], cells.at[d // CORES * CORES + a, heads], sems.at[r]
                    ).start()

        else:
            pltpu.make_async_copy(states.at[r], cells.at[d, rank], sems.at[r]).start()
        return carry

    lax.fori_loop(0, reqs, send, 0, unroll=4)

    for s in range(n_group):

        def tally(r, total, s=s):
            return total + jnp.where(placed[s * reqs + r] == mine, 1, 0)

        live[s] = lax.fori_loop(0, reqs, tally, 0, unroll=8)

    def drain(r, carry):
        landed = cells.at[0, pl.ds(0, heads)] if spare else cells.at[0, 0]
        pltpu.make_async_copy(states.at[r], landed, sems.at[r]).wait()
        return carry

    lax.fori_loop(0, reqs, drain, 0, unroll=4)


def pack(placed, states, n_group, spare):
    reqs, heads, key_size, value_size = states.shape
    cell = (heads + 1,) if spare else (SLOT_CAP, heads)
    cells = (n_group * SUBGROUPS,) + cell + (key_size, value_size)
    return pl.pallas_call(
        lambda *refs: pack_kernel(n_group, reqs, spare, *refs),
        out_shape=(
            pltpu.VMEM(cells, states.dtype),
            jax.ShapeDtypeStruct((n_group,), jnp.int32),
        ),
        in_specs=[
            pl.BlockSpec(memory_space=pltpu.SMEM),
            pl.BlockSpec(memory_space=pltpu.HBM),
        ],
        out_specs=(
            pl.BlockSpec(memory_space=pltpu.VMEM),
            pl.BlockSpec(memory_space=pltpu.SMEM),
        ),
        scratch_shapes=[
            pltpu.SMEM((n_group * SUBGROUPS,), jnp.int32),
            pltpu.SemaphoreType.DMA((reqs,)),
        ],
        compiler_params=pltpu.CompilerParams(vmem_limit_bytes=32 * 1024 * 1024),
    )(placed, pltpu.with_memory_space_constraint(states, pltpu.HBM))


def split(x):
    high = x.astype(jnp.bfloat16)
    return high, (x - high.astype(jnp.float32)).astype(jnp.bfloat16)


def row_sums(parts):
    rows, lanes = parts[0].shape
    high, low = split(jnp.concatenate(parts, axis=0))
    sums = jnp.dot(
        jnp.concatenate([high, low], axis=1),
        jnp.ones((2 * lanes, lanes), jnp.bfloat16),
        preferred_element_type=jnp.float32,
    )
    return [sums[n * rows : (n + 1) * rows] for n in range(len(parts))]


def widen(columns, width):
    rows, count = columns.shape
    high, rest = split(columns)
    low = columns - high.astype(jnp.float32) - rest.astype(jnp.float32)
    parts = [high.astype(jnp.float32), rest.astype(jnp.float32), low]
    lane = lax.broadcasted_iota(jnp.int32, (count, count * width), 1)
    column = lax.broadcasted_iota(jnp.int32, (count, count * width), 0)
    wide = jnp.dot(
        jnp.concatenate(parts, axis=0).astype(jnp.bfloat16),
        jnp.where(lane // width == column, 1.0, 0.0).astype(jnp.bfloat16),
        preferred_element_type=jnp.float32,
    )
    return wide[:rows] + wide[rows : 2 * rows] + wide[2 * rows :]


def decode_kernel(
    load, sources, slot, first, live, query, key, value, gate, strength, decay, gain, tokens, states,
    by_key, by_query, values, fades, writes, key_rows, query_rows, kept,
):
    size, width = states.shape[2:]
    heads = states.shape[1] // SUBGROUPS
    steps = key.shape[4]
    units = [(n, i) for n in range(sources) for i in range(SUBGROUPS)]
    count = len(units)

    def keys(i):
        return slice(i * size, (i + 1) * size)

    def lanes(i):
        return slice(i * heads * width, (i + 1) * heads * width)

    def state_of(n, i):
        return jnp.concatenate(load(first + n, i), axis=1)

    def rows(t):
        return slice(t * count, (t + 1) * count)

    def spread(ref, u, x):
        for a in range(heads):
            ref[a, pl.ds(u, steps, stride=count), :] = x[:, a * width : (a + 1) * width]

    def gather(ref, u):
        return jnp.concatenate(
            [ref[a, pl.ds(u, steps, stride=count), :] for a in range(heads)], axis=1
        )

    for u, (n, i) in enumerate(units):
        for ref, x in ((key_rows, key), (query_rows, query)):
            part = x[0, 0, first + n, slot, :, keys(i)]
            ref[pl.ds(u, steps, stride=count), :] = part.astype(jnp.float32)
    wide = widen(
        jnp.concatenate(
            [x[0, 0, first + n, slot] for x in (decay, strength) for n in range(sources)], axis=0
        ),
        width,
    )
    for u, (n, i) in enumerate(units):
        key_f = key[0, 0, first + n, slot, :, keys(i)].astype(jnp.float32)
        query_f = query[0, 0, first + n, slot, :, keys(i)].astype(jnp.float32)
        both = jnp.concatenate([key_f, query_f], axis=0).astype(jnp.bfloat16)
        high, low = split(state_of(n, i))
        product = jnp.dot(
            jnp.concatenate([both, both], axis=1),
            jnp.concatenate([high, low], axis=0),
            preferred_element_type=jnp.float32,
        )
        spread(by_key, u, product[:steps])
        spread(by_query, u, product[steps:])
        spread(values, u, value[0, 0, first + n, slot, :, lanes(i)].astype(jnp.float32))
        spread(fades, u, wide[n * steps : (n + 1) * steps, lanes(i)])
        spread(writes, u, wide[(sources + n) * steps : (sources + n + 1) * steps, lanes(i)])

    on_key = [[by_key[a, rows(t)] for a in range(heads)] for t in range(steps)]
    on_query = [[by_query[a, rows(t)] for a in range(heads)] for t in range(steps)]
    keyed = [key_rows[rows(t)] for t in range(steps)]
    asked = [query_rows[rows(t)] for t in range(steps)]
    pairs = [(l, t) for t in range(steps) for l in range(t, steps)]
    key_key = dict(zip(pairs, row_sums([keyed[l] * keyed[t] for l, t in pairs])))
    query_key = dict(zip(pairs, row_sums([asked[l] * keyed[t] for l, t in pairs])))
    query_norms = [lax.rsqrt(x + EPS) / math.sqrt(size) for x in row_sums([q * q for q in asked])]
    written, total = [], None
    for t in range(steps):
        fade = [fades[a, rows(t)] for a in range(heads)]
        total = fade if total is None else [x * f for x, f in zip(total, fade)]
        norm = lax.rsqrt(key_key[t, t] + EPS)
        write = []
        for a in range(heads):
            residual = values[a, rows(t)] - norm * (on_key[t][a] * fade[a])
            write.append(writes[a, rows(t)] * norm * residual)
        written = [[w * f for w, f in zip(old, fade)] for old in written] + [write]
        for later in range(t, steps):
            for on, dots in ((on_key, key_key), (on_query, query_key)):
                if on is on_query or later > t:
                    dot = dots[later, t]
                    on[later] = [x * f + dot * w for x, f, w in zip(on[later], fade, write)]
    kept[...] = jnp.concatenate(total, axis=1)
    readouts = [x * query_norms[t] for t in range(steps) for x in on_query[t]]
    squares = row_sums([x * x for x in readouts])
    for t in range(steps):
        for a in range(heads):
            by_key[a, rows(t)] = written[t][a]
            norm = lax.rsqrt(squares[t * heads + a] / width + EPS)
            by_query[a, rows(t)] = readouts[t * heads + a] * norm * gain[...]

    for u, (n, i) in enumerate(units):
        key_f = key[0, 0, first + n, slot, :, keys(i)].astype(jnp.float32)
        high, low = split(gather(by_key, u))
        update = lax.dot_general(
            jnp.concatenate([key_f, key_f], axis=0).astype(jnp.bfloat16),
            jnp.concatenate([high.astype(jnp.float32), low.astype(jnp.float32)], axis=0).astype(
                jnp.bfloat16
            ),
            (((0,), (0,)), ((), ())),
            preferred_element_type=jnp.float32,
        )
        state = kept[u : u + 1, :] * state_of(n, i) + update
        for a in range(heads):
            states[first + n, heads * i + a] = state[:, a * width : (a + 1) * width]
        opened = gate[0, 0, first + n, slot, :, lanes(i)].astype(jnp.float32)
        token = gather(by_query, u) * (opened * jax.nn.sigmoid(opened))
        tokens[first + n, :, lanes(i)] = token.astype(tokens.dtype)

    for n in range(sources):

        @pl.when(live[first + n] <= slot)
        def _(n=n):
            tokens[first + n] = jnp.zeros(tokens.shape[1:], tokens.dtype)
            states[first + n] = jnp.zeros(states.shape[1:], states.dtype)


def decode(live, sources, load, slot, small, gain, earlier=None):
    queries, values = small[0], small[2]
    n_group, cap, steps = queries.shape[2:5]
    key_size, value_size = queries.shape[5] // SUBGROUPS, gain.shape[1]
    heads = values.shape[5] // (SUBGROUPS * value_size)
    block = (SUBGROUPS * heads, key_size, value_size)
    batch_size = SOURCES * 2 if earlier else SOURCES
    units = batch_size * SUBGROUPS
    rows = (steps + 1) * units
    by_step = (heads, rows, value_size)
    scratch = [by_step] * 5 + [(rows, key_size)] * 2 + [(units, heads * value_size)]
    kept = () if earlier is None else (earlier[2], *earlier[:2])

    def kernel(live, *refs):
        blocks, refs = refs[: len(sources)], refs[len(sources) :]
        ins, refs = refs[: len(small) + 1], refs[len(small) + 1 :]
        before, refs = refs[: len(kept)], refs[len(kept) :]
        result, finals, *refs = refs
        handed, refs = refs[: 0 if kept else 1], refs[0 if kept else 1 :]
        states, sems, *work = refs
        tokens, blank = work.pop(), work.pop()
        n_sem = 2 * n_group

        def erase(group):
            return pltpu.make_async_copy(
                blank, finals.at[0, 0, group, cap - 1], sems.at[n_group + group]
            )

        def place(group):
            return pltpu.make_async_copy(
                states.at[group], finals.at[0, 0, group, slot], sems.at[group]
            )

        def run(batch, carry):
            first = batch * batch_size

            def compute(core):
                decode_kernel(
                    lambda s, i: load(s, i, core, *blocks), batch_size, slot, first, live, *ins,
                    tokens.at[0, 0, :, slot], states, *work,
                )

            if kept:
                some = live[first] > slot
                for n in range(1, batch_size):
                    some = some | (live[first + n] > slot)
                if len(sources) > 1:
                    me = lax.axis_index("sub") % CORES
                    for core in range(CORES):
                        pl.when(some & (me == core))(lambda core=core: compute(core))
                else:
                    pl.when(some)(lambda: compute(0))
                for n in range(batch_size):
                    pl.when(live[first + n] > slot)(lambda n=n: place(first + n).start())
            else:
                compute(0)
                for n in range(batch_size):
                    place(first + n).start()
            return carry

        def add_slot():
            lax.fori_loop(0, n_group // batch_size, run, 0)
            tokens[0, 0, :, 0] = before[0][...]
            copy = pltpu.make_async_copy(tokens, result, sems.at[n_sem])
            copy.start()
            for group in range(n_group):
                pl.when(live[group] > slot)(lambda group=group: place(group).wait())
            copy.wait()

        if kept:
            tokens[0, 0, :, slot] = jnp.zeros((n_group,) + values.shape[4:], jnp.bfloat16)
            some = live[0] > slot
            for group in range(1, n_group):
                some = some | (live[group] > slot)
            pl.when(some)(add_slot)
        else:
            blank[...] = jnp.zeros(block, jnp.float32)
            for group in range(n_group):
                pl.when(live[group] < cap)(lambda group=group: erase(group).start())
            tokens[0, 0, :, cap - 1] = jnp.zeros((n_group,) + values.shape[4:], jnp.bfloat16)
            lax.fori_loop(0, n_group // batch_size, run, 0)
            handed[0][...] = tokens[0, 0, :, slot]
            copy = pltpu.make_async_copy(tokens, result, sems.at[n_sem])
            copy.start()
            for group in range(n_group):
                place(group).wait()
                pl.when(live[group] < cap)(lambda group=group: erase(group).wait())
            copy.wait()

    vmem, any_space = pl.BlockSpec(memory_space=pltpu.VMEM), pl.BlockSpec(memory_space=pl.ANY)
    in_vmem = [pltpu.with_memory_space_constraint(x, pltpu.VMEM) for x in sources]
    return pl.pallas_call(
        kernel,
        out_shape=(
            jax.ShapeDtypeStruct(values.shape, jnp.bfloat16),
            jax.ShapeDtypeStruct((1, 1, n_group, cap) + block, jnp.float32),
        )
        + (() if kept else (jax.ShapeDtypeStruct((n_group,) + values.shape[4:], jnp.bfloat16),)),
        in_specs=[pl.BlockSpec(memory_space=pltpu.SMEM)]
        + [vmem] * (len(sources) + len(small) + 1)
        + [vmem, any_space, any_space][: len(kept)],
        out_specs=(any_space, any_space) + (() if kept else (vmem,)),
        scratch_shapes=[
            pltpu.VMEM((n_group,) + block, jnp.float32),
            pltpu.SemaphoreType.DMA((2 * n_group + 1,)),
        ]
        + [pltpu.VMEM(shape, jnp.float32) for shape in scratch]
        + [pltpu.VMEM(block, jnp.float32), pltpu.VMEM(values.shape, jnp.bfloat16)],
        input_output_aliases={len(sources) + len(small) + 3 + n: n for n in range(2)}
        if kept
        else {},
        compiler_params=pltpu.CompilerParams(vmem_limit_bytes=32 * 1024 * 1024),
    )(live, *in_vmem, *small, gain, *kept)


def exchange(cells):
    return lax.all_to_all(cells, ("group", "sub"), split_axis=0, concat_axis=0, tiled=True)


def with_spare(placed, states, small, gain, n_group):
    cells, live = pack(placed, states, n_group, True)
    heads, key_size, value_size = states.shape[1:]
    square = (key_size, value_size)
    arrived = exchange(cells)
    spare = arrived[:, heads]
    swap = [(n, n ^ 1) for n in range(SUBGROUPS)]
    other = lax.ppermute(spare, "sub", swap)
    by_source = arrived.reshape((n_group, SUBGROUPS, heads + 1) + square)
    other = other.reshape((n_group, SUBGROUPS) + square)
    earlier = decode(
        live, [by_source], lambda s, i, _, x: [x[s, i, a] for a in range(heads)], 0, small, gain
    )

    def load(s, i, core, x, y):
        return [x[s, i, heads] if core == a else y[s, i] for a in range(heads)]

    return decode(live, [by_source, other], load, 1, small, gain, earlier)


def without_spare(placed, states, small, gain, n_group):
    cells, live = pack(placed, states, n_group, False)
    heads, key_size, value_size = states.shape[1:]
    square = (key_size, value_size)
    arrived = exchange(cells).reshape((n_group, SUBGROUPS, SLOT_CAP, heads) + square)
    earlier = None
    for slot in range(SLOT_CAP):
        earlier = decode(
            live,
            [arrived],
            lambda s, i, _, x, slot=slot: [x[s, i, slot, a] for a in range(heads)],
            slot,
            small,
            gain,
            earlier,
        )
    return earlier


def local(states, placement, queries, key_vectors, value_vectors, gate_inputs, strength, decay, gain):
    n_group = lax.axis_size("group")
    placed = placement.reshape(placement.shape[0])
    fits = cells_fit(placed, n_group * SUBGROUPS, states.shape[0])
    small = (queries, key_vectors, value_vectors, gate_inputs, strength, decay)
    gain = gain.reshape(1, gain.shape[0])
    return lax.switch(
        fits[0],
        [lambda *x: without_spare(*x, n_group), lambda *x: with_spare(*x, n_group)],
        placed,
        states,
        small,
        gain,
    )


def solution(mesh):
    n_group, n_head = mesh.devices.shape
    quads = Mesh(
        mesh.devices.reshape(n_group, n_head // SUBGROUPS, SUBGROUPS), ("group", "block", "sub")
    )
    spread = P("group", ("block", "sub"))
    return jax.shard_map(
        local,
        mesh=quads,
        in_specs=(spread, P(), spread, spread, spread, spread, spread, spread, P()),
        out_specs=(spread, spread),
        check_vma=False,
    )
```

```python
import math

import jax
import jax.numpy as jnp
from jax import lax
from jax.experimental import pallas as pl
from jax.experimental.pallas import tpu as pltpu
from jax.sharding import Mesh
from jax.sharding import PartitionSpec as P

SUBGROUPS = 4
SLOT_CAP = 2
CORES = 2
SOURCES = 2
EPS = 1e-06


def fits_kernel(dec_groups, reqs, placed, fits):
    lanes = placed.shape[1]
    chips = placed[...] // CORES
    named = [jnp.where(chips == chip, 1.0, 0.0) for chip in range(dec_groups // CORES)]
    lane = lax.broadcasted_iota(jnp.int32, (lanes, lanes), 0)
    group = lax.broadcasted_iota(jnp.int32, (lanes, lanes), 1)
    counts = jnp.dot(
        jnp.concatenate(named, axis=0).astype(jnp.bfloat16),
        jnp.where(lane // reqs == group, 1.0, 0.0).astype(jnp.bfloat16),
        preferred_element_type=jnp.float32,
    )
    fits[0] = jnp.where(jnp.max(counts) < SLOT_CAP + 1.5, 1, 0)


def cells_fit(placed, dec_groups, reqs):
    return pl.pallas_call(
        lambda *refs: fits_kernel(dec_groups, reqs, *refs),
        out_shape=jax.ShapeDtypeStruct((1,), jnp.int32),
        in_specs=[pl.BlockSpec(memory_space=pltpu.VMEM)],
        out_specs=pl.BlockSpec(memory_space=pltpu.SMEM),
    )(placed.reshape(-1, 128))


def pack_kernel(n_group, reqs, spare, placed, states, cells, live, count, sems):
    group = lax.axis_index("group")
    mine = group * SUBGROUPS + lax.axis_index("sub")
    heads = states.shape[1]

    def clear(d, carry):
        count[d] = 0
        return carry

    lax.fori_loop(0, n_group * SUBGROUPS, clear, 0, unroll=8)

    def send(r, carry):
        d = placed[group * reqs + r]
        rank = count[d]
        count[d] = rank + 1
        if spare:

            @pl.when(rank == 0)
            def _():
                pltpu.make_async_copy(
                    states.at[r], cells.at[d, pl.ds(0, heads)], sems.at[r]
                ).start()

            @pl.when(rank > 0)
            def _():
                for a in range(heads):
                    pltpu.make_async_copy(
                        states.at[r, a], cells.at[d // CORES * CORES + a, heads], sems.at[r]
                    ).start()

        else:
            pltpu.make_async_copy(states.at[r], cells.at[d, rank], sems.at[r]).start()
        return carry

    lax.fori_loop(0, reqs, send, 0, unroll=4)

    for s in range(n_group):

        def tally(r, total, s=s):
            return total + jnp.where(placed[s * reqs + r] == mine, 1, 0)

        live[s] = lax.fori_loop(0, reqs, tally, 0, unroll=8)

    def drain(r, carry):
        landed = cells.at[0, pl.ds(0, heads)] if spare else cells.at[0, 0]
        pltpu.make_async_copy(states.at[r], landed, sems.at[r]).wait()
        return carry

    lax.fori_loop(0, reqs, drain, 0, unroll=4)


def pack(placed, states, n_group, spare):
    reqs, heads, key_size, value_size = states.shape
    cell = (heads + 1,) if spare else (SLOT_CAP, heads)
    cells = (n_group * SUBGROUPS,) + cell + (key_size, value_size)
    return pl.pallas_call(
        lambda *refs: pack_kernel(n_group, reqs, spare, *refs),
        out_shape=(
            pltpu.VMEM(cells, states.dtype),
            jax.ShapeDtypeStruct((n_group,), jnp.int32),
        ),
        in_specs=[
            pl.BlockSpec(memory_space=pltpu.SMEM),
            pl.BlockSpec(memory_space=pltpu.HBM),
        ],
        out_specs=(
            pl.BlockSpec(memory_space=pltpu.VMEM),
            pl.BlockSpec(memory_space=pltpu.SMEM),
        ),
        scratch_shapes=[
            pltpu.SMEM((n_group * SUBGROUPS,), jnp.int32),
            pltpu.SemaphoreType.DMA((reqs,)),
        ],
        compiler_params=pltpu.CompilerParams(vmem_limit_bytes=32 * 1024 * 1024),
    )(placed, pltpu.with_memory_space_constraint(states, pltpu.HBM))


def split(x):
    high = x.astype(jnp.bfloat16)
    return high, (x - high.astype(jnp.float32)).astype(jnp.bfloat16)


def row_sums(parts):
    rows, lanes = parts[0].shape
    high, low = split(jnp.concatenate(parts, axis=0))
    sums = jnp.dot(
        jnp.concatenate([high, low], axis=1),
        jnp.ones((2 * lanes, lanes), jnp.bfloat16),
        preferred_element_type=jnp.float32,
    )
    return [sums[n * rows : (n + 1) * rows] for n in range(len(parts))]


def widen(columns, width):
    rows, count = columns.shape
    high, rest = split(columns)
    low = columns - high.astype(jnp.float32) - rest.astype(jnp.float32)
    parts = [high.astype(jnp.float32), rest.astype(jnp.float32), low]
    lane = lax.broadcasted_iota(jnp.int32, (count, count * width), 1)
    column = lax.broadcasted_iota(jnp.int32, (count, count * width), 0)
    wide = jnp.dot(
        jnp.concatenate(parts, axis=0).astype(jnp.bfloat16),
        jnp.where(lane // width == column, 1.0, 0.0).astype(jnp.bfloat16),
        preferred_element_type=jnp.float32,
    )
    return wide[:rows] + wide[rows : 2 * rows] + wide[2 * rows :]


def decode_kernel(
    load, sources, slot, first, live, query, key, value, gate, strength, decay, gain, tokens, states,
    by_key, by_query, values, fades, writes, key_rows, query_rows, kept,
):
    size, width = states.shape[2:]
    heads = states.shape[1] // SUBGROUPS
    steps = key.shape[4]
    units = [(n, i) for n in range(sources) for i in range(SUBGROUPS)]
    count = len(units)

    def keys(i):
        return slice(i * size, (i + 1) * size)

    def lanes(i):
        return slice(i * heads * width, (i + 1) * heads * width)

    def state_of(n, i):
        return jnp.concatenate(load(first + n, i), axis=1)

    def rows(t):
        return slice(t * count, (t + 1) * count)

    def spread(ref, u, x):
        for a in range(heads):
            ref[a, pl.ds(u, steps, stride=count), :] = x[:, a * width : (a + 1) * width]

    def gather(ref, u):
        return jnp.concatenate(
            [ref[a, pl.ds(u, steps, stride=count), :] for a in range(heads)], axis=1
        )

    for u, (n, i) in enumerate(units):
        for ref, x in ((key_rows, key), (query_rows, query)):
            part = x[0, 0, first + n, slot, :, keys(i)]
            ref[pl.ds(u, steps, stride=count), :] = part.astype(jnp.float32)
    wide = widen(
        jnp.concatenate(
            [x[0, 0, first + n, slot] for x in (decay, strength) for n in range(sources)], axis=0
        ),
        width,
    )
    for u, (n, i) in enumerate(units):
        key_f = key[0, 0, first + n, slot, :, keys(i)].astype(jnp.float32)
        query_f = query[0, 0, first + n, slot, :, keys(i)].astype(jnp.float32)
        both = jnp.concatenate([key_f, query_f], axis=0).astype(jnp.bfloat16)
        high, low = split(state_of(n, i))
        product = jnp.dot(both, high, preferred_element_type=jnp.float32)
        product = product + jnp.dot(both, low, preferred_element_type=jnp.float32)
        spread(by_key, u, product[:steps])
        spread(by_query, u, product[steps:])
        spread(values, u, value[0, 0, first + n, slot, :, lanes(i)].astype(jnp.float32))
        spread(fades, u, wide[n * steps : (n + 1) * steps, lanes(i)])
        spread(writes, u, wide[(sources + n) * steps : (sources + n + 1) * steps, lanes(i)])

    on_key = [[by_key[a, rows(t)] for a in range(heads)] for t in range(steps)]
    on_query = [[by_query[a, rows(t)] for a in range(heads)] for t in range(steps)]
    keyed = [key_rows[rows(t)] for t in range(steps)]
    asked = [query_rows[rows(t)] for t in range(steps)]
    pairs = [(l, t) for t in range(steps) for l in range(t, steps)]
    key_key = dict(zip(pairs, row_sums([keyed[l] * keyed[t] for l, t in pairs])))
    query_key = dict(zip(pairs, row_sums([asked[l] * keyed[t] for l, t in pairs])))
    query_norms = [lax.rsqrt(x + EPS) / math.sqrt(size) for x in row_sums([q * q for q in asked])]
    written, total = [], None
    for t in range(steps):
        fade = [fades[a, rows(t)] for a in range(heads)]
        total = fade if total is None else [x * f for x, f in zip(total, fade)]
        norm = lax.rsqrt(key_key[t, t] + EPS)
        write = []
        for a in range(heads):
            residual = values[a, rows(t)] - norm * (on_key[t][a] * fade[a])
            write.append(writes[a, rows(t)] * norm * residual)
        written = [[w * f for w, f in zip(old, fade)] for old in written] + [write]
        for later in range(t, steps):
            for on, dots in ((on_key, key_key), (on_query, query_key)):
                if on is on_query or later > t:
                    dot = dots[later, t]
                    on[later] = [x * f + dot * w for x, f, w in zip(on[later], fade, write)]
    kept[...] = jnp.concatenate(total, axis=1)
    readouts = [x * query_norms[t] for t in range(steps) for x in on_query[t]]
    squares = row_sums([x * x for x in readouts])
    for t in range(steps):
        for a in range(heads):
            by_key[a, rows(t)] = written[t][a]
            norm = lax.rsqrt(squares[t * heads + a] / width + EPS)
            by_query[a, rows(t)] = readouts[t * heads + a] * norm * gain[...]

    for u, (n, i) in enumerate(units):
        key_f = key[0, 0, first + n, slot, :, keys(i)].astype(jnp.float32)
        high, low = split(gather(by_key, u))
        update = lax.dot_general(
            jnp.concatenate([key_f, key_f], axis=0).astype(jnp.bfloat16),
            jnp.concatenate([high.astype(jnp.float32), low.astype(jnp.float32)], axis=0).astype(
                jnp.bfloat16
            ),
            (((0,), (0,)), ((), ())),
            preferred_element_type=jnp.float32,
        )
        state = kept[u : u + 1, :] * state_of(n, i) + update
        for a in range(heads):
            states[first + n, heads * i + a] = state[:, a * width : (a + 1) * width]
        opened = gate[0, 0, first + n, slot, :, lanes(i)].astype(jnp.float32)
        token = gather(by_query, u) * (opened * jax.nn.sigmoid(opened))
        tokens[first + n, :, lanes(i)] = token.astype(tokens.dtype)

    for n in range(sources):

        @pl.when(live[first + n] <= slot)
        def _(n=n):
            tokens[first + n] = jnp.zeros(tokens.shape[1:], tokens.dtype)
            states[first + n] = jnp.zeros(states.shape[1:], states.dtype)


def decode(live, sources, load, slot, small, gain, earlier=None):
    queries, values = small[0], small[2]
    n_group, cap, steps = queries.shape[2:5]
    key_size, value_size = queries.shape[5] // SUBGROUPS, gain.shape[1]
    heads = values.shape[5] // (SUBGROUPS * value_size)
    block = (SUBGROUPS * heads, key_size, value_size)
    batch_size = SOURCES * 2 if earlier else SOURCES
    units = batch_size * SUBGROUPS
    rows = (steps + 1) * units
    by_step = (heads, rows, value_size)
    scratch = [by_step] * 5 + [(rows, key_size)] * 2 + [(units, heads * value_size)]
    kept = () if earlier is None else (earlier[2], *earlier[:2])

    def kernel(live, *refs):
        blocks, refs = refs[: len(sources)], refs[len(sources) :]
        ins, refs = refs[: len(small) + 1], refs[len(small) + 1 :]
        before, refs = refs[: len(kept)], refs[len(kept) :]
        result, finals, *refs = refs
        handed, refs = refs[: 0 if kept else 1], refs[0 if kept else 1 :]
        states, sems, *work = refs
        tokens, blank = work.pop(), work.pop()
        n_sem = 2 * n_group

        def erase(group):
            return pltpu.make_async_copy(
                blank, finals.at[0, 0, group, cap - 1], sems.at[n_group + group]
            )

        def place(group):
            return pltpu.make_async_copy(
                states.at[group], finals.at[0, 0, group, slot], sems.at[group]
            )

        def run(batch, carry):
            first = batch * batch_size

            def compute(core):
                decode_kernel(
                    lambda s, i: load(s, i, core, *blocks), batch_size, slot, first, live, *ins,
                    tokens.at[0, 0, :, slot], states, *work,
                )

            if kept:
                some = live[first] > slot
                for n in range(1, batch_size):
                    some = some | (live[first + n] > slot)
                if len(sources) > 1:
                    me = lax.axis_index("sub") % CORES
                    for core in range(CORES):
                        pl.when(some & (me == core))(lambda core=core: compute(core))
                else:
                    pl.when(some)(lambda: compute(0))
                for n in range(batch_size):
                    pl.when(live[first + n] > slot)(lambda n=n: place(first + n).start())
            else:
                compute(0)
                for n in range(batch_size):
                    place(first + n).start()
            return carry

        def add_slot():
            lax.fori_loop(0, n_group // batch_size, run, 0)
            tokens[0, 0, :, 0] = before[0][...]
            copy = pltpu.make_async_copy(tokens, result, sems.at[n_sem])
            copy.start()
            for group in range(n_group):
                pl.when(live[group] > slot)(lambda group=group: place(group).wait())
            copy.wait()

        if kept:
            tokens[0, 0, :, slot] = jnp.zeros((n_group,) + values.shape[4:], jnp.bfloat16)
            some = live[0] > slot
            for group in range(1, n_group):
                some = some | (live[group] > slot)
            pl.when(some)(add_slot)
        else:
            blank[...] = jnp.zeros(block, jnp.float32)
            for group in range(n_group):
                pl.when(live[group] < cap)(lambda group=group: erase(group).start())
            tokens[0, 0, :, cap - 1] = jnp.zeros((n_group,) + values.shape[4:], jnp.bfloat16)
            lax.fori_loop(0, n_group // batch_size, run, 0)
            handed[0][...] = tokens[0, 0, :, slot]
            copy = pltpu.make_async_copy(tokens, result, sems.at[n_sem])
            copy.start()
            for group in range(n_group):
                place(group).wait()
                pl.when(live[group] < cap)(lambda group=group: erase(group).wait())
            copy.wait()

    vmem, any_space = pl.BlockSpec(memory_space=pltpu.VMEM), pl.BlockSpec(memory_space=pl.ANY)
    in_vmem = [pltpu.with_memory_space_constraint(x, pltpu.VMEM) for x in sources]
    return pl.pallas_call(
        kernel,
        out_shape=(
            jax.ShapeDtypeStruct(values.shape, jnp.bfloat16),
            jax.ShapeDtypeStruct((1, 1, n_group, cap) + block, jnp.float32),
        )
        + (() if kept else (jax.ShapeDtypeStruct((n_group,) + values.shape[4:], jnp.bfloat16),)),
        in_specs=[pl.BlockSpec(memory_space=pltpu.SMEM)]
        + [vmem] * (len(sources) + len(small) + 1)
        + [vmem, any_space, any_space][: len(kept)],
        out_specs=(any_space, any_space) + (() if kept else (vmem,)),
        scratch_shapes=[
            pltpu.VMEM((n_group,) + block, jnp.float32),
            pltpu.SemaphoreType.DMA((2 * n_group + 1,)),
        ]
        + [pltpu.VMEM(shape, jnp.float32) for shape in scratch]
        + [pltpu.VMEM(block, jnp.float32), pltpu.VMEM(values.shape, jnp.bfloat16)],
        input_output_aliases={len(sources) + len(small) + 3 + n: n for n in range(2)}
        if kept
        else {},
        compiler_params=pltpu.CompilerParams(vmem_limit_bytes=32 * 1024 * 1024),
    )(live, *in_vmem, *small, gain, *kept)


def exchange(cells):
    return lax.all_to_all(cells, ("group", "sub"), split_axis=0, concat_axis=0, tiled=True)


def with_spare(placed, states, small, gain, n_group):
    cells, live = pack(placed, states, n_group, True)
    heads, key_size, value_size = states.shape[1:]
    square = (key_size, value_size)
    arrived = exchange(cells)
    spare = arrived[:, heads]
    swap = [(n, n ^ 1) for n in range(SUBGROUPS)]
    other = lax.ppermute(spare, "sub", swap)
    by_source = arrived.reshape((n_group, SUBGROUPS, heads + 1) + square)
    other = other.reshape((n_group, SUBGROUPS) + square)
    earlier = decode(
        live, [by_source], lambda s, i, _, x: [x[s, i, a] for a in range(heads)], 0, small, gain
    )

    def load(s, i, core, x, y):
        return [x[s, i, heads] if core == a else y[s, i] for a in range(heads)]

    return decode(live, [by_source, other], load, 1, small, gain, earlier)


def without_spare(placed, states, small, gain, n_group):
    cells, live = pack(placed, states, n_group, False)
    heads, key_size, value_size = states.shape[1:]
    square = (key_size, value_size)
    arrived = exchange(cells).reshape((n_group, SUBGROUPS, SLOT_CAP, heads) + square)
    earlier = None
    for slot in range(SLOT_CAP):
        earlier = decode(
            live,
            [arrived],
            lambda s, i, _, x, slot=slot: [x[s, i, slot, a] for a in range(heads)],
            slot,
            small,
            gain,
            earlier,
        )
    return earlier


def local(states, placement, queries, key_vectors, value_vectors, gate_inputs, strength, decay, gain):
    n_group = lax.axis_size("group")
    placed = placement.reshape(placement.shape[0])
    fits = cells_fit(placed, n_group * SUBGROUPS, states.shape[0])
    small = (queries, key_vectors, value_vectors, gate_inputs, strength, decay)
    gain = gain.reshape(1, gain.shape[0])
    return lax.switch(
        fits[0],
        [lambda *x: without_spare(*x, n_group), lambda *x: with_spare(*x, n_group)],
        placed,
        states,
        small,
        gain,
    )


def solution(mesh):
    n_group, n_head = mesh.devices.shape
    quads = Mesh(
        mesh.devices.reshape(n_group, n_head // SUBGROUPS, SUBGROUPS), ("group", "block", "sub")
    )
    spread = P("group", ("block", "sub"))
    return jax.shard_map(
        local,
        mesh=quads,
        in_specs=(spread, P(), spread, spread, spread, spread, spread, spread, P()),
        out_specs=(spread, spread),
        check_vma=False,
    )
```

```python
import math

import jax
import jax.numpy as jnp
from jax import lax
from jax.experimental import pallas as pl
from jax.experimental.pallas import tpu as pltpu
from jax.sharding import Mesh
from jax.sharding import PartitionSpec as P

SUBGROUPS = 4
SLOT_CAP = 2
CORES = 2
SOURCES = 2
EPS = 1e-06


def fits_kernel(dec_groups, reqs, placed, fits):
    lanes = placed.shape[1]
    chips = placed[...] // CORES
    named = [jnp.where(chips == chip, 1.0, 0.0) for chip in range(dec_groups // CORES)]
    lane = lax.broadcasted_iota(jnp.int32, (lanes, lanes), 0)
    group = lax.broadcasted_iota(jnp.int32, (lanes, lanes), 1)
    counts = jnp.dot(
        jnp.concatenate(named, axis=0).astype(jnp.bfloat16),
        jnp.where(lane // reqs == group, 1.0, 0.0).astype(jnp.bfloat16),
        preferred_element_type=jnp.float32,
    )
    fits[0] = jnp.where(jnp.max(counts) < SLOT_CAP + 1.5, 1, 0)


def cells_fit(placed, dec_groups, reqs):
    return pl.pallas_call(
        lambda *refs: fits_kernel(dec_groups, reqs, *refs),
        out_shape=jax.ShapeDtypeStruct((1,), jnp.int32),
        in_specs=[pl.BlockSpec(memory_space=pltpu.VMEM)],
        out_specs=pl.BlockSpec(memory_space=pltpu.SMEM),
    )(placed.reshape(-1, 128))


def pack_kernel(n_group, reqs, spare, placed, states, cells, live, count, sems):
    group = lax.axis_index("group")
    mine = group * SUBGROUPS + lax.axis_index("sub")
    heads = states.shape[1]

    def clear(d, carry):
        count[d] = 0
        return carry

    lax.fori_loop(0, n_group * SUBGROUPS, clear, 0, unroll=8)

    def send(r, carry):
        d = placed[group * reqs + r]
        rank = count[d]
        count[d] = rank + 1
        if spare:

            @pl.when(rank == 0)
            def _():
                pltpu.make_async_copy(
                    states.at[r], cells.at[d, pl.ds(0, heads)], sems.at[r]
                ).start()

            @pl.when(rank > 0)
            def _():
                for a in range(heads):
                    pltpu.make_async_copy(
                        states.at[r, a], cells.at[d // CORES * CORES + a, heads], sems.at[r]
                    ).start()

        else:
            pltpu.make_async_copy(states.at[r], cells.at[d, rank], sems.at[r]).start()
        return carry

    lax.fori_loop(0, reqs, send, 0, unroll=4)

    for s in range(n_group):

        def tally(r, total, s=s):
            return total + jnp.where(placed[s * reqs + r] == mine, 1, 0)

        live[s] = lax.fori_loop(0, reqs, tally, 0, unroll=8)

    def drain(r, carry):
        landed = cells.at[0, pl.ds(0, heads)] if spare else cells.at[0, 0]
        pltpu.make_async_copy(states.at[r], landed, sems.at[r]).wait()
        return carry

    lax.fori_loop(0, reqs, drain, 0, unroll=4)


def pack(placed, states, n_group, spare):
    reqs, heads, key_size, value_size = states.shape
    cell = (heads + 1,) if spare else (SLOT_CAP, heads)
    cells = (n_group * SUBGROUPS,) + cell + (key_size, value_size)
    return pl.pallas_call(
        lambda *refs: pack_kernel(n_group, reqs, spare, *refs),
        out_shape=(
            pltpu.VMEM(cells, states.dtype),
            jax.ShapeDtypeStruct((n_group,), jnp.int32),
        ),
        in_specs=[
            pl.BlockSpec(memory_space=pltpu.SMEM),
            pl.BlockSpec(memory_space=pltpu.HBM),
        ],
        out_specs=(
            pl.BlockSpec(memory_space=pltpu.VMEM),
            pl.BlockSpec(memory_space=pltpu.SMEM),
        ),
        scratch_shapes=[
            pltpu.SMEM((n_group * SUBGROUPS,), jnp.int32),
            pltpu.SemaphoreType.DMA((reqs,)),
        ],
        compiler_params=pltpu.CompilerParams(vmem_limit_bytes=32 * 1024 * 1024),
    )(placed, pltpu.with_memory_space_constraint(states, pltpu.HBM))


def split(x):
    high = x.astype(jnp.bfloat16)
    return high, (x - high.astype(jnp.float32)).astype(jnp.bfloat16)


def row_sums(parts):
    rows, lanes = parts[0].shape
    high, low = split(jnp.concatenate(parts, axis=0))
    sums = jnp.dot(
        jnp.concatenate([high, low], axis=1),
        jnp.ones((2 * lanes, lanes), jnp.bfloat16),
        preferred_element_type=jnp.float32,
    )
    return [sums[n * rows : (n + 1) * rows] for n in range(len(parts))]


def widen(columns, width):
    rows, count = columns.shape
    high, rest = split(columns)
    low = columns - high.astype(jnp.float32) - rest.astype(jnp.float32)
    parts = [high.astype(jnp.float32), rest.astype(jnp.float32), low]
    lane = lax.broadcasted_iota(jnp.int32, (count, count * width), 1)
    column = lax.broadcasted_iota(jnp.int32, (count, count * width), 0)
    wide = jnp.dot(
        jnp.concatenate(parts, axis=0).astype(jnp.bfloat16),
        jnp.where(lane // width == column, 1.0, 0.0).astype(jnp.bfloat16),
        preferred_element_type=jnp.float32,
    )
    return wide[:rows] + wide[rows : 2 * rows] + wide[2 * rows :]


def decode_kernel(
    load, sources, slot, first, live, query, key, value, gate, strength, decay, gain, tokens, states,
    by_key, by_query, values, fades, writes, key_rows, query_rows, kept,
):
    size, width = states.shape[2:]
    heads = states.shape[1] // SUBGROUPS
    steps = key.shape[4]
    units = [(n, i) for n in range(sources) for i in range(SUBGROUPS)]
    count = len(units)

    def keys(i):
        return slice(i * size, (i + 1) * size)

    def lanes(i):
        return slice(i * heads * width, (i + 1) * heads * width)

    def state_of(n, i):
        return jnp.concatenate(load(first + n, i), axis=1)

    def rows(t):
        return slice(t * count, (t + 1) * count)

    def spread(ref, u, x):
        for a in range(heads):
            ref[a, pl.ds(u, steps, stride=count), :] = x[:, a * width : (a + 1) * width]

    def gather(ref, u):
        return jnp.concatenate(
            [ref[a, pl.ds(u, steps, stride=count), :] for a in range(heads)], axis=1
        )

    for u, (n, i) in enumerate(units):
        for ref, x in ((key_rows, key), (query_rows, query)):
            part = x[0, 0, first + n, slot, :, keys(i)]
            ref[pl.ds(u, steps, stride=count), :] = part.astype(jnp.float32)
    wide = widen(
        jnp.concatenate(
            [x[0, 0, first + n, slot] for x in (decay, strength) for n in range(sources)], axis=0
        ),
        width,
    )
    for u, (n, i) in enumerate(units):
        key_f = key[0, 0, first + n, slot, :, keys(i)].astype(jnp.float32)
        query_f = query[0, 0, first + n, slot, :, keys(i)].astype(jnp.float32)
        both = jnp.concatenate([key_f, query_f], axis=0).astype(jnp.bfloat16)
        high, low = split(state_of(n, i))
        product = jnp.dot(both, high, preferred_element_type=jnp.float32)
        product = product + jnp.dot(both, low, preferred_element_type=jnp.float32)
        spread(by_key, u, product[:steps])
        spread(by_query, u, product[steps:])
        spread(values, u, value[0, 0, first + n, slot, :, lanes(i)].astype(jnp.float32))
        spread(fades, u, wide[n * steps : (n + 1) * steps, lanes(i)])
        spread(writes, u, wide[(sources + n) * steps : (sources + n + 1) * steps, lanes(i)])

    on_key = [[by_key[a, rows(t)] for a in range(heads)] for t in range(steps)]
    on_query = [[by_query[a, rows(t)] for a in range(heads)] for t in range(steps)]
    keyed = [key_rows[rows(t)] for t in range(steps)]
    asked = [query_rows[rows(t)] for t in range(steps)]
    pairs = [(l, t) for t in range(steps) for l in range(t, steps)]
    key_key = dict(zip(pairs, row_sums([keyed[l] * keyed[t] for l, t in pairs])))
    query_key = dict(zip(pairs, row_sums([asked[l] * keyed[t] for l, t in pairs])))
    query_norms = [lax.rsqrt(x + EPS) / math.sqrt(size) for x in row_sums([q * q for q in asked])]
    written, total = [], None
    for t in range(steps):
        fade = [fades[a, rows(t)] for a in range(heads)]
        total = fade if total is None else [x * f for x, f in zip(total, fade)]
        norm = lax.rsqrt(key_key[t, t] + EPS)
        write = []
        for a in range(heads):
            residual = values[a, rows(t)] - norm * (on_key[t][a] * fade[a])
            write.append(writes[a, rows(t)] * norm * residual)
        written = [[w * f for w, f in zip(old, fade)] for old in written] + [write]
        for later in range(t, steps):
            for on, dots in ((on_key, key_key), (on_query, query_key)):
                if on is on_query or later > t:
                    dot = dots[later, t]
                    on[later] = [x * f + dot * w for x, f, w in zip(on[later], fade, write)]
    kept[...] = jnp.concatenate(total, axis=1)
    readouts = [x * query_norms[t] for t in range(steps) for x in on_query[t]]
    squares = row_sums([x * x for x in readouts])
    for t in range(steps):
        for a in range(heads):
            by_key[a, rows(t)] = written[t][a]
            norm = lax.rsqrt(squares[t * heads + a] / width + EPS)
            by_query[a, rows(t)] = readouts[t * heads + a] * norm * gain[...]

    for u, (n, i) in enumerate(units):
        key_f = key[0, 0, first + n, slot, :, keys(i)].astype(jnp.float32)
        high, low = split(gather(by_key, u))
        update = lax.dot_general(
            jnp.concatenate([key_f, key_f], axis=0).astype(jnp.bfloat16),
            jnp.concatenate([high.astype(jnp.float32), low.astype(jnp.float32)], axis=0).astype(
                jnp.bfloat16
            ),
            (((0,), (0,)), ((), ())),
            preferred_element_type=jnp.float32,
        )
        state = kept[u : u + 1, :] * state_of(n, i) + update
        for a in range(heads):
            states[first + n, heads * i + a] = state[:, a * width : (a + 1) * width]
        opened = gate[0, 0, first + n, slot, :, lanes(i)].astype(jnp.float32)
        token = gather(by_query, u) * (opened * jax.nn.sigmoid(opened))
        tokens[first + n, :, lanes(i)] = token.astype(tokens.dtype)

    for n in range(sources):

        @pl.when(live[first + n] <= slot)
        def _(n=n):
            tokens[first + n] = jnp.zeros(tokens.shape[1:], tokens.dtype)
            states[first + n] = jnp.zeros(states.shape[1:], states.dtype)


def decode(live, sources, load, slot, small, gain, earlier=None):
    queries, values = small[0], small[2]
    n_group, cap, steps = queries.shape[2:5]
    key_size, value_size = queries.shape[5] // SUBGROUPS, gain.shape[1]
    heads = values.shape[5] // (SUBGROUPS * value_size)
    block = (SUBGROUPS * heads, key_size, value_size)
    batch_size = SOURCES * 2 if earlier else SOURCES
    units = batch_size * SUBGROUPS
    rows = (steps + 1) * units
    by_step = (heads, rows, value_size)
    scratch = [by_step] * 5 + [(rows, key_size)] * 2 + [(units, heads * value_size)]
    kept = () if earlier is None else (earlier[2], *earlier[:2])

    def kernel(live, *refs):
        blocks, refs = refs[: len(sources)], refs[len(sources) :]
        ins, refs = refs[: len(small) + 1], refs[len(small) + 1 :]
        before, refs = refs[: len(kept)], refs[len(kept) :]
        result, finals, *refs = refs
        handed, refs = refs[: 0 if kept else 1], refs[0 if kept else 1 :]
        states, sems, *work = refs
        tokens, blank = work.pop(), work.pop()
        n_sem = 2 * n_group

        def erase(group):
            return pltpu.make_async_copy(
                blank, finals.at[0, 0, group, cap - 1], sems.at[n_group + group]
            )

        def place(group):
            return pltpu.make_async_copy(
                states.at[group], finals.at[0, 0, group, slot], sems.at[group]
            )

        def run(batch, carry):
            first = batch * batch_size

            def compute(core):
                decode_kernel(
                    lambda s, i: load(s, i, core, *blocks), batch_size, slot, first, live, *ins,
                    tokens.at[0, 0, :, slot], states, *work,
                )

            if kept:
                some = live[first] > slot
                for n in range(1, batch_size):
                    some = some | (live[first + n] > slot)
                if len(sources) > 1:
                    me = lax.axis_index("sub") % CORES
                    for core in range(CORES):
                        pl.when(some & (me == core))(lambda core=core: compute(core))
                else:
                    pl.when(some)(lambda: compute(0))
                for n in range(batch_size):
                    pl.when(live[first + n] > slot)(lambda n=n: place(first + n).start())
            else:
                compute(0)
                for n in range(batch_size):
                    place(first + n).start()
                for n in range(batch_size):
                    group = first + n
                    pl.when(live[group] < cap)(lambda group=group: erase(group).start())
            return carry

        def add_slot():
            lax.fori_loop(0, n_group // batch_size, run, 0)
            tokens[0, 0, :, 0] = before[0][...]
            copy = pltpu.make_async_copy(tokens, result, sems.at[n_sem])
            copy.start()
            for group in range(n_group):
                pl.when(live[group] > slot)(lambda group=group: place(group).wait())
            copy.wait()

        if kept:
            tokens[0, 0, :, slot] = jnp.zeros((n_group,) + values.shape[4:], jnp.bfloat16)
            some = live[0] > slot
            for group in range(1, n_group):
                some = some | (live[group] > slot)
            pl.when(some)(add_slot)
        else:
            blank[...] = jnp.zeros(block, jnp.float32)
            tokens[0, 0, :, cap - 1] = jnp.zeros((n_group,) + values.shape[4:], jnp.bfloat16)
            lax.fori_loop(0, n_group // batch_size, run, 0)
            handed[0][...] = tokens[0, 0, :, slot]
            copy = pltpu.make_async_copy(tokens, result, sems.at[n_sem])
            copy.start()
            for group in range(n_group):
                place(group).wait()
                pl.when(live[group] < cap)(lambda group=group: erase(group).wait())
            copy.wait()

    vmem, any_space = pl.BlockSpec(memory_space=pltpu.VMEM), pl.BlockSpec(memory_space=pl.ANY)
    in_vmem = [pltpu.with_memory_space_constraint(x, pltpu.VMEM) for x in sources]
    return pl.pallas_call(
        kernel,
        out_shape=(
            jax.ShapeDtypeStruct(values.shape, jnp.bfloat16),
            jax.ShapeDtypeStruct((1, 1, n_group, cap) + block, jnp.float32),
        )
        + (() if kept else (jax.ShapeDtypeStruct((n_group,) + values.shape[4:], jnp.bfloat16),)),
        in_specs=[pl.BlockSpec(memory_space=pltpu.SMEM)]
        + [vmem] * (len(sources) + len(small) + 1)
        + [vmem, any_space, any_space][: len(kept)],
        out_specs=(any_space, any_space) + (() if kept else (vmem,)),
        scratch_shapes=[
            pltpu.VMEM((n_group,) + block, jnp.float32),
            pltpu.SemaphoreType.DMA((2 * n_group + 1,)),
        ]
        + [pltpu.VMEM(shape, jnp.float32) for shape in scratch]
        + [pltpu.VMEM(block, jnp.float32), pltpu.VMEM(values.shape, jnp.bfloat16)],
        input_output_aliases={len(sources) + len(small) + 3 + n: n for n in range(2)}
        if kept
        else {},
        compiler_params=pltpu.CompilerParams(vmem_limit_bytes=32 * 1024 * 1024),
    )(live, *in_vmem, *small, gain, *kept)


def exchange(cells):
    return lax.all_to_all(cells, ("group", "sub"), split_axis=0, concat_axis=0, tiled=True)


def with_spare(placed, states, small, gain, n_group):
    cells, live = pack(placed, states, n_group, True)
    heads, key_size, value_size = states.shape[1:]
    square = (key_size, value_size)
    arrived = exchange(cells)
    spare = arrived[:, heads]
    swap = [(n, n ^ 1) for n in range(SUBGROUPS)]
    other = lax.ppermute(spare, "sub", swap)
    by_source = arrived.reshape((n_group, SUBGROUPS, heads + 1) + square)
    other = other.reshape((n_group, SUBGROUPS) + square)
    earlier = decode(
        live, [by_source], lambda s, i, _, x: [x[s, i, a] for a in range(heads)], 0, small, gain
    )

    def load(s, i, core, x, y):
        return [x[s, i, heads] if core == a else y[s, i] for a in range(heads)]

    return decode(live, [by_source, other], load, 1, small, gain, earlier)


def without_spare(placed, states, small, gain, n_group):
    cells, live = pack(placed, states, n_group, False)
    heads, key_size, value_size = states.shape[1:]
    square = (key_size, value_size)
    arrived = exchange(cells).reshape((n_group, SUBGROUPS, SLOT_CAP, heads) + square)
    earlier = None
    for slot in range(SLOT_CAP):
        earlier = decode(
            live,
            [arrived],
            lambda s, i, _, x, slot=slot: [x[s, i, slot, a] for a in range(heads)],
            slot,
            small,
            gain,
            earlier,
        )
    return earlier


def local(states, placement, queries, key_vectors, value_vectors, gate_inputs, strength, decay, gain):
    n_group = lax.axis_size("group")
    placed = placement.reshape(placement.shape[0])
    fits = cells_fit(placed, n_group * SUBGROUPS, states.shape[0])
    small = (queries, key_vectors, value_vectors, gate_inputs, strength, decay)
    gain = gain.reshape(1, gain.shape[0])
    return lax.switch(
        fits[0],
        [lambda *x: without_spare(*x, n_group), lambda *x: with_spare(*x, n_group)],
        placed,
        states,
        small,
        gain,
    )


def solution(mesh):
    n_group, n_head = mesh.devices.shape
    quads = Mesh(
        mesh.devices.reshape(n_group, n_head // SUBGROUPS, SUBGROUPS), ("group", "block", "sub")
    )
    spread = P("group", ("block", "sub"))
    return jax.shard_map(
        local,
        mesh=quads,
        in_specs=(spread, P(), spread, spread, spread, spread, spread, spread, P()),
        out_specs=(spread, spread),
        check_vma=False,
    )
```
